32 devices in a mesh: section: 8 (over z, x), tensor: 4 (over y, core).
Axes of the slice: x: 2, y: 2, z: 4, core: 2. Of those that a mesh axis runs over, the one named last changes fastest.
Arguments:
- section_input: bfloat16 [8, 128, 3072], P('section', 'tensor'), may hold values from -6 to 6
- query: bfloat16 [8, 3072, 128], P('section', 'tensor'), may hold values from -100 to 100
- key_stash: bfloat16 [8, 3072, 128], P('section', 'tensor'), may hold values from -4 to 4
- incoming: bfloat16 [8, 128, 3072], P('section', 'tensor'), may hold values from -6 to 6
- version: int32 [8], P('section'), may hold values from 0 to 1
- w_value: bfloat16 [8, 2, 3072, 1536], P('section', None, 'tensor'), may hold values from -0.109375 to 0.109375
- w_out: bfloat16 [8, 2, 3072, 1536], P('section', None, 'tensor'), may hold values from -0.109375 to 0.109375
Outputs:
- input_grad: bfloat16 [8, 128, 3072], P('section', 'tensor')
- grad_value: bfloat16 [8, 3072, 1536], P('section', 'tensor')
- grad_out: bfloat16 [8, 3072, 1536], P('section', 'tensor')
The draws below stay inside these ranges and needn't reach their ends.
All inputs are finite; a program needn't handle non-finite values.
Results may differ from the reference program's by a relative error of at most 0.018.
Values may be sent and summed in bfloat16 or wider, within the bound.
No kernel may reach another device: no remote copies, remote signals or barrier semaphores. Data moves between devices by JAX's collectives and lax.ppermute only.
A program may use at most 128 MiB of HBM per device.

```python
import math
import jax
import jax.numpy as jnp
from jax import lax

D = 3072
HEADS = 32
HEAD_DIM = 96
TOKENS = 128
ATTN = 3072
SLOTS = 8
N_TENSOR = 4


def stash_base(key):
    base_key = jax.random.fold_in(key, 5)
    return jnp.clip(jax.random.normal(base_key, (SLOTS, ATTN, TOKENS), jnp.float32), -4.0, 4.0)


def draw_query(key, part):
    base = stash_base(key)
    key = jax.random.fold_in(key, 21)
    drawn = jnp.clip(jax.random.normal(key, base.shape, jnp.float32), -4.0, 4.0)
    return drawn.astype(jnp.bfloat16)


def draw_key_stash(key, part):
    base = stash_base(key)
    drawn = base
    return drawn.astype(jnp.bfloat16)


def place_ends(values, rng, smallest, top_value):
    spot = [jax.random.randint(jax.random.fold_in(rng, axis), (), 0, length) for axis, length in enumerate(values.shape)]
    widest = values.shape.index(max(values.shape))
    beside = spot[:widest] + [(spot[widest] + 1) % values.shape[widest]] + spot[widest + 1:]
    return values.at[tuple(spot)].set(smallest).at[tuple(beside)].set(top_value)


def block_scale(own_key, shape, cuts, low, largest):
    factor_of = 1.0
    for dim, shards_of in cuts:
        draws = jax.random.uniform(jax.random.fold_in(jax.random.fold_in(own_key, 6), dim), (shards_of,), jnp.float32, low / len(cuts), largest / len(cuts))
        factor_of = factor_of * jnp.repeat(jnp.exp(draws), shape[dim] // shards_of).reshape((-1,) + (1,) * (len(shape) - 1 - dim))
    return factor_of


def normal_values(key, extent, scale, reach, shards=(), dtype=jnp.bfloat16):
    values = scale * jax.random.normal(key, extent, jnp.float32)
    if shards:
        values = values * block_scale(key, extent, shards, -0.22, 0.18)
    return jnp.clip(values, -reach, reach).astype(dtype)


def setup_inputs(seed: int = 0) -> dict:
    seeds = jax.random.split(jax.random.key(seed), 8)
    return {
        "section_input": normal_values(seeds[0], (SLOTS, TOKENS, D), 1.0, 6.0, ((0, 8), (1, 4))),
        "query": draw_query(jax.random.fold_in(seeds[7], 71), 0),
        "key_stash": draw_key_stash(jax.random.fold_in(seeds[7], 71), 0),
        "incoming": normal_values(seeds[3], (SLOTS, TOKENS, D), 1.0, 6.0, ((0, 8), (1, 4))),
        "version": place_ends(jax.random.randint(seeds[4], (SLOTS,), 0, 2), jax.random.fold_in(seeds[4], 1), 0, 1).astype(jnp.int32),
        "w_value": normal_values(seeds[5], (SLOTS, 2, ATTN, D // 2), D ** -0.5, 0.109375, ((0, 8), (2, 4))),
        "w_out": normal_values(seeds[6], (SLOTS, 2, ATTN, D // 2), ATTN ** -0.5, 0.109375, ((0, 8), (2, 4))),
    }


def attention_probs(query, key_stash):
    query_heads = query.astype(jnp.float32).reshape(HEADS, HEAD_DIM, TOKENS)
    key_heads = key_stash.astype(jnp.float32).reshape(HEADS, HEAD_DIM, TOKENS)
    scores = jnp.einsum('hdi,hdj->hij', query_heads, key_heads) * (1.0 / math.sqrt(HEAD_DIM))
    causal = lax.broadcasted_iota(jnp.int32, (TOKENS, TOKENS), 1) <= lax.broadcasted_iota(jnp.int32, (TOKENS, TOKENS), 0)
    scores = jnp.where(causal, scores, -jnp.inf)
    row_max = lax.optimization_barrier(jnp.max(scores, axis=2, keepdims=True))
    expo = jnp.exp(scores - row_max)
    return (expo / lax.optimization_barrier(jnp.sum(expo, axis=2, keepdims=True))).astype(jnp.bfloat16)

def section_backward(inputs, query, key_stash, value_weight, out_weight, upstream_grad):
    values = jnp.dot(value_weight, inputs.T, preferred_element_type=jnp.float32).astype(jnp.bfloat16)
    attend = attention_probs(query, key_stash).astype(jnp.float32)
    value_heads = values.astype(jnp.float32).reshape(HEADS, HEAD_DIM, TOKENS)
    context = jnp.einsum('hdj,hij->hdi', value_heads, attend).astype(jnp.bfloat16).reshape(ATTN, TOKENS)
    context_grad = jnp.dot(out_weight, upstream_grad.T, preferred_element_type=jnp.float32).astype(jnp.bfloat16)
    context_heads = context_grad.astype(jnp.float32).reshape(HEADS, HEAD_DIM, TOKENS)
    value_grad = jnp.einsum('hdi,hij->hdj', context_heads, attend).astype(jnp.bfloat16).reshape(ATTN, TOKENS)
    grad_groups = value_grad.astype(jnp.float32).reshape(N_TENSOR, ATTN // N_TENSOR, TOKENS)
    weight_groups = value_weight.astype(jnp.float32).reshape(N_TENSOR, ATTN // N_TENSOR, D)
    partials = jnp.einsum('gat,gad->gtd', grad_groups, weight_groups).astype(jnp.bfloat16)
    partials = lax.optimization_barrier(partials).astype(jnp.float32)
    input_grad = (upstream_grad.astype(jnp.float32) + lax.optimization_barrier(jnp.sum(partials, axis=0))).astype(jnp.bfloat16)
    value_wgrad = jnp.dot(value_grad, inputs, preferred_element_type=jnp.float32)
    out_wgrad = jnp.dot(context, upstream_grad, preferred_element_type=jnp.float32)
    return (input_grad, value_wgrad, out_wgrad)

def section_weights(table, slot_index, chosen):
    pair_index = slot_index // 2
    return jnp.concatenate([table[2 * pair_index][chosen], table[2 * pair_index + 1][chosen]], axis=-1)

def reference(section_input, query, key_stash, incoming, version, w_value, w_out):
    grads_in = [None] * SLOTS
    value_wgrads = [None] * SLOTS
    out_wgrads = [None] * SLOTS
    order = [slot for slot in range(SLOTS) if slot // 2 % 2 == 1] + [slot for slot in range(SLOTS) if slot // 2 % 2 == 0]
    for slot_index in order:
        chosen = version[slot_index]
        value_weight = section_weights(w_value, slot_index, chosen)
        out_weight = section_weights(w_out, slot_index, chosen)
        if slot_index // 2 % 2 == 1:
            upstream_grad = incoming[slot_index]
        else:
            upstream_grad = grads_in[slot_index + 2]
        result = section_backward(section_input[slot_index], query[slot_index], key_stash[slot_index], value_weight, out_weight, upstream_grad)
        grads_in[slot_index], value_wgrads[slot_index], out_wgrads[slot_index] = result
    half_width = D // 2
    value_parts = []
    out_parts = []
    for pair_index in range(SLOTS // 2):
        value_total = value_wgrads[2 * pair_index] + value_wgrads[2 * pair_index + 1]
        out_total = out_wgrads[2 * pair_index] + out_wgrads[2 * pair_index + 1]
        value_parts.append(value_total[:, :half_width].astype(jnp.bfloat16))
        value_parts.append(value_total[:, half_width:].astype(jnp.bfloat16))
        out_parts.append(out_total[:, :half_width].astype(jnp.bfloat16))
        out_parts.append(out_total[:, half_width:].astype(jnp.bfloat16))
    return (jnp.stack(grads_in), jnp.stack(value_parts), jnp.stack(out_parts))
```

```python
import math

import jax
import jax.numpy as jnp
from jax import lax
from jax.sharding import Mesh, PartitionSpec as P

HEAD_DIM = 96


def swap_half(array):
    return lax.ppermute(array, "half", [(0, 1), (1, 0)])


def nt_dot(left_side, right_side):
    return lax.dot_general(
        left_side, right_side, (((1,), (1,)), ((), ())), preferred_element_type=jnp.float32
    )


def tn_dot(left_side, right_side):
    return lax.dot_general(
        left_side, right_side, (((0,), (0,)), ((), ())), preferred_element_type=jnp.float32
    )


def attention_probs(query, key_stash):
    tokens = query.shape[-1]
    query_heads = query.reshape(-1, HEAD_DIM, tokens)
    key_heads = key_stash.reshape(-1, HEAD_DIM, tokens)
    scores = jnp.einsum(
        "hdi,hdj->hij", query_heads, key_heads, preferred_element_type=jnp.float32
    ) * (1.0 / math.sqrt(HEAD_DIM))
    causal = lax.broadcasted_iota(jnp.int32, (tokens, tokens), 1) <= lax.broadcasted_iota(
        jnp.int32, (tokens, tokens), 0
    )
    scores = jnp.where(causal, scores, -jnp.inf)
    row_max = jnp.max(scores, axis=2, keepdims=True)
    expo = jnp.exp(scores - row_max)
    return (expo / jnp.sum(expo, axis=2, keepdims=True)).astype(jnp.bfloat16)


def on_device(section_input, query, key_stash, incoming, version, w_value, w_out):
    half = lax.axis_index("half")
    odd = lax.axis_index("pair") % 2 == 1
    n_pairs = lax.axis_size("pair")
    n_tensor = lax.axis_size("tensor")
    width = w_value.shape[3]
    rows = w_value.shape[2]
    shard = section_input.shape[1]
    tokens = query.shape[2]

    def own_columns(array):
        return lax.dynamic_slice_in_dim(array, half * width, width, 1)

    def other_columns(array):
        return lax.dynamic_slice_in_dim(array, (1 - half) * width, width, 1)

    first = jnp.where(odd, incoming[0], section_input[0])
    second_own = section_input[0]
    first_pair = jnp.stack([own_columns(first), swap_half(other_columns(first))])
    other_version = swap_half(version)
    stash = jnp.concatenate([query, key_stash])
    stash_other = swap_half(stash)
    input_pair = jnp.stack([own_columns(second_own), swap_half(other_columns(second_own))])

    def chosen(table, which):
        return lax.dynamic_index_in_dim(table[0], which[0], 0, keepdims=False)

    value_weights = [chosen(w_value, version), chosen(w_value, other_version)]
    out_weights = [chosen(w_out, version), chosen(w_out, other_version)]

    probs = attention_probs(
        jnp.concatenate([query[0], stash_other[0]]), jnp.concatenate([key_stash[0], stash_other[1]])
    )
    flipped = jnp.swapaxes(probs, 1, 2)
    mix_first = jnp.where(odd, probs, flipped)
    mix_second = jnp.where(odd, flipped, probs)

    def gathered(pair):
        return lax.all_gather(pair, "tensor", axis=1, tiled=True)

    def mixed(weights, full, mix):
        partial = jnp.stack([nt_dot(weights[0], full[0]), nt_dot(weights[1], full[1])])
        arrived = swap_half(partial.astype(jnp.bfloat16))
        total = (partial + arrived[::-1].astype(jnp.float32)).astype(jnp.bfloat16)
        heads = total.reshape(-1, HEAD_DIM, tokens)
        result = jnp.einsum("hdi,hij->hdj", heads, mix, preferred_element_type=jnp.float32)
        return result.astype(jnp.bfloat16).reshape(2, rows, tokens)

    def scattered(result):
        partial = jnp.stack(
            [tn_dot(result[0], value_weights[0]), tn_dot(result[1], value_weights[1])]
        ).astype(jnp.bfloat16)
        pieces = partial.reshape(2, n_tensor, shard, width)
        arrived = lax.all_to_all(pieces, "tensor", 1, 1, tiled=True)
        return jnp.sum(arrived.astype(jnp.float32), axis=1)

    first_full = gathered(first_pair)
    first_result = mixed(
        [jnp.where(odd, o, v) for v, o in zip(value_weights, out_weights)], first_full, mix_first
    )
    first_dx = (first_pair.astype(jnp.float32) + scattered(first_result)).astype(jnp.bfloat16)
    received = lax.ppermute(
        first_dx, "pair", [(source, source - 1) for source in range(1, n_pairs, 2)]
    )
    second_pair = jnp.where(odd, input_pair, received)
    second_full = gathered(second_pair)
    second_result = mixed(
        [jnp.where(odd, v, o) for v, o in zip(value_weights, out_weights)], second_full, mix_second
    )
    second_dx = (second_pair.astype(jnp.float32) + scattered(second_result)).astype(jnp.bfloat16)

    final_dx = jnp.where(odd, first_dx, second_dx)
    final_other = swap_half(final_dx[1])
    input_grad = jnp.where(
        half == 0,
        jnp.concatenate([final_dx[0], final_other], axis=1),
        jnp.concatenate([final_other, final_dx[0]], axis=1),
    )

    def pair_sum(left_pair, right_pair):
        return (
            jnp.dot(left_pair[0], right_pair[0], preferred_element_type=jnp.float32)
            + jnp.dot(left_pair[1], right_pair[1], preferred_element_type=jnp.float32)
        ).astype(jnp.bfloat16)

    grad_first = pair_sum(first_result, second_full)
    grad_second = pair_sum(second_result, first_full)
    grad_value = jnp.where(odd, grad_first, grad_second)
    grad_out = jnp.where(odd, grad_second, grad_first)
    return (input_grad[None], grad_value[None], grad_out[None])


def solution(mesh):
    sections, tensor = mesh.devices.shape
    split = Mesh(mesh.devices.reshape(sections // 2, 2, tensor), ("pair", "half", "tensor"))
    slots = ("pair", "half")
    by_tokens = P(slots, "tensor", None)
    by_rows = P(slots, None, "tensor", None)
    return jax.shard_map(
        on_device,
        mesh=split,
        in_specs=(by_tokens, by_tokens, by_tokens, by_tokens, P(slots), by_rows, by_rows),
        out_specs=(by_tokens, by_tokens, by_tokens),
        check_vma=False,
    )
```

```python
import functools
import math

import jax
import jax.numpy as jnp
from jax import lax
from jax.experimental import pallas as pl
from jax.experimental.pallas import tpu as pltpu
from jax.sharding import Mesh, PartitionSpec as P

HEAD_DIM = 96
CHUNKS = 4
VMEM_BYTES = 32 * 2**20
NN = (((1,), (0,)), ((), ()))
NT = (((1,), (1,)), ((), ()))
TN = (((0,), (0,)), ((), ()))


def matmul(left_side, right_side, dims):
    return lax.dot_general(left_side, right_side, dims, preferred_element_type=jnp.float32)


def in_vmem():
    return pl.BlockSpec(memory_space=pltpu.VMEM)


def in_smem():
    return pl.BlockSpec(memory_space=pltpu.SMEM)


def in_place():
    return pl.BlockSpec(memory_space=pl.ANY)


def project_kernel(pick_ref, value_ref, out_ref, tokens_ref, partial_ref, held, sems):
    version = pick_ref[1]
    step = held.shape[0] // CHUNKS

    def copy(table_ref, chunk):
        rows = pl.ds(chunk * step, step)
        return pltpu.make_async_copy(table_ref.at[0, version, rows], held.at[rows], sems.at[chunk])

    @pl.when(pick_ref[0] == 1)
    def _():
        for chunk in range(CHUNKS):
            copy(out_ref, chunk).start()

    @pl.when(pick_ref[0] == 0)
    def _():
        for chunk in range(CHUNKS):
            copy(value_ref, chunk).start()

    for chunk in range(CHUNKS):
        copy(value_ref, chunk).wait()
        rows = pl.ds(chunk * step, step)
        partial_ref[rows, :] = matmul(held[rows, :], tokens_ref[...], NT).astype(jnp.bfloat16)


def project(use_out, version, w_value, w_out, tokens):
    rows, width = w_value.shape[2:]
    return pl.pallas_call(
        project_kernel,
        out_shape=jax.ShapeDtypeStruct((rows, tokens.shape[0]), jnp.bfloat16),
        in_specs=[in_smem(), in_place(), in_place(), in_vmem()],
        out_specs=in_vmem(),
        scratch_shapes=[
            pltpu.VMEM((rows, width), jnp.bfloat16),
            pltpu.SemaphoreType.DMA((CHUNKS,)),
        ],
        compiler_params=pltpu.CompilerParams(vmem_limit_bytes=VMEM_BYTES),
        cost_estimate=pl.CostEstimate(
            flops=2 * rows * width * tokens.shape[0],
            bytes_accessed=2 * rows * width,
            transcendentals=0,
        ),
        name="project",
    )(jnp.stack([use_out, version]), w_value, w_out, tokens)


def mix_kernel(
    outer, pick_ref, value_ref, mine_ref, arrived_ref, probs_ref, result_ref, keep_ref, send_ref, held, sems
):
    version = pick_ref[1]
    width = held.shape[1]
    step = width // CHUNKS

    def copy(chunk):
        columns = pl.ds(chunk * step, step)
        return pltpu.make_async_copy(
            value_ref.at[0, version, :, columns], held.at[:, columns], sems.at[chunk]
        )

    for chunk in range(CHUNKS):
        copy(chunk).start()

    def heads(dims):
        for head in range(probs_ref.shape[0]):
            rows = pl.ds(head * HEAD_DIM, HEAD_DIM)
            total = mine_ref[rows, :].astype(jnp.float32) + arrived_ref[rows, :].astype(jnp.float32)
            mixed = matmul(total.astype(jnp.bfloat16), probs_ref[head], dims)
            result_ref[rows, :] = mixed.astype(jnp.bfloat16)

    @pl.when(pick_ref[0] == 1)
    def _():
        heads(NN)

    @pl.when(pick_ref[0] == 0)
    def _():
        heads(NT)

    flipped = result_ref[...].T
    second_core = pick_ref[2] == 1
    shard = flipped.shape[0] // (2 * outer)
    for chunk in range(CHUNKS):
        copy(chunk).wait()
        columns = pl.ds(chunk * step, step)
        partial = matmul(flipped, held[:, columns], NN)
        for index in range(outer):
            low = partial[2 * index * shard : (2 * index + 1) * shard]
            high = partial[(2 * index + 1) * shard : (2 * index + 2) * shard]
            rows = pl.ds(index * shard, shard)
            keep_ref[rows, columns] = jnp.where(second_core, high, low).astype(jnp.bfloat16)
            send_ref[rows, columns] = jnp.where(second_core, low, high).astype(jnp.bfloat16)


def mix(natural, version, core, w_value, mine, arrived, probs, outer):
    rows, width = w_value.shape[2:]
    tokens = mine.shape[1]
    half = jax.ShapeDtypeStruct((tokens // 2, width), jnp.bfloat16)
    return pl.pallas_call(
        functools.partial(mix_kernel, outer),
        out_shape=(jax.ShapeDtypeStruct((rows, tokens), jnp.bfloat16), half, half),
        in_specs=[in_smem(), in_place(), in_vmem(), in_vmem(), in_vmem()],
        out_specs=(in_vmem(), in_vmem(), in_vmem()),
        scratch_shapes=[
            pltpu.VMEM((rows, width), jnp.bfloat16),
            pltpu.SemaphoreType.DMA((CHUNKS,)),
        ],
        compiler_params=pltpu.CompilerParams(vmem_limit_bytes=VMEM_BYTES),
        cost_estimate=pl.CostEstimate(
            flops=2 * rows * (width + tokens) * tokens,
            bytes_accessed=2 * rows * width,
            transcendentals=0,
        ),
        name="mix",
    )(jnp.stack([natural, version, core]), w_value, mine, arrived, probs)


def weight_grad_kernel(odd_ref, a0, a1, b0, b1, first0, first1, second0, second1, value_ref, out_ref):
    odd = odd_ref[0] == 1
    left_first = jnp.concatenate([a0[...], a1[...]], axis=1)
    left_second = jnp.concatenate([b0[...], b1[...]], axis=1)
    right_second = jnp.concatenate([second0[...], second1[...]], axis=0)
    right_first = jnp.concatenate([first0[...], first1[...]], axis=0)
    grad_first = matmul(left_first, right_second, NN)
    grad_second = matmul(left_second, right_first, NN)
    value_ref[0] = jnp.where(odd, grad_first, grad_second).astype(jnp.bfloat16)
    out_ref[0] = jnp.where(odd, grad_second, grad_first).astype(jnp.bfloat16)


def weight_grads(odd, first_results, second_results, first_full, second_full):
    rows, tokens = first_results[0].shape
    width = first_full[0].shape[1]
    step = rows // CHUNKS
    grad = jax.ShapeDtypeStruct((1, rows, width), jnp.bfloat16)
    left = pl.BlockSpec((step, tokens), lambda i: (i, 0))
    right = pl.BlockSpec((tokens, width), lambda i: (0, 0))
    wide = pl.BlockSpec((1, step, width), lambda i: (0, i, 0))
    return pl.pallas_call(
        weight_grad_kernel,
        grid=(CHUNKS,),
        out_shape=(grad, grad),
        in_specs=[in_smem()] + [left] * 4 + [right] * 4,
        out_specs=(wide, wide),
        compiler_params=pltpu.CompilerParams(vmem_limit_bytes=VMEM_BYTES),
        cost_estimate=pl.CostEstimate(
            flops=8 * rows * width * tokens, bytes_accessed=4 * rows * width, transcendentals=0
        ),
        name="weight_grads",
    )(odd[None], *first_results, *second_results, *first_full, *second_full)


def attention_probs(query, key_stash):
    tokens = query.shape[-1]
    query_heads = query.reshape(-1, HEAD_DIM, tokens)
    key_heads = key_stash.reshape(-1, HEAD_DIM, tokens)
    scores = jnp.einsum(
        "hdi,hdj->hij", query_heads, key_heads, preferred_element_type=jnp.float32
    ) * (1.0 / math.sqrt(HEAD_DIM))
    causal = lax.broadcasted_iota(jnp.int32, (tokens, tokens), 1) <= lax.broadcasted_iota(
        jnp.int32, (tokens, tokens), 0
    )
    scores = jnp.where(causal, scores, -jnp.inf)
    row_max = jnp.max(scores, axis=2, keepdims=True)
    expo = jnp.exp(scores - row_max)
    return (expo / jnp.sum(expo, axis=2, keepdims=True)).astype(jnp.bfloat16)


def on_device(section_input, query, key_stash, incoming, version, w_value, w_out):
    half = lax.axis_index("half")
    odd_flag = lax.axis_index("pair") % 2
    odd = odd_flag == 1
    place = lax.axis_index("tensor")
    core, row = place % 2, place // 2
    n_pairs = lax.axis_size("pair")
    n_tensor = lax.axis_size("tensor")
    outer = n_tensor // 2
    width = w_value.shape[3]
    shard = section_input.shape[1]

    def swap_half(array):
        return lax.ppermute(array, "half", [(0, 1), (1, 0)])

    def swap_core(array):
        return lax.ppermute(array, "tensor", [(i, i ^ 1) for i in range(n_tensor)])

    def to_row(array, delta):
        return lax.ppermute(array, "tensor", [(i, i ^ (2 * delta)) for i in range(n_tensor)])

    def to_other_half(array, delta):
        pairs = [
            (h * n_tensor + i, (1 - h) * n_tensor + (i ^ (2 * delta)))
            for h in range(2)
            for i in range(n_tensor)
        ]
        return lax.ppermute(array, ("half", "tensor"), pairs)

    def to_section_below(array, delta):
        pairs = [
            (p * n_tensor + i, (p - 1) * n_tensor + (i ^ (2 * delta)))
            for p in range(1, n_pairs, 2)
            for i in range(n_tensor)
        ]
        return lax.ppermute(array, ("pair", "tensor"), pairs)

    def own_columns(array):
        return lax.dynamic_slice_in_dim(array, half * width, width, 1)

    def other_columns(array):
        return lax.dynamic_slice_in_dim(array, (1 - half) * width, width, 1)

    def gathered(piece):
        return lax.all_gather(piece, "tensor", axis=0, tiled=True)

    def pieces(keep, arrived, addend):
        pair = (keep.astype(jnp.float32) + arrived.astype(jnp.float32)).reshape(outer, shard, width)
        taken = [lax.dynamic_index_in_dim(pair, row ^ d, 0, keepdims=False) for d in range(outer)]
        taken[0] = taken[0] + addend.astype(jnp.float32)
        return [piece.astype(jnp.bfloat16) for piece in taken]

    def added(parts):
        total = parts[0].astype(jnp.float32)
        for part in parts[1:]:
            total = total + part.astype(jnp.float32)
        return total.astype(jnp.bfloat16)

    first = jnp.where(odd, incoming[0], section_input[0])
    first_piece = [own_columns(first), swap_half(other_columns(first))]
    versions = [version[0], swap_half(version)[0]]
    stash = jnp.concatenate([query, key_stash])
    stash_other = swap_half(stash)
    input_piece = [own_columns(section_input[0]), swap_half(other_columns(section_input[0]))]

    first_full = [gathered(first_piece[0]), gathered(first_piece[1])]
    partial = [None, None]
    for m in (1, 0):
        partial[m] = project(odd_flag, versions[m], w_value, w_out, first_full[m])
    arrived = [swap_half(partial[1]), swap_half(partial[0])]
    probs = [attention_probs(query[0], key_stash[0]), attention_probs(stash_other[0], stash_other[1])]
    first_result, keep, send = [None, None], [None, None], [None, None]
    first_sent, second_piece, second_full = [None, None], [None, None], [None, None]
    for m in range(2):
        first_result[m], keep[m], send[m] = mix(
            odd_flag, versions[m], core, w_value, partial[m], arrived[m], probs[m], outer
        )
    for m in range(2):
        first_sent[m] = pieces(keep[m], swap_core(send[m]), first_piece[m])
        received = added([to_section_below(part, d) for d, part in enumerate(first_sent[m])])
        second_piece[m] = jnp.where(odd, input_piece[m], received)
    for m in range(2):
        second_full[m] = gathered(second_piece[m])
        partial[m] = project(1 - odd_flag, versions[m], w_value, w_out, second_full[m])
    arrived = [swap_half(partial[1]), swap_half(partial[0])]
    second_result, last_sent = [None, None], [None, None]
    for m in (1, 0):
        second_result[m], keep[m], send[m] = mix(
            1 - odd_flag, versions[m], core, w_value, partial[m], arrived[m], probs[m], outer
        )
    for m in (1, 0):
        second_sent = pieces(keep[m], swap_core(send[m]), second_piece[m])
        last_sent[m] = [jnp.where(odd, f, s) for f, s in zip(first_sent[m], second_sent)]
    other_grad = added([to_other_half(part, d) for d, part in enumerate(last_sent[1])])
    own_grad = added(
        [last_sent[0][0]] + [to_row(part, d + 1) for d, part in enumerate(last_sent[0][1:])]
    )
    input_grad = jnp.where(
        half == 0,
        jnp.concatenate([own_grad, other_grad], axis=1),
        jnp.concatenate([other_grad, own_grad], axis=1),
    )
    grad_value, grad_out = weight_grads(
        odd_flag, first_result, second_result, first_full, second_full
    )
    return (input_grad[None], grad_value, grad_out)


def solution(mesh):
    sections, tensor = mesh.devices.shape
    split = Mesh(mesh.devices.reshape(sections // 2, 2, tensor), ("pair", "half", "tensor"))
    slots = ("pair", "half")
    by_tokens = P(slots, "tensor", None)
    by_rows = P(slots, None, "tensor", None)
    return jax.shard_map(
        on_device,
        mesh=split,
        in_specs=(by_tokens, by_tokens, by_tokens, by_tokens, P(slots), by_rows, by_rows),
        out_specs=(by_tokens, by_tokens, by_tokens),
        check_vma=False,
    )
```

```python
import functools
import math

import jax
import jax.numpy as jnp
from jax import lax
from jax.experimental import pallas as pl
from jax.experimental.pallas import tpu as pltpu
from jax.sharding import Mesh, PartitionSpec as P

HEAD_DIM = 96
CHUNKS = 4
VMEM_BYTES = 8 * 2**20
GRAD_VMEM_BYTES = 16 * 2**20
PREPARE_VMEM_BYTES = 50 * 2**20
ODD, EVEN, OWN, OTHER, CORE, ROW, HALF = range(7)
NN = (((1,), (0,)), ((), ()))
NT = (((1,), (1,)), ((), ()))
TN = (((0,), (0,)), ((), ()))


def matmul(left_side, right_side, dims):
    return lax.dot_general(left_side, right_side, dims, preferred_element_type=jnp.float32)


def in_vmem():
    return pl.BlockSpec(memory_space=pltpu.VMEM)


def in_smem():
    return pl.BlockSpec(memory_space=pltpu.SMEM)


def in_hbm():
    return pl.BlockSpec(memory_space=pltpu.HBM)


def project_kernel(use_out, micro, index, facts_ref, value_ref, out_ref, tokens_ref, partial_ref):
    version = facts_ref[micro]
    flipped = tokens_ref[index].T

    def rows_of(table_ref):
        partial = matmul(table_ref[0, version], flipped, NN)
        partial_ref[...] = partial.astype(jnp.bfloat16)

    pl.when(facts_ref[use_out] == 1)(lambda: rows_of(out_ref))
    pl.when(facts_ref[use_out] == 0)(lambda: rows_of(value_ref))


def project(use_out, micro, index, facts, w_value, w_out, tokens):
    rows, width = w_value.shape[2:]
    return pl.pallas_call(
        functools.partial(project_kernel, use_out, micro, index),
        out_shape=jax.ShapeDtypeStruct((rows, tokens.shape[1]), jnp.bfloat16),
        in_specs=[in_smem(), in_vmem(), in_vmem(), in_vmem()],
        out_specs=in_vmem(),
        compiler_params=pltpu.CompilerParams(vmem_limit_bytes=VMEM_BYTES),
        cost_estimate=pl.CostEstimate(
            flops=2 * rows * width * tokens.shape[1],
            bytes_accessed=2 * rows * width,
            transcendentals=0,
        ),
        name="project",
    )(facts, w_value, w_out, tokens)


def mix_kernel(
    outer, natural, micro, facts_ref, value_ref, mine_ref, arrived_ref, probs_ref, result_ref, keep_ref, send_ref
):
    version = facts_ref[micro]
    width = value_ref.shape[3]
    step = width // CHUNKS

    def heads(dims):
        for head in range(probs_ref.shape[0]):
            rows = pl.ds(head * HEAD_DIM, HEAD_DIM)
            total = mine_ref[rows, :].astype(jnp.float32) + arrived_ref[rows, :].astype(jnp.float32)
            mixed = matmul(total.astype(jnp.bfloat16), probs_ref[head], dims)
            result_ref[rows, :] = mixed.astype(jnp.bfloat16)

    pl.when(facts_ref[natural] == 1)(lambda: heads(NN))
    pl.when(facts_ref[natural] == 0)(lambda: heads(NT))

    flipped = result_ref[...].T
    second_core = facts_ref[CORE] == 1
    shard = flipped.shape[0] // (2 * outer)
    for chunk in range(CHUNKS):
        columns = pl.ds(chunk * step, step)
        partial = matmul(flipped, value_ref[0, version, :, columns], NN)
        for index in range(outer):
            low = partial[2 * index * shard : (2 * index + 1) * shard]
            high = partial[(2 * index + 1) * shard : (2 * index + 2) * shard]
            keep_ref[index, :, columns] = jnp.where(second_core, high, low).astype(jnp.bfloat16)
            send_ref[index, :, columns] = jnp.where(second_core, low, high).astype(jnp.bfloat16)


def mix(natural, micro, facts, w_value, mine, arrived, probs, outer):
    rows, width = w_value.shape[2:]
    tokens = mine.shape[1]
    half = jax.ShapeDtypeStruct((outer, tokens // (2 * outer), width), jnp.bfloat16)
    return pl.pallas_call(
        functools.partial(mix_kernel, outer, natural, micro),
        out_shape=(jax.ShapeDtypeStruct((rows, tokens), jnp.bfloat16), half, half),
        in_specs=[in_smem(), in_vmem(), in_vmem(), in_vmem(), in_vmem()],
        out_specs=(in_vmem(), in_vmem(), in_vmem()),
        compiler_params=pltpu.CompilerParams(vmem_limit_bytes=VMEM_BYTES),
        cost_estimate=pl.CostEstimate(
            flops=2 * rows * (width + tokens) * tokens,
            bytes_accessed=2 * rows * width,
            transcendentals=0,
        ),
        name="mix",
    )(facts, w_value, mine, arrived, probs)


def combine_kernel(outer, last, facts_ref, keep_ref, arrived_ref, addend_ref, *refs):
    first_refs, sent_refs = refs[:-outer], refs[-outer:]
    for delta in range(outer):
        spot = facts_ref[ROW] ^ delta
        total = keep_ref[spot].astype(jnp.float32) + arrived_ref[spot].astype(jnp.float32)
        if delta == 0:
            total = total + addend_ref[...].astype(jnp.float32)
        total = total.astype(jnp.bfloat16)
        if last:
            total = jnp.where(facts_ref[ODD] == 1, first_refs[delta][...], total)
        sent_refs[delta][...] = total


def combine(facts, keep, arrived, addend, first_sent=()):
    outer, shard, width = keep.shape
    piece = jax.ShapeDtypeStruct((shard, width), jnp.bfloat16)
    return pl.pallas_call(
        functools.partial(combine_kernel, outer, len(first_sent) > 0),
        out_shape=(piece,) * outer,
        in_specs=[in_smem()] + [in_vmem()] * (3 + len(first_sent)),
        out_specs=(in_vmem(),) * outer,
        compiler_params=pltpu.CompilerParams(vmem_limit_bytes=VMEM_BYTES),
        cost_estimate=pl.CostEstimate(
            flops=2 * outer * shard * width,
            bytes_accessed=6 * outer * shard * width,
            transcendentals=0,
        ),
        name="combine",
    )(facts, keep, arrived, addend, *first_sent)


def assemble_kernel(n_own, facts_ref, *refs):
    grad_ref = refs[-1]
    width = refs[0].shape[1]

    def total(parts):
        value = parts[0][...].astype(jnp.float32)
        for part in parts[1:]:
            value = value + part[...].astype(jnp.float32)
        return value.astype(jnp.bfloat16)

    half = facts_ref[HALF]
    own = pl.ds(pl.multiple_of(half * width, width), width)
    other = pl.ds(pl.multiple_of((1 - half) * width, width), width)
    grad_ref[0, :, other] = total(refs[n_own:-1])
    grad_ref[0, :, own] = total(refs[:n_own])


def assemble(facts, own_parts, other_parts):
    shard, width = own_parts[0].shape
    return pl.pallas_call(
        functools.partial(assemble_kernel, len(own_parts)),
        out_shape=jax.ShapeDtypeStruct((1, shard, 2 * width), jnp.bfloat16),
        in_specs=[in_smem()] + [in_vmem()] * (len(own_parts) + len(other_parts)),
        out_specs=in_vmem(),
        compiler_params=pltpu.CompilerParams(vmem_limit_bytes=VMEM_BYTES),
        name="assemble",
    )(facts, *own_parts, *other_parts)


def weight_grad_kernel(facts_ref, a0, a1, b0, b1, first, second0, second1, value_ref, out_ref):
    odd = facts_ref[ODD] == 1
    tokens = a0.shape[1]
    left_first = jnp.concatenate([a0[...], a1[...]], axis=1)
    left_second = jnp.concatenate([b0[...], b1[...]], axis=1)
    right_second = jnp.concatenate([second0[0], second1[0]], axis=0)
    right_first = first[...].reshape(2 * tokens, first.shape[2])
    grad_first = matmul(left_first, right_second, NN)
    grad_second = matmul(left_second, right_first, NN)
    value_ref[0] = jnp.where(odd, grad_first, grad_second).astype(jnp.bfloat16)
    out_ref[0] = jnp.where(odd, grad_second, grad_first).astype(jnp.bfloat16)


def weight_grads(facts, first_results, second_results, first_full, second_full):
    rows, tokens = first_results[0].shape
    width = first_full.shape[2]
    step = rows // CHUNKS
    grad = jax.ShapeDtypeStruct((1, rows, width), jnp.bfloat16)
    left = pl.BlockSpec((step, tokens), lambda i: (i, 0))
    both = pl.BlockSpec((2, tokens, width), lambda i: (0, 0, 0))
    right = pl.BlockSpec((1, tokens, width), lambda i: (0, 0, 0))
    wide = pl.BlockSpec((1, step, width), lambda i: (0, i, 0))
    return pl.pallas_call(
        weight_grad_kernel,
        grid=(CHUNKS,),
        out_shape=(grad, grad),
        in_specs=[in_smem()] + [left] * 4 + [both, right, right],
        out_specs=(wide, wide),
        compiler_params=pltpu.CompilerParams(vmem_limit_bytes=GRAD_VMEM_BYTES),
        cost_estimate=pl.CostEstimate(
            flops=8 * rows * width * tokens, bytes_accessed=4 * rows * width, transcendentals=0
        ),
        name="weight_grads",
    )(facts, *first_results, *second_results, first_full, *second_full)


def prepare_kernel(query_ref, key_ref, value_ref, out_ref, probs_ref, value_held, out_held, sems):
    copies = [
        pltpu.make_async_copy(value_ref, value_held, sems.at[0]),
        pltpu.make_async_copy(out_ref, out_held, sems.at[1]),
    ]
    for copy in copies:
        copy.start()
    tokens = query_ref.shape[2]
    causal = lax.broadcasted_iota(jnp.int32, (tokens, tokens), 1) <= lax.broadcasted_iota(
        jnp.int32, (tokens, tokens), 0
    )
    for head in range(probs_ref.shape[0]):
        rows = pl.ds(head * HEAD_DIM, HEAD_DIM)
        scores = matmul(query_ref[0, rows, :], key_ref[0, rows, :], TN)
        scores = jnp.where(causal, scores * (1.0 / math.sqrt(HEAD_DIM)), -jnp.inf)
        expo = jnp.exp(scores - jnp.max(scores, axis=1, keepdims=True))
        probs_ref[head] = (expo / jnp.sum(expo, axis=1, keepdims=True)).astype(jnp.bfloat16)
    for copy in copies:
        copy.wait()


def prepare(query, key_stash, w_value, w_out):
    rows, tokens = query.shape[1:]
    heads = rows // HEAD_DIM
    table = jax.ShapeDtypeStruct(w_value.shape, jnp.bfloat16)
    return pl.pallas_call(
        prepare_kernel,
        out_shape=(jax.ShapeDtypeStruct((heads, tokens, tokens), jnp.bfloat16), table, table),
        in_specs=[in_vmem(), in_vmem(), in_hbm(), in_hbm()],
        out_specs=(in_vmem(), in_vmem(), in_vmem()),
        scratch_shapes=[pltpu.SemaphoreType.DMA((2,))],
        compiler_params=pltpu.CompilerParams(vmem_limit_bytes=PREPARE_VMEM_BYTES),
        cost_estimate=pl.CostEstimate(
            flops=2 * rows * tokens * tokens,
            bytes_accessed=4 * w_value.size,
            transcendentals=heads * tokens * tokens,
        ),
        name="prepare",
    )(query, key_stash, w_value, w_out)


def on_device(section_input, query, key_stash, incoming, version, w_value, w_out):
    half = lax.axis_index("half")
    odd_flag = lax.axis_index("pair") % 2
    odd = odd_flag == 1
    place = lax.axis_index("tensor")
    core, row = place % 2, place // 2
    n_pairs = lax.axis_size("pair")
    n_tensor = lax.axis_size("tensor")
    outer = n_tensor // 2
    width = w_value.shape[3]
    shard = section_input.shape[1]

    def swap_half(array):
        return lax.ppermute(array, "half", [(0, 1), (1, 0)])

    def swap_core(array):
        return lax.ppermute(array, "tensor", [(i, i ^ 1) for i in range(n_tensor)])

    def to_row(array, delta):
        return lax.ppermute(array, "tensor", [(i, i ^ (2 * delta)) for i in range(n_tensor)])

    def to_other_half(array, delta):
        pairs = [
            (h * n_tensor + i, (1 - h) * n_tensor + (i ^ (2 * delta)))
            for h in range(2)
            for i in range(n_tensor)
        ]
        return lax.ppermute(array, ("half", "tensor"), pairs)

    def to_section_below(array, delta):
        pairs = [
            (p * n_tensor + i, (p - 1) * n_tensor + (i ^ (2 * delta)))
            for p in range(1, n_pairs, 2)
            for i in range(n_tensor)
        ]
        return lax.ppermute(array, ("pair", "tensor"), pairs)

    def own_columns(array):
        return lax.dynamic_slice_in_dim(array, half * width, width, 1)

    def other_columns(array):
        return lax.dynamic_slice_in_dim(array, (1 - half) * width, width, 1)

    def gathered(pieces):
        return lax.all_gather(jnp.stack(pieces), "tensor", axis=1, tiled=True)

    micros = (OWN, OTHER)
    first = jnp.where(odd, incoming[0], section_input[0])
    first_piece = [own_columns(first), swap_half(other_columns(first))]
    other_version = swap_half(version)[0]
    facts = jnp.stack([odd_flag, 1 - odd_flag, version[0], other_version, core, row, half])
    own_probs, w_value, w_out = prepare(query, key_stash, w_value, w_out)
    probs = [own_probs, swap_half(own_probs)]

    first_full = gathered(first_piece)
    partial = [None, None]
    for m in (1, 0):
        partial[m] = project(ODD, micros[m], m, facts, w_value, w_out, first_full)
    arrived = [swap_half(partial[1]), swap_half(partial[0])]
    later_input, _ = lax.optimization_barrier((section_input[0], partial[0]))
    input_piece = [own_columns(later_input), swap_half(other_columns(later_input))]
    first_result, first_sent = [None, None], [None, None]
    second_piece, second_full = [None, None], [None, None]
    for m in range(2):
        first_result[m], keep, send = mix(
            ODD, micros[m], facts, w_value, partial[m], arrived[m], probs[m], outer
        )
        first_sent[m] = combine(facts, keep, swap_core(send), first_piece[m])
        received = [to_section_below(part, d) for d, part in enumerate(first_sent[m])]
        total = sum(part.astype(jnp.float32) for part in received).astype(jnp.bfloat16)
        second_piece[m] = jnp.where(odd, input_piece[m], total)
    for m in range(2):
        second_full[m] = gathered([second_piece[m]])
        partial[m] = project(EVEN, micros[m], 0, facts, w_value, w_out, second_full[m])
    arrived = [swap_half(partial[1]), swap_half(partial[0])]
    second_result, last_sent = [None, None], [None, None]
    for m in (1, 0):
        second_result[m], keep, send = mix(
            EVEN, micros[m], facts, w_value, partial[m], arrived[m], probs[m], outer
        )
        last_sent[m] = combine(facts, keep, swap_core(send), second_piece[m], first_sent[m])
    other_parts = [to_other_half(part, d) for d, part in enumerate(last_sent[1])]
    own_parts = [last_sent[0][0]] + [to_row(part, d + 1) for d, part in enumerate(last_sent[0][1:])]
    second_result, _ = lax.optimization_barrier((second_result, last_sent))
    grad_value, grad_out = weight_grads(
        facts, first_result, second_result, first_full, second_full
    )
    own_parts, other_parts, _ = lax.optimization_barrier((own_parts, other_parts, grad_value))
    input_grad = assemble(facts, own_parts, other_parts)
    return (input_grad, grad_value, grad_out)


def solution(mesh):
    sections, tensor = mesh.devices.shape
    split = Mesh(mesh.devices.reshape(sections // 2, 2, tensor), ("pair", "half", "tensor"))
    slots = ("pair", "half")
    by_tokens = P(slots, "tensor", None)
    by_rows = P(slots, None, "tensor", None)
    return jax.shard_map(
        on_device,
        mesh=split,
        in_specs=(by_tokens, by_tokens, by_tokens, by_tokens, P(slots), by_rows, by_rows),
        out_specs=(by_tokens, by_tokens, by_tokens),
        check_vma=False,
    )
```

```python
import functools
import math

import jax
import jax.numpy as jnp
from jax import lax
from jax.experimental import pallas as pl
from jax.experimental.pallas import tpu as pltpu
from jax.sharding import Mesh, PartitionSpec as P

HEAD_DIM = 96
CHUNKS = 4
VMEM_BYTES = 8 * 2**20
GRAD_VMEM_BYTES = 16 * 2**20
FIRST_VMEM_BYTES = 48 * 2**20
SECOND_VMEM_BYTES = 47 * 2**20
ODD, EVEN, OWN, OTHER, CORE, ROW, HALF = range(7)
SMALL = pl.CostEstimate(flops=1, bytes_accessed=1, transcendentals=0)
NN = (((1,), (0,)), ((), ()))
NT = (((1,), (1,)), ((), ()))
TN = (((0,), (0,)), ((), ()))


def matmul(left_side, right_side, dims):
    return lax.dot_general(left_side, right_side, dims, preferred_element_type=jnp.float32)


def in_vmem():
    return pl.BlockSpec(memory_space=pltpu.VMEM)


def in_smem():
    return pl.BlockSpec(memory_space=pltpu.SMEM)


def in_hbm():
    return pl.BlockSpec(memory_space=pltpu.HBM)


def project_kernel(micro, index, facts_ref, table_ref, tokens_ref, partial_ref):
    flipped = tokens_ref[index].T
    partial = matmul(table_ref[0, facts_ref[micro]], flipped, NN)
    partial_ref[...] = partial.astype(jnp.bfloat16)


def project(micro, index, facts, table, tokens):
    rows, width = table.shape[2:]
    return pl.pallas_call(
        functools.partial(project_kernel, micro, index),
        out_shape=jax.ShapeDtypeStruct((rows, tokens.shape[1]), jnp.bfloat16),
        in_specs=[in_smem(), in_vmem(), in_vmem()],
        out_specs=in_vmem(),
        compiler_params=pltpu.CompilerParams(vmem_limit_bytes=VMEM_BYTES),
        cost_estimate=SMALL,
        name="project",
    )(facts, table, tokens)


def mix_kernel(
    outer, natural, micro, facts_ref, first_ref, second_ref, mine_ref, arrived_ref, probs_ref, result_ref, keep_ref, send_ref
):
    version = facts_ref[micro]
    step = first_ref.shape[3] // CHUNKS

    def heads(dims):
        for head in range(probs_ref.shape[0]):
            rows = pl.ds(head * HEAD_DIM, HEAD_DIM)
            total = mine_ref[rows, :].astype(jnp.float32) + arrived_ref[rows, :].astype(jnp.float32)
            mixed = matmul(total.astype(jnp.bfloat16), probs_ref[head], dims)
            result_ref[rows, :] = mixed.astype(jnp.bfloat16)

    pl.when(facts_ref[natural] == 1)(lambda: heads(NN))
    pl.when(facts_ref[natural] == 0)(lambda: heads(NT))

    def spread(value_ref):
        flipped = result_ref[...].T
        second_core = facts_ref[CORE] == 1
        shard = flipped.shape[0] // (2 * outer)
        for chunk in range(CHUNKS):
            columns = pl.ds(chunk * step, step)
            partial = matmul(flipped, value_ref[0, version, :, columns], NN)
            for index in range(outer):
                low = partial[2 * index * shard : (2 * index + 1) * shard]
                high = partial[(2 * index + 1) * shard : (2 * index + 2) * shard]
                keep_ref[index, :, columns] = jnp.where(second_core, high, low).astype(jnp.bfloat16)
                send_ref[index, :, columns] = jnp.where(second_core, low, high).astype(jnp.bfloat16)

    pl.when(facts_ref[ODD] == 0)(lambda: spread(first_ref))
    pl.when(facts_ref[ODD] == 1)(lambda: spread(second_ref))


def mix(natural, micro, facts, tables, mine, arrived, probs, outer):
    rows, width = tables[0].shape[2:]
    tokens = mine.shape[1]
    half = jax.ShapeDtypeStruct((outer, tokens // (2 * outer), width), jnp.bfloat16)
    return pl.pallas_call(
        functools.partial(mix_kernel, outer, natural, micro),
        out_shape=(jax.ShapeDtypeStruct((rows, tokens), jnp.bfloat16), half, half),
        in_specs=[in_smem()] + [in_vmem()] * 5,
        out_specs=(in_vmem(), in_vmem(), in_vmem()),
        compiler_params=pltpu.CompilerParams(vmem_limit_bytes=VMEM_BYTES),
        cost_estimate=SMALL,
        name="mix",
    )(facts, *tables, mine, arrived, probs)


def combine_kernel(outer, last, facts_ref, keep_ref, arrived_ref, addend_ref, *refs):
    first_refs, sent_refs = refs[:-outer], refs[-outer:]
    for delta in range(outer):
        spot = facts_ref[ROW] ^ delta
        total = keep_ref[spot].astype(jnp.float32) + arrived_ref[spot].astype(jnp.float32)
        if delta == 0:
            total = total + addend_ref[...].astype(jnp.float32)
        total = total.astype(jnp.bfloat16)
        if last:
            total = jnp.where(facts_ref[ODD] == 1, first_refs[delta][...], total)
        sent_refs[delta][...] = total


def combine(facts, keep, arrived, addend, first_sent=()):
    outer, shard, width = keep.shape
    piece = jax.ShapeDtypeStruct((shard, width), jnp.bfloat16)
    return pl.pallas_call(
        functools.partial(combine_kernel, outer, len(first_sent) > 0),
        out_shape=(piece,) * outer,
        in_specs=[in_smem()] + [in_vmem()] * (3 + len(first_sent)),
        out_specs=(in_vmem(),) * outer,
        compiler_params=pltpu.CompilerParams(vmem_limit_bytes=VMEM_BYTES),
        cost_estimate=SMALL,
        name="combine",
    )(facts, keep, arrived, addend, *first_sent)


def assemble_kernel(n_own, facts_ref, *refs):
    grad_ref = refs[-1]
    width = refs[0].shape[1]

    def total(parts):
        value = parts[0][...].astype(jnp.float32)
        for part in parts[1:]:
            value = value + part[...].astype(jnp.float32)
        return value.astype(jnp.bfloat16)

    half = facts_ref[HALF]
    own = pl.ds(pl.multiple_of(half * width, width), width)
    other = pl.ds(pl.multiple_of((1 - half) * width, width), width)
    grad_ref[0, :, other] = total(refs[n_own:-1])
    grad_ref[0, :, own] = total(refs[:n_own])


def assemble(facts, own_parts, other_parts):
    shard, width = own_parts[0].shape
    return pl.pallas_call(
        functools.partial(assemble_kernel, len(own_parts)),
        out_shape=jax.ShapeDtypeStruct((1, shard, 2 * width), jnp.bfloat16),
        in_specs=[in_smem()] + [in_vmem()] * (len(own_parts) + len(other_parts)),
        out_specs=in_vmem(),
        compiler_params=pltpu.CompilerParams(vmem_limit_bytes=VMEM_BYTES),
        name="assemble",
    )(facts, *own_parts, *other_parts)


def weight_grad_kernel(facts_ref, a0, a1, b0, b1, first, second0, second1, value_ref, out_ref):
    odd = facts_ref[ODD] == 1
    tokens = a0.shape[1]
    left_first = jnp.concatenate([a0[...], a1[...]], axis=1)
    left_second = jnp.concatenate([b0[...], b1[...]], axis=1)
    right_second = jnp.concatenate([second0[0], second1[0]], axis=0)
    right_first = first[...].reshape(2 * tokens, first.shape[2])
    grad_first = matmul(left_first, right_second, NN)
    grad_second = matmul(left_second, right_first, NN)
    value_ref[0] = jnp.where(odd, grad_first, grad_second).astype(jnp.bfloat16)
    out_ref[0] = jnp.where(odd, grad_second, grad_first).astype(jnp.bfloat16)


def weight_grads(facts, first_results, second_results, first_full, second_full):
    rows, tokens = first_results[0].shape
    width = first_full.shape[2]
    step = rows // CHUNKS
    grad = jax.ShapeDtypeStruct((1, rows, width), jnp.bfloat16)
    left = pl.BlockSpec((step, tokens), lambda i: (i, 0))
    both = pl.BlockSpec((2, tokens, width), lambda i: (0, 0, 0))
    right = pl.BlockSpec((1, tokens, width), lambda i: (0, 0, 0))
    wide = pl.BlockSpec((1, step, width), lambda i: (0, i, 0))
    return pl.pallas_call(
        weight_grad_kernel,
        grid=(CHUNKS,),
        out_shape=(grad, grad),
        in_specs=[in_smem()] + [left] * 4 + [both, right, right],
        out_specs=(wide, wide),
        compiler_params=pltpu.CompilerParams(vmem_limit_bytes=GRAD_VMEM_BYTES),
        cost_estimate=SMALL,
        name="weight_grads",
    )(facts, *first_results, *second_results, first_full, *second_full)


def load_table(use_out, value_ref, out_ref, table_ref, sems):
    step = table_ref.shape[2] // CHUNKS
    spots = [
        (slice(None), version, pl.ds(chunk * step, step))
        for version in range(2)
        for chunk in range(CHUNKS)
    ]

    def copies(source_ref):
        return [
            pltpu.make_async_copy(source_ref.at[spot], table_ref.at[spot], sems.at[i])
            for i, spot in enumerate(spots)
        ]

    @pl.when(use_out)
    def _():
        for copy in copies(out_ref):
            copy.start()

    @pl.when(jnp.logical_not(use_out))
    def _():
        for copy in copies(value_ref):
            copy.start()

    return copies(value_ref)


def prepare_kernel(odd_ref, query_ref, key_ref, value_ref, out_ref, probs_ref, table_ref, sems):
    waits = load_table(odd_ref[0] == 1, value_ref, out_ref, table_ref, sems)
    tokens = query_ref.shape[2]
    causal = lax.broadcasted_iota(jnp.int32, (tokens, tokens), 1) <= lax.broadcasted_iota(
        jnp.int32, (tokens, tokens), 0
    )
    for head in range(probs_ref.shape[0]):
        rows = pl.ds(head * HEAD_DIM, HEAD_DIM)
        scores = matmul(query_ref[0, rows, :], key_ref[0, rows, :], TN)
        scores = jnp.where(causal, scores * (1.0 / math.sqrt(HEAD_DIM)), -jnp.inf)
        expo = jnp.exp(scores - jnp.max(scores, axis=1, keepdims=True))
        probs_ref[head] = (expo / jnp.sum(expo, axis=1, keepdims=True)).astype(jnp.bfloat16)
    for wait in waits:
        wait.wait()


def prepare(odd_flag, query, key_stash, w_value, w_out):
    rows, tokens = query.shape[1:]
    heads = rows // HEAD_DIM
    table = jax.ShapeDtypeStruct(w_value.shape, jnp.bfloat16)
    return pl.pallas_call(
        prepare_kernel,
        out_shape=(jax.ShapeDtypeStruct((heads, tokens, tokens), jnp.bfloat16), table),
        in_specs=[in_smem(), in_vmem(), in_vmem(), in_hbm(), in_hbm()],
        out_specs=(in_vmem(), in_vmem()),
        scratch_shapes=[pltpu.SemaphoreType.DMA((2 * CHUNKS,))],
        compiler_params=pltpu.CompilerParams(vmem_limit_bytes=FIRST_VMEM_BYTES),
        cost_estimate=SMALL,
        name="prepare",
    )(odd_flag[None], query, key_stash, w_value, w_out)


def second_kernel(odd_ref, value_ref, out_ref, table_ref, sems):
    for wait in load_table(odd_ref[0] == 0, value_ref, out_ref, table_ref, sems):
        wait.wait()


def second_table(odd_flag, w_value, w_out):
    return pl.pallas_call(
        second_kernel,
        out_shape=jax.ShapeDtypeStruct(w_value.shape, jnp.bfloat16),
        in_specs=[in_smem(), in_hbm(), in_hbm()],
        out_specs=in_vmem(),
        scratch_shapes=[pltpu.SemaphoreType.DMA((2 * CHUNKS,))],
        compiler_params=pltpu.CompilerParams(vmem_limit_bytes=SECOND_VMEM_BYTES),
        cost_estimate=SMALL,
        name="second_table",
    )(odd_flag[None], w_value, w_out)


def on_device(section_input, query, key_stash, incoming, version, w_value, w_out):
    half = lax.axis_index("half")
    odd_flag = lax.axis_index("pair") % 2
    odd = odd_flag == 1
    place = lax.axis_index("tensor")
    core, row = place % 2, place // 2
    n_pairs = lax.axis_size("pair")
    n_tensor = lax.axis_size("tensor")
    outer = n_tensor // 2
    width = w_value.shape[3]
    shard = section_input.shape[1]

    def swap_half(array):
        return lax.ppermute(array, "half", [(0, 1), (1, 0)])

    def swap_core(array):
        return lax.ppermute(array, "tensor", [(i, i ^ 1) for i in range(n_tensor)])

    def to_row(array, delta):
        return lax.ppermute(array, "tensor", [(i, i ^ (2 * delta)) for i in range(n_tensor)])

    def to_other_half(array, delta):
        pairs = [
            (h * n_tensor + i, (1 - h) * n_tensor + (i ^ (2 * delta)))
            for h in range(2)
            for i in range(n_tensor)
        ]
        return lax.ppermute(array, ("half", "tensor"), pairs)

    def to_section_below(array, delta):
        pairs = [
            (p * n_tensor + i, (p - 1) * n_tensor + (i ^ (2 * delta)))
            for p in range(1, n_pairs, 2)
            for i in range(n_tensor)
        ]
        return lax.ppermute(array, ("pair", "tensor"), pairs)

    def own_columns(array):
        return lax.dynamic_slice_in_dim(array, half * width, width, 1)

    def other_columns(array):
        return lax.dynamic_slice_in_dim(array, (1 - half) * width, width, 1)

    def gathered(pieces):
        return lax.all_gather(jnp.stack(pieces), "tensor", axis=1, tiled=True)

    micros = (OWN, OTHER)
    first = jnp.where(odd, incoming[0], section_input[0])
    first_piece = [own_columns(first), swap_half(other_columns(first))]
    other_version = swap_half(version)[0]
    facts = jnp.stack([odd_flag, 1 - odd_flag, version[0], other_version, core, row, half])
    own_probs, first_table = prepare(odd_flag, query, key_stash, w_value, w_out)
    other_probs = swap_half(own_probs)
    input_other = swap_half(other_columns(section_input[0]))

    first_full = gathered(first_piece)
    first_full, other_probs, input_other = lax.optimization_barrier(
        (first_full, other_probs, input_other)
    )
    probs = [own_probs, other_probs]
    input_piece = [own_columns(section_input[0]), input_other]
    partial = [None, None]
    for m in (1, 0):
        partial[m] = project(micros[m], m, facts, first_table, first_full)
    arrived = [swap_half(partial[1]), swap_half(partial[0])]
    later_tables, _ = lax.optimization_barrier(((w_value, w_out), partial[0]))
    tables = [first_table, second_table(odd_flag, *later_tables)]
    first_result, first_sent = [None, None], [None, None]
    second_piece, second_full = [None, None], [None, None]
    for m in range(2):
        first_result[m], keep, send = mix(
            ODD, micros[m], facts, tables, partial[m], arrived[m], probs[m], outer
        )
        first_sent[m] = combine(facts, keep, swap_core(send), first_piece[m])
    for m in range(2):
        received = [to_section_below(part, d) for d, part in enumerate(first_sent[m])]
        total = sum(part.astype(jnp.float32) for part in received).astype(jnp.bfloat16)
        second_piece[m] = jnp.where(odd, input_piece[m], total)
    for m in range(2):
        second_full[m] = gathered([second_piece[m]])
        partial[m] = project(micros[m], 0, facts, tables[1], second_full[m])
    arrived = [swap_half(partial[1]), swap_half(partial[0])]
    second_result, last_sent = [None, None], [None, None]
    for m in (1, 0):
        second_result[m], keep, send = mix(
            EVEN, micros[m], facts, tables, partial[m], arrived[m], probs[m], outer
        )
        last_sent[m] = combine(facts, keep, swap_core(send), second_piece[m], first_sent[m])
    other_parts = [to_other_half(part, d) for d, part in enumerate(last_sent[1])]
    own_parts = [last_sent[0][0]] + [to_row(part, d + 1) for d, part in enumerate(last_sent[0][1:])]
    second_result, _ = lax.optimization_barrier((second_result, last_sent))
    grad_value, grad_out = weight_grads(
        facts, first_result, second_result, first_full, second_full
    )
    own_parts, other_parts, _ = lax.optimization_barrier((own_parts, other_parts, grad_value))
    input_grad = assemble(facts, own_parts, other_parts)
    return (input_grad, grad_value, grad_out)


def solution(mesh):
    sections, tensor = mesh.devices.shape
    split = Mesh(mesh.devices.reshape(sections // 2, 2, tensor), ("pair", "half", "tensor"))
    slots = ("pair", "half")
    by_tokens = P(slots, "tensor", None)
    by_rows = P(slots, None, "tensor", None)
    return jax.shard_map(
        on_device,
        mesh=split,
        in_specs=(by_tokens, by_tokens, by_tokens, by_tokens, P(slots), by_rows, by_rows),
        out_specs=(by_tokens, by_tokens, by_tokens),
        check_vma=False,
    )
```

```python
import functools
import math

import jax
import jax.numpy as jnp
from jax import lax
from jax.experimental import pallas as pl
from jax.experimental.pallas import tpu as pltpu
from jax.sharding import Mesh, PartitionSpec as P

HEAD_DIM = 96
CHUNKS = 4
VMEM_BYTES = 8 * 2**20
GRAD_VMEM_BYTES = 16 * 2**20
FIRST_VMEM_BYTES = 50 * 2**20
VALUE_VMEM_BYTES = 47 * 2**20
OUT_VMEM_BYTES = 42 * 2**20
ODD, EVEN, VERSION, CORE, ROW, HALF = range(6)
LANES = 128
NOTE_ROWS = 16
SMALL = pl.CostEstimate(flops=1, bytes_accessed=1, transcendentals=0)
NN = (((1,), (0,)), ((), ()))
NT = (((1,), (1,)), ((), ()))
TN = (((0,), (0,)), ((), ()))


def matmul(left_side, right_side, dims):
    return lax.dot_general(left_side, right_side, dims, preferred_element_type=jnp.float32)


def in_vmem():
    return pl.BlockSpec(memory_space=pltpu.VMEM)


def in_smem():
    return pl.BlockSpec(memory_space=pltpu.SMEM)


def in_hbm():
    return pl.BlockSpec(memory_space=pltpu.HBM)


def in_place():
    return pl.BlockSpec(memory_space=pl.ANY)


def picked_version(index, facts_ref, message_ref):
    if index == 0:
        return facts_ref[VERSION]
    note = message_ref[message_ref.shape[0] - NOTE_ROWS :, :].astype(jnp.float32)
    return (jnp.max(note) > 0.5).astype(jnp.int32)


def first_project_kernel(
    index, facts_ref, message_ref, value_ref, out_ref, tokens_ref, partial_ref, held, sems
):
    version = picked_version(index, facts_ref, message_ref)
    step = held.shape[0] // CHUNKS

    def copy(table_ref, chunk):
        rows = pl.ds(chunk * step, step)
        return pltpu.make_async_copy(table_ref.at[0, version, rows], held.at[rows], sems.at[chunk])

    def start(table_ref):
        for chunk in range(CHUNKS):
            copy(table_ref, chunk).start()

    pl.when(facts_ref[ODD] == 1)(lambda: start(out_ref))
    pl.when(facts_ref[ODD] == 0)(lambda: start(value_ref))
    flipped = tokens_ref[index].T
    for chunk in range(CHUNKS):
        copy(value_ref, chunk).wait()
        rows = pl.ds(chunk * step, step)
        partial_ref[rows, :] = matmul(held[rows, :], flipped, NN).astype(jnp.bfloat16)


def first_project(index, facts, message, w_value, w_out, tokens):
    rows, width = w_value.shape[2:]
    return pl.pallas_call(
        functools.partial(first_project_kernel, index),
        out_shape=jax.ShapeDtypeStruct((rows, tokens.shape[1]), jnp.bfloat16),
        in_specs=[in_smem(), in_vmem(), in_hbm(), in_hbm(), in_vmem()],
        out_specs=in_vmem(),
        scratch_shapes=[
            pltpu.VMEM((rows, width), jnp.bfloat16),
            pltpu.SemaphoreType.DMA((CHUNKS,)),
        ],
        compiler_params=pltpu.CompilerParams(vmem_limit_bytes=FIRST_VMEM_BYTES),
        cost_estimate=SMALL,
        name="first_project",
    )(facts, message, w_value, w_out, tokens)


def project_kernel(index, facts_ref, message_ref, value_ref, out_ref, tokens_ref, partial_ref):
    version = picked_version(index, facts_ref, message_ref)
    flipped = tokens_ref[0].T

    def rows_of(table_ref):
        partial_ref[...] = matmul(table_ref[0, version], flipped, NN).astype(jnp.bfloat16)

    pl.when(facts_ref[ODD] == 1)(lambda: rows_of(value_ref))
    pl.when(facts_ref[ODD] == 0)(lambda: rows_of(out_ref))


def project(index, facts, message, tables, tokens):
    rows = tables[0].shape[2]
    return pl.pallas_call(
        functools.partial(project_kernel, index),
        out_shape=jax.ShapeDtypeStruct((rows, tokens.shape[1]), jnp.bfloat16),
        in_specs=[in_smem()] + [in_vmem()] * 4,
        out_specs=in_vmem(),
        compiler_params=pltpu.CompilerParams(vmem_limit_bytes=VMEM_BYTES),
        cost_estimate=SMALL,
        name="project",
    )(facts, message, *tables, tokens)


def mix_kernel(
    outer,
    natural,
    index,
    facts_ref,
    message_ref,
    value_ref,
    mine_ref,
    arrived_ref,
    probs_ref,
    result_ref,
    keep_ref,
    send_ref,
):
    version = picked_version(index, facts_ref, message_ref)
    step = value_ref.shape[3] // CHUNKS
    tokens = mine_ref.shape[1]

    def heads(dims):
        for head in range(mine_ref.shape[0] // HEAD_DIM):
            rows = pl.ds(head * HEAD_DIM, HEAD_DIM)
            total = mine_ref[rows, :].astype(jnp.float32) + arrived_ref[rows, :].astype(jnp.float32)
            probs = probs_ref[head * tokens : (head + 1) * tokens, :]
            mixed = matmul(total.astype(jnp.bfloat16), probs, dims)
            result_ref[rows, :] = mixed.astype(jnp.bfloat16)

    pl.when(facts_ref[natural] == 1)(lambda: heads(NN))
    pl.when(facts_ref[natural] == 0)(lambda: heads(NT))

    flipped = result_ref[...].T
    second_core = facts_ref[CORE] == 1
    shard = tokens // (2 * outer)
    for chunk in range(CHUNKS):
        columns = pl.ds(chunk * step, step)
        partial = matmul(flipped, value_ref[0, version, :, columns], NN)
        for place in range(outer):
            low = partial[2 * place * shard : (2 * place + 1) * shard]
            high = partial[(2 * place + 1) * shard : (2 * place + 2) * shard]
            keep_ref[place, :, columns] = jnp.where(second_core, high, low).astype(jnp.bfloat16)
            send_ref[place, :, columns] = jnp.where(second_core, low, high).astype(jnp.bfloat16)


def mix(natural, index, facts, messages, w_value, mine, arrived, outer):
    rows, width = w_value.shape[2:]
    tokens = mine.shape[1]
    half = jax.ShapeDtypeStruct((outer, tokens // (2 * outer), width), jnp.bfloat16)
    return pl.pallas_call(
        functools.partial(mix_kernel, outer, natural, index),
        out_shape=(jax.ShapeDtypeStruct((rows, tokens), jnp.bfloat16), half, half),
        in_specs=[in_smem()] + [in_vmem()] * 5,
        out_specs=(in_vmem(), in_vmem(), in_vmem()),
        compiler_params=pltpu.CompilerParams(vmem_limit_bytes=VMEM_BYTES),
        cost_estimate=SMALL,
        name="mix",
    )(facts, messages[1], w_value, mine, arrived, messages[index])


def combine_kernel(outer, last, facts_ref, keep_ref, arrived_ref, addend_ref, *refs):
    first_refs, sent_refs = refs[:-outer], refs[-outer:]
    for delta in range(outer):
        spot = facts_ref[ROW] ^ delta
        total = keep_ref[spot].astype(jnp.float32) + arrived_ref[spot].astype(jnp.float32)
        if delta == 0:
            total = total + addend_ref[...].astype(jnp.float32)
        total = total.astype(jnp.bfloat16)
        if last:
            total = jnp.where(facts_ref[ODD] == 1, first_refs[delta][...], total)
        sent_refs[delta][...] = total


def combine(facts, keep, arrived, addend, first_sent=()):
    outer, shard, width = keep.shape
    piece = jax.ShapeDtypeStruct((shard, width), jnp.bfloat16)
    return pl.pallas_call(
        functools.partial(combine_kernel, outer, len(first_sent) > 0),
        out_shape=(piece,) * outer,
        in_specs=[in_smem()] + [in_vmem()] * (3 + len(first_sent)),
        out_specs=(in_vmem(),) * outer,
        compiler_params=pltpu.CompilerParams(vmem_limit_bytes=VMEM_BYTES),
        cost_estimate=SMALL,
        name="combine",
    )(facts, keep, arrived, addend, *first_sent)


def assemble_kernel(n_own, facts_ref, *refs):
    grad_ref = refs[-1]
    width = refs[0].shape[1]

    def total(parts):
        value = parts[0][...].astype(jnp.float32)
        for part in parts[1:]:
            value = value + part[...].astype(jnp.float32)
        return value.astype(jnp.bfloat16)

    half = facts_ref[HALF]
    own = pl.ds(pl.multiple_of(half * width, width), width)
    other = pl.ds(pl.multiple_of((1 - half) * width, width), width)
    grad_ref[0, :, other] = total(refs[n_own:-1])
    grad_ref[0, :, own] = total(refs[:n_own])


def assemble(facts, own_parts, other_parts):
    shard, width = own_parts[0].shape
    return pl.pallas_call(
        functools.partial(assemble_kernel, len(own_parts)),
        out_shape=jax.ShapeDtypeStruct((1, shard, 2 * width), jnp.bfloat16),
        in_specs=[in_smem()] + [in_vmem()] * (len(own_parts) + len(other_parts)),
        out_specs=in_vmem(),
        compiler_params=pltpu.CompilerParams(vmem_limit_bytes=VMEM_BYTES),
        name="assemble",
    )(facts, *own_parts, *other_parts)


def weight_grad_kernel(facts_ref, a0, a1, b0, b1, first, second0, second1, value_ref, out_ref):
    odd = facts_ref[ODD] == 1
    tokens = a0.shape[1]
    left_first = jnp.concatenate([a0[...], a1[...]], axis=1)
    left_second = jnp.concatenate([b0[...], b1[...]], axis=1)
    right_second = jnp.concatenate([second0[0], second1[0]], axis=0)
    right_first = first[...].reshape(2 * tokens, first.shape[2])
    grad_first = matmul(left_first, right_second, NN)
    grad_second = matmul(left_second, right_first, NN)
    value_ref[0] = jnp.where(odd, grad_first, grad_second).astype(jnp.bfloat16)
    out_ref[0] = jnp.where(odd, grad_second, grad_first).astype(jnp.bfloat16)


def weight_grads(facts, first_results, second_results, first_full, second_full):
    rows, tokens = first_results[0].shape
    width = first_full.shape[2]
    step = rows // CHUNKS
    grad = jax.ShapeDtypeStruct((1, rows, width), jnp.bfloat16)
    left = pl.BlockSpec((step, tokens), lambda i: (i, 0))
    both = pl.BlockSpec((2, tokens, width), lambda i: (0, 0, 0))
    right = pl.BlockSpec((1, tokens, width), lambda i: (0, 0, 0))
    wide = pl.BlockSpec((1, step, width), lambda i: (0, i, 0))
    return pl.pallas_call(
        weight_grad_kernel,
        grid=(CHUNKS,),
        out_shape=(grad, grad),
        in_specs=[in_smem()] + [left] * 4 + [both, right, right],
        out_specs=(wide, wide),
        compiler_params=pltpu.CompilerParams(vmem_limit_bytes=GRAD_VMEM_BYTES),
        cost_estimate=SMALL,
        name="weight_grads",
    )(facts, *first_results, *second_results, first_full, *second_full)


def pack_kernel(
    facts_ref, query_ref, key_ref, input_ref, message_ref, own_ref, query_held, key_held, input_held, sems
):
    pairs = ((query_ref, query_held), (key_ref, key_held), (input_ref, input_held))
    copies = [
        pltpu.make_async_copy(source, held, sems.at[i]) for i, (source, held) in enumerate(pairs)
    ]
    for copy in copies:
        copy.start()
    tokens = query_ref.shape[2]
    shard, width = own_ref.shape
    heads = query_ref.shape[1] // HEAD_DIM
    causal = lax.broadcasted_iota(jnp.int32, (tokens, tokens), 1) <= lax.broadcasted_iota(
        jnp.int32, (tokens, tokens), 0
    )
    copies[0].wait()
    copies[1].wait()
    for head in range(heads):
        rows = pl.ds(head * HEAD_DIM, HEAD_DIM)
        scores = matmul(query_held[0, rows, :], key_held[0, rows, :], TN)
        scores = jnp.where(causal, scores * (1.0 / math.sqrt(HEAD_DIM)), -jnp.inf)
        expo = jnp.exp(scores - jnp.max(scores, axis=1, keepdims=True))
        probs = (expo / jnp.sum(expo, axis=1, keepdims=True)).astype(jnp.bfloat16)
        message_ref[head * tokens : (head + 1) * tokens, :] = probs
    copies[2].wait()
    half = facts_ref[HALF]
    own_ref[...] = input_held[0, :, pl.ds(pl.multiple_of(half * width, width), width)]
    other = input_held[0, :, pl.ds(pl.multiple_of((1 - half) * width, width), width)]
    for block in range(width // LANES):
        start = heads * tokens + block * shard
        message_ref[start : start + shard, :] = other[:, block * LANES : (block + 1) * LANES]
    note = jnp.zeros((NOTE_ROWS, LANES), jnp.int32) + facts_ref[VERSION]
    message_ref[message_ref.shape[0] - NOTE_ROWS :, :] = note.astype(jnp.bfloat16)


def pack(facts, query, key_stash, section_input):
    rows, tokens = query.shape[1:]
    shard = section_input.shape[1]
    width = section_input.shape[2] // 2
    length = rows // HEAD_DIM * tokens + width // LANES * shard + NOTE_ROWS
    return pl.pallas_call(
        pack_kernel,
        out_shape=(
            jax.ShapeDtypeStruct((length, LANES), jnp.bfloat16),
            jax.ShapeDtypeStruct((shard, width), jnp.bfloat16),
        ),
        in_specs=[in_smem(), in_place(), in_place(), in_place()],
        out_specs=(in_vmem(), in_vmem()),
        scratch_shapes=[
            pltpu.VMEM(query.shape, jnp.bfloat16),
            pltpu.VMEM(query.shape, jnp.bfloat16),
            pltpu.VMEM(section_input.shape, jnp.bfloat16),
            pltpu.SemaphoreType.DMA((3,)),
        ],
        compiler_params=pltpu.CompilerParams(vmem_limit_bytes=VMEM_BYTES),
        cost_estimate=SMALL,
        name="pack",
    )(facts, query, key_stash, section_input)


def load_kernel(source_ref, table_ref, sems):
    step = table_ref.shape[2] // CHUNKS
    copies = []
    for version in range(2):
        for chunk in range(CHUNKS):
            spot = (slice(None), version, pl.ds(chunk * step, step))
            copies.append(
                pltpu.make_async_copy(
                    source_ref.at[spot], table_ref.at[spot], sems.at[version * CHUNKS + chunk]
                )
            )
    for copy in copies:
        copy.start()
    for copy in copies:
        copy.wait()


def load_table(table, grant):
    return pl.pallas_call(
        load_kernel,
        out_shape=jax.ShapeDtypeStruct(table.shape, jnp.bfloat16),
        in_specs=[in_hbm()],
        out_specs=in_vmem(),
        scratch_shapes=[pltpu.SemaphoreType.DMA((2 * CHUNKS,))],
        compiler_params=pltpu.CompilerParams(vmem_limit_bytes=grant),
        cost_estimate=SMALL,
        name="load_table",
    )(table)


def arrive_kernel(index, heads, facts_ref, input_ref, *refs):
    parts, piece_ref = refs[:-1], refs[-1]
    shard, width = piece_ref.shape

    @pl.when(facts_ref[ODD] == 1)
    def _():
        if index == 0:
            piece_ref[...] = input_ref[...]
        else:
            for block in range(width // LANES):
                start = heads * LANES + block * shard
                piece_ref[:, block * LANES : (block + 1) * LANES] = input_ref[start : start + shard, :]

    @pl.when(facts_ref[ODD] == 0)
    def _():
        total = parts[0][...].astype(jnp.float32)
        for part in parts[1:]:
            total = total + part[...].astype(jnp.float32)
        piece_ref[...] = total.astype(jnp.bfloat16)


def arrive(index, heads, facts, source, parts):
    return pl.pallas_call(
        functools.partial(arrive_kernel, index, heads),
        out_shape=jax.ShapeDtypeStruct(parts[0].shape, jnp.bfloat16),
        in_specs=[in_smem()] + [in_vmem()] * (1 + len(parts)),
        out_specs=in_vmem(),
        compiler_params=pltpu.CompilerParams(vmem_limit_bytes=VMEM_BYTES),
        cost_estimate=SMALL,
        name="arrive",
    )(facts, source, *parts)


def on_device(section_input, query, key_stash, incoming, version, w_value, w_out):
    half = lax.axis_index("half")
    odd_flag = lax.axis_index("pair") % 2
    odd = odd_flag == 1
    place = lax.axis_index("tensor")
    core, row = place % 2, place // 2
    n_pairs = lax.axis_size("pair")
    n_tensor = lax.axis_size("tensor")
    outer = n_tensor // 2
    width = w_value.shape[3]
    shard = section_input.shape[1]

    def swap_half(array):
        return lax.ppermute(array, "half", [(0, 1), (1, 0)])

    def swap_core(array):
        return lax.ppermute(array, "tensor", [(i, i ^ 1) for i in range(n_tensor)])

    def to_row(array, delta):
        return lax.ppermute(array, "tensor", [(i, i ^ (2 * delta)) for i in range(n_tensor)])

    def to_other_half(array, delta):
        pairs = [
            (h * n_tensor + i, (1 - h) * n_tensor + (i ^ (2 * delta)))
            for h in range(2)
            for i in range(n_tensor)
        ]
        return lax.ppermute(array, ("half", "tensor"), pairs)

    def swap_section(array, delta):
        pairs = [
            (p * n_tensor + i, (p ^ 1) * n_tensor + (i ^ (2 * delta)))
            for p in range(n_pairs)
            for i in range(n_tensor)
        ]
        return lax.ppermute(array, ("pair", "tensor"), pairs)

    def own_columns(array):
        return lax.dynamic_slice_in_dim(array, half * width, width, 1)

    def other_columns(array):
        return lax.dynamic_slice_in_dim(array, (1 - half) * width, width, 1)

    def gathered(pieces):
        return lax.all_gather(jnp.stack(pieces), "tensor", axis=1, tiled=True)

    heads = query.shape[1] // HEAD_DIM
    facts = jnp.stack([odd_flag, 1 - odd_flag, version[0], core, row, half])
    first = jnp.where(odd, incoming[0], section_input[0])
    first_piece = [own_columns(first), swap_half(other_columns(first))]
    own_message, input_own = pack(facts, query, key_stash, section_input)
    other_message = swap_half(own_message)
    first_full = gathered(first_piece)
    first_full, other_message = lax.optimization_barrier((first_full, other_message))
    messages = [own_message, other_message]

    partial = [None, None]
    partial[1] = first_project(1, facts, other_message, w_value, w_out, first_full)
    partial[0] = first_project(0, facts, other_message, w_value, w_out, first_full)
    arrived = [swap_half(partial[1]), swap_half(partial[0])]
    later_value, _ = lax.optimization_barrier((w_value, partial))
    value_table = load_table(later_value, VALUE_VMEM_BYTES)
    first_result, first_sent = [None, None], [None, None]
    second_piece, second_full = [None, None], [None, None]
    for m in range(2):
        first_result[m], keep, send = mix(
            ODD, m, facts, messages, value_table, partial[m], arrived[m], outer
        )
        first_sent[m] = combine(facts, keep, swap_core(send), first_piece[m])
    later_out, _ = lax.optimization_barrier((w_out, first_sent))
    out_table = load_table(later_out, OUT_VMEM_BYTES)
    input_own, other_input, _ = lax.optimization_barrier((input_own, other_message, out_table))
    for m in range(2):
        received = [swap_section(part, d) for d, part in enumerate(first_sent[m])]
        source = other_input if m else input_own
        second_piece[m] = arrive(m, heads, facts, source, received)
    tables = (value_table, out_table)
    for m in range(2):
        second_full[m] = gathered([second_piece[m]])
        partial[m] = project(m, facts, other_message, tables, second_full[m])
    arrived = [swap_half(partial[1]), swap_half(partial[0])]
    second_result, last_sent = [None, None], [None, None]
    for m in (1, 0):
        second_result[m], keep, send = mix(
            EVEN, m, facts, messages, value_table, partial[m], arrived[m], outer
        )
        last_sent[m] = combine(facts, keep, swap_core(send), second_piece[m], first_sent[m])
    other_parts = [to_other_half(part, d) for d, part in enumerate(last_sent[1])]
    own_parts = [last_sent[0][0]] + [to_row(part, d + 1) for d, part in enumerate(last_sent[0][1:])]
    second_result, _ = lax.optimization_barrier((second_result, last_sent))
    grad_value, grad_out = weight_grads(
        facts, first_result, second_result, first_full, second_full
    )
    own_parts, other_parts, _ = lax.optimization_barrier((own_parts, other_parts, grad_value))
    input_grad = assemble(facts, own_parts, other_parts)
    return (input_grad, grad_value, grad_out)


def solution(mesh):
    sections, tensor = mesh.devices.shape
    split = Mesh(mesh.devices.reshape(sections // 2, 2, tensor), ("pair", "half", "tensor"))
    slots = ("pair", "half")
    by_tokens = P(slots, "tensor", None)
    by_rows = P(slots, None, "tensor", None)
    return jax.shard_map(
        on_device,
        mesh=split,
        in_specs=(by_tokens, by_tokens, by_tokens, by_tokens, P(slots), by_rows, by_rows),
        out_specs=(by_tokens, by_tokens, by_tokens),
        check_vma=False,
    )
```

```python
import functools
import math

import jax
import jax.numpy as jnp
from jax import lax
from jax.experimental import pallas as pl
from jax.experimental.pallas import tpu as pltpu
from jax.sharding import Mesh, PartitionSpec as P

HEAD_DIM = 96
CHUNKS = 4
VMEM_BYTES = 8 * 2**20
GRAD_VMEM_BYTES = 16 * 2**20
FIRST_VMEM_BYTES = 46 * 2**20
VALUE_VMEM_BYTES = 47 * 2**20
OUT_VMEM_BYTES = 42 * 2**20
ODD, EVEN, VERSION, CORE, ROW, HALF = range(6)
LANES = 128
NOTE_ROWS = 16
SMALL = pl.CostEstimate(flops=1, bytes_accessed=1, transcendentals=0)
NN = (((1,), (0,)), ((), ()))
NT = (((1,), (1,)), ((), ()))
TN = (((0,), (0,)), ((), ()))


def matmul(left_side, right_side, dims):
    return lax.dot_general(left_side, right_side, dims, preferred_element_type=jnp.float32)


def in_vmem():
    return pl.BlockSpec(memory_space=pltpu.VMEM)


def in_smem():
    return pl.BlockSpec(memory_space=pltpu.SMEM)


def in_hbm():
    return pl.BlockSpec(memory_space=pltpu.HBM)


def in_place():
    return pl.BlockSpec(memory_space=pl.ANY)


def picked_version(index, facts_ref, message_ref):
    if index == 0:
        return facts_ref[VERSION]
    note = message_ref[message_ref.shape[0] - NOTE_ROWS :, :].astype(jnp.float32)
    return (jnp.max(note) > 0.5).astype(jnp.int32)


def project_kernel(index, facts_ref, message_ref, *refs):
    tables, (tokens_ref, partial_ref) = refs[:-2], refs[-2:]
    version = picked_version(index, facts_ref, message_ref)
    flipped = tokens_ref[index].T

    def rows_of(table_ref):
        partial_ref[...] = matmul(table_ref[0, version], flipped, NN).astype(jnp.bfloat16)

    if len(tables) == 1:
        rows_of(tables[0])
    else:
        pl.when(facts_ref[ODD] == 1)(lambda: rows_of(tables[0]))
        pl.when(facts_ref[ODD] == 0)(lambda: rows_of(tables[1]))


def project(index, facts, message, tables, tokens):
    rows = tables[0].shape[2]
    return pl.pallas_call(
        functools.partial(project_kernel, index),
        out_shape=jax.ShapeDtypeStruct((rows, tokens.shape[1]), jnp.bfloat16),
        in_specs=[in_smem()] + [in_vmem()] * (2 + len(tables)),
        out_specs=in_vmem(),
        compiler_params=pltpu.CompilerParams(vmem_limit_bytes=VMEM_BYTES),
        cost_estimate=SMALL,
        name="project",
    )(facts, message, *tables, tokens)


def mix_kernel(
    outer,
    natural,
    index,
    facts_ref,
    message_ref,
    value_ref,
    mine_ref,
    arrived_ref,
    probs_ref,
    result_ref,
    keep_ref,
    send_ref,
):
    version = picked_version(index, facts_ref, message_ref)
    step = value_ref.shape[3] // CHUNKS
    tokens = mine_ref.shape[1]

    def heads(dims):
        for head in range(mine_ref.shape[0] // HEAD_DIM):
            rows = pl.ds(head * HEAD_DIM, HEAD_DIM)
            total = mine_ref[rows, :].astype(jnp.float32) + arrived_ref[rows, :].astype(jnp.float32)
            probs = probs_ref[head * tokens : (head + 1) * tokens, :]
            mixed = matmul(total.astype(jnp.bfloat16), probs, dims)
            result_ref[rows, :] = mixed.astype(jnp.bfloat16)

    pl.when(facts_ref[natural] == 1)(lambda: heads(NN))
    pl.when(facts_ref[natural] == 0)(lambda: heads(NT))

    flipped = result_ref[...].T
    second_core = facts_ref[CORE] == 1
    shard = tokens // (2 * outer)
    for chunk in range(CHUNKS):
        columns = pl.ds(chunk * step, step)
        partial = matmul(flipped, value_ref[0, version, :, columns], NN)
        for place in range(outer):
            low = partial[2 * place * shard : (2 * place + 1) * shard]
            high = partial[(2 * place + 1) * shard : (2 * place + 2) * shard]
            keep_ref[place, :, columns] = jnp.where(second_core, high, low).astype(jnp.bfloat16)
            send_ref[place, :, columns] = jnp.where(second_core, low, high).astype(jnp.bfloat16)


def mix(natural, index, facts, messages, w_value, mine, arrived, outer):
    rows, width = w_value.shape[2:]
    tokens = mine.shape[1]
    half = jax.ShapeDtypeStruct((outer, tokens // (2 * outer), width), jnp.bfloat16)
    return pl.pallas_call(
        functools.partial(mix_kernel, outer, natural, index),
        out_shape=(jax.ShapeDtypeStruct((rows, tokens), jnp.bfloat16), half, half),
        in_specs=[in_smem()] + [in_vmem()] * 5,
        out_specs=(in_vmem(), in_vmem(), in_vmem()),
        compiler_params=pltpu.CompilerParams(vmem_limit_bytes=VMEM_BYTES),
        cost_estimate=SMALL,
        name="mix",
    )(facts, messages[1], w_value, mine, arrived, messages[index])


def combine_kernel(outer, last, index, facts_ref, keep_ref, arrived_ref, addend_ref, *refs):
    first_refs, sent_refs = refs[:-outer], refs[-outer:]
    for delta in range(outer):
        spot = facts_ref[ROW] ^ delta
        total = keep_ref[spot].astype(jnp.float32) + arrived_ref[spot].astype(jnp.float32)
        if delta == 0:
            total = total + addend_ref[index].astype(jnp.float32)
        total = total.astype(jnp.bfloat16)
        if last:
            total = jnp.where(facts_ref[ODD] == 1, first_refs[delta][...], total)
        sent_refs[delta][...] = total


def combine(index, facts, keep, arrived, addend, first_sent=()):
    outer, shard, width = keep.shape
    piece = jax.ShapeDtypeStruct((shard, width), jnp.bfloat16)
    return pl.pallas_call(
        functools.partial(combine_kernel, outer, len(first_sent) > 0, index),
        out_shape=(piece,) * outer,
        in_specs=[in_smem()] + [in_vmem()] * (3 + len(first_sent)),
        out_specs=(in_vmem(),) * outer,
        compiler_params=pltpu.CompilerParams(vmem_limit_bytes=VMEM_BYTES),
        cost_estimate=SMALL,
        name="combine",
    )(facts, keep, arrived, addend, *first_sent)


def assemble_kernel(n_own, facts_ref, *refs):
    grad_ref = refs[-1]
    width = refs[0].shape[1]

    def total(parts):
        value = parts[0][...].astype(jnp.float32)
        for part in parts[1:]:
            value = value + part[...].astype(jnp.float32)
        return value.astype(jnp.bfloat16)

    half = facts_ref[HALF]
    own = pl.ds(pl.multiple_of(half * width, width), width)
    other = pl.ds(pl.multiple_of((1 - half) * width, width), width)
    grad_ref[0, :, other] = total(refs[n_own:-1])
    grad_ref[0, :, own] = total(refs[:n_own])


def assemble(facts, own_parts, other_parts):
    shard, width = own_parts[0].shape
    return pl.pallas_call(
        functools.partial(assemble_kernel, len(own_parts)),
        out_shape=jax.ShapeDtypeStruct((1, shard, 2 * width), jnp.bfloat16),
        in_specs=[in_smem()] + [in_vmem()] * (len(own_parts) + len(other_parts)),
        out_specs=in_vmem(),
        compiler_params=pltpu.CompilerParams(vmem_limit_bytes=VMEM_BYTES),
        name="assemble",
    )(facts, *own_parts, *other_parts)


def weight_grad_kernel(facts_ref, a0, a1, b0, b1, first, second, value_ref, out_ref):
    odd = facts_ref[ODD] == 1
    tokens = a0.shape[1]
    left_first = jnp.concatenate([a0[...], a1[...]], axis=1)
    left_second = jnp.concatenate([b0[...], b1[...]], axis=1)
    right_second = second[...].reshape(2 * tokens, second.shape[2])
    right_first = first[...].reshape(2 * tokens, first.shape[2])
    grad_first = matmul(left_first, right_second, NN)
    grad_second = matmul(left_second, right_first, NN)
    value_ref[0] = jnp.where(odd, grad_first, grad_second).astype(jnp.bfloat16)
    out_ref[0] = jnp.where(odd, grad_second, grad_first).astype(jnp.bfloat16)


def weight_grads(facts, first_results, second_results, first_full, second_full):
    rows, tokens = first_results[0].shape
    width = first_full.shape[2]
    step = rows // CHUNKS
    grad = jax.ShapeDtypeStruct((1, rows, width), jnp.bfloat16)
    left = pl.BlockSpec((step, tokens), lambda i: (i, 0))
    both = pl.BlockSpec((2, tokens, width), lambda i: (0, 0, 0))
    wide = pl.BlockSpec((1, step, width), lambda i: (0, i, 0))
    return pl.pallas_call(
        weight_grad_kernel,
        grid=(CHUNKS,),
        out_shape=(grad, grad),
        in_specs=[in_smem()] + [left] * 4 + [both] * 2,
        out_specs=(wide, wide),
        compiler_params=pltpu.CompilerParams(vmem_limit_bytes=GRAD_VMEM_BYTES),
        cost_estimate=SMALL,
        name="weight_grads",
    )(facts, *first_results, *second_results, first_full, second_full)


def load(source_ref, table_ref, sems):
    step = table_ref.shape[2] // CHUNKS
    copies = []
    for version in range(2):
        for chunk in range(CHUNKS):
            spot = (slice(None), version, pl.ds(chunk * step, step))
            copies.append(
                pltpu.make_async_copy(
                    source_ref.at[spot], table_ref.at[spot], sems.at[version * CHUNKS + chunk]
                )
            )
    return copies


def pack_kernel(
    facts_ref,
    query_ref,
    key_ref,
    input_ref,
    value_ref,
    out_ref,
    message_ref,
    own_ref,
    table_ref,
    query_held,
    key_held,
    input_held,
    sems,
    table_sems,
):
    pairs = ((query_ref, query_held), (key_ref, key_held), (input_ref, input_held))
    copies = [
        pltpu.make_async_copy(source, held, sems.at[i]) for i, (source, held) in enumerate(pairs)
    ]
    for copy in copies:
        copy.start()

    @pl.when(facts_ref[ODD] == 1)
    def _():
        for copy in load(out_ref, table_ref, table_sems):
            copy.start()

    @pl.when(facts_ref[ODD] == 0)
    def _():
        for copy in load(value_ref, table_ref, table_sems):
            copy.start()

    tokens = query_ref.shape[2]
    shard, width = own_ref.shape
    heads = query_ref.shape[1] // HEAD_DIM
    causal = lax.broadcasted_iota(jnp.int32, (tokens, tokens), 1) <= lax.broadcasted_iota(
        jnp.int32, (tokens, tokens), 0
    )
    copies[0].wait()
    copies[1].wait()
    for head in range(heads):
        rows = pl.ds(head * HEAD_DIM, HEAD_DIM)
        scores = matmul(query_held[0, rows, :], key_held[0, rows, :], TN)
        scores = jnp.where(causal, scores * (1.0 / math.sqrt(HEAD_DIM)), -jnp.inf)
        expo = jnp.exp(scores - jnp.max(scores, axis=1, keepdims=True))
        probs = (expo / jnp.sum(expo, axis=1, keepdims=True)).astype(jnp.bfloat16)
        message_ref[head * tokens : (head + 1) * tokens, :] = probs
    copies[2].wait()
    half = facts_ref[HALF]
    own_ref[...] = input_held[0, :, pl.ds(pl.multiple_of(half * width, width), width)]
    other = input_held[0, :, pl.ds(pl.multiple_of((1 - half) * width, width), width)]
    for block in range(width // LANES):
        start = heads * tokens + block * shard
        message_ref[start : start + shard, :] = other[:, block * LANES : (block + 1) * LANES]
    note = jnp.zeros((NOTE_ROWS, LANES), jnp.int32) + facts_ref[VERSION]
    message_ref[message_ref.shape[0] - NOTE_ROWS :, :] = note.astype(jnp.bfloat16)
    for copy in load(value_ref, table_ref, table_sems):
        copy.wait()


def pack(facts, query, key_stash, section_input, w_value, w_out):
    rows, tokens = query.shape[1:]
    shard = section_input.shape[1]
    width = section_input.shape[2] // 2
    length = rows // HEAD_DIM * tokens + width // LANES * shard + NOTE_ROWS
    return pl.pallas_call(
        pack_kernel,
        out_shape=(
            jax.ShapeDtypeStruct((length, LANES), jnp.bfloat16),
            jax.ShapeDtypeStruct((shard, width), jnp.bfloat16),
            jax.ShapeDtypeStruct(w_value.shape, jnp.bfloat16),
        ),
        in_specs=[in_smem(), in_place(), in_place(), in_place(), in_hbm(), in_hbm()],
        out_specs=(in_vmem(), in_vmem(), in_vmem()),
        scratch_shapes=[
            pltpu.VMEM(query.shape, jnp.bfloat16),
            pltpu.VMEM(query.shape, jnp.bfloat16),
            pltpu.VMEM(section_input.shape, jnp.bfloat16),
            pltpu.SemaphoreType.DMA((3,)),
            pltpu.SemaphoreType.DMA((2 * CHUNKS,)),
        ],
        compiler_params=pltpu.CompilerParams(vmem_limit_bytes=FIRST_VMEM_BYTES),
        cost_estimate=SMALL,
        name="pack",
    )(facts, query, key_stash, section_input, w_value, w_out)


def load_kernel(source_ref, table_ref, sems):
    copies = load(source_ref, table_ref, sems)
    for copy in copies:
        copy.start()
    for copy in copies:
        copy.wait()


def load_table(table, grant):
    return pl.pallas_call(
        load_kernel,
        out_shape=jax.ShapeDtypeStruct(table.shape, jnp.bfloat16),
        in_specs=[in_hbm()],
        out_specs=in_vmem(),
        scratch_shapes=[pltpu.SemaphoreType.DMA((2 * CHUNKS,))],
        compiler_params=pltpu.CompilerParams(vmem_limit_bytes=grant),
        cost_estimate=SMALL,
        name="load_table",
    )(table)


def arrive_kernel(outer, facts_ref, own_ref, message_ref, *refs):
    parts, pair_ref = refs[:-1], refs[-1]
    shard, width = own_ref.shape

    @pl.when(facts_ref[ODD] == 1)
    def _():
        pair_ref[0] = own_ref[...]
        first_row = message_ref.shape[0] - NOTE_ROWS - width // LANES * shard
        for block in range(width // LANES):
            start = first_row + block * shard
            columns = pl.ds(block * LANES, LANES)
            pair_ref[1, :, columns] = message_ref[start : start + shard, :]

    @pl.when(facts_ref[ODD] == 0)
    def _():
        for index in range(2):
            total = parts[index * outer][...].astype(jnp.float32)
            for part in parts[index * outer + 1 : (index + 1) * outer]:
                total = total + part[...].astype(jnp.float32)
            pair_ref[index] = total.astype(jnp.bfloat16)


def arrive(facts, input_own, message, parts):
    return pl.pallas_call(
        functools.partial(arrive_kernel, len(parts) // 2),
        out_shape=jax.ShapeDtypeStruct((2,) + input_own.shape, jnp.bfloat16),
        in_specs=[in_smem()] + [in_vmem()] * (2 + len(parts)),
        out_specs=in_vmem(),
        compiler_params=pltpu.CompilerParams(vmem_limit_bytes=VMEM_BYTES),
        cost_estimate=SMALL,
        name="arrive",
    )(facts, input_own, message, *parts)


def on_device(section_input, query, key_stash, incoming, version, w_value, w_out):
    half = lax.axis_index("half")
    odd_flag = lax.axis_index("pair") % 2
    odd = odd_flag == 1
    place = lax.axis_index("tensor")
    core, row = place % 2, place // 2
    n_pairs = lax.axis_size("pair")
    n_tensor = lax.axis_size("tensor")
    outer = n_tensor // 2
    width = w_value.shape[3]
    shard = section_input.shape[1]

    def swap_half(array):
        return lax.ppermute(array, "half", [(0, 1), (1, 0)])

    def swap_core(array):
        return lax.ppermute(array, "tensor", [(i, i ^ 1) for i in range(n_tensor)])

    def to_row(array, delta):
        return lax.ppermute(array, "tensor", [(i, i ^ (2 * delta)) for i in range(n_tensor)])

    def to_other_half(array, delta):
        pairs = [
            (h * n_tensor + i, (1 - h) * n_tensor + (i ^ (2 * delta)))
            for h in range(2)
            for i in range(n_tensor)
        ]
        return lax.ppermute(array, ("half", "tensor"), pairs)

    def swap_section(array, delta):
        pairs = [
            (p * n_tensor + i, (p ^ 1) * n_tensor + (i ^ (2 * delta)))
            for p in range(n_pairs)
            for i in range(n_tensor)
        ]
        return lax.ppermute(array, ("pair", "tensor"), pairs)

    def own_columns(array):
        return lax.dynamic_slice_in_dim(array, half * width, width, 1)

    def other_columns(array):
        return lax.dynamic_slice_in_dim(array, (1 - half) * width, width, 1)

    def gathered(pair):
        return lax.all_gather(pair, "tensor", axis=1, tiled=True)

    facts = jnp.stack([odd_flag, 1 - odd_flag, version[0], core, row, half])
    first = jnp.where(odd, incoming[0], section_input[0])
    first_pair = jnp.stack([own_columns(first), swap_half(other_columns(first))])
    own_message, input_own, first_table = pack(
        facts, query, key_stash, section_input, w_value, w_out
    )
    other_message = swap_half(own_message)
    first_full = gathered(first_pair)
    first_full, other_message = lax.optimization_barrier((first_full, other_message))
    messages = [own_message, other_message]

    partial = [None, None]
    for m in (1, 0):
        partial[m] = project(m, facts, other_message, (first_table,), first_full)
    arrived = [swap_half(partial[1]), swap_half(partial[0])]
    later_value, _ = lax.optimization_barrier((w_value, partial))
    value_table = load_table(later_value, VALUE_VMEM_BYTES)
    first_result, first_sent = [None, None], [None, None]
    for m in range(2):
        first_result[m], keep, send = mix(
            ODD, m, facts, messages, value_table, partial[m], arrived[m], outer
        )
        first_sent[m] = combine(m, facts, keep, swap_core(send), first_pair)
    later_out, _ = lax.optimization_barrier((w_out, first_sent))
    out_table = load_table(later_out, OUT_VMEM_BYTES)
    input_own, _ = lax.optimization_barrier((input_own, out_table))
    received = [swap_section(part, d) for m in range(2) for d, part in enumerate(first_sent[m])]
    second_pair = arrive(facts, input_own, other_message, received)
    second_full = gathered(second_pair)
    for m in range(2):
        partial[m] = project(m, facts, other_message, (value_table, out_table), second_full)
    arrived = [swap_half(partial[1]), swap_half(partial[0])]
    second_result, last_sent = [None, None], [None, None]
    for m in (1, 0):
        second_result[m], keep, send = mix(
            EVEN, m, facts, messages, value_table, partial[m], arrived[m], outer
        )
        last_sent[m] = combine(m, facts, keep, swap_core(send), second_pair, first_sent[m])
    other_parts = [to_other_half(part, d) for d, part in enumerate(last_sent[1])]
    own_parts = [last_sent[0][0]] + [to_row(part, d + 1) for d, part in enumerate(last_sent[0][1:])]
    second_result, _ = lax.optimization_barrier((second_result, last_sent))
    grad_value, grad_out = weight_grads(
        facts, first_result, second_result, first_full, second_full
    )
    own_parts, other_parts, _ = lax.optimization_barrier((own_parts, other_parts, grad_value))
    input_grad = assemble(facts, own_parts, other_parts)
    return (input_grad, grad_value, grad_out)


def solution(mesh):
    sections, tensor = mesh.devices.shape
    split = Mesh(mesh.devices.reshape(sections // 2, 2, tensor), ("pair", "half", "tensor"))
    slots = ("pair", "half")
    by_tokens = P(slots, "tensor", None)
    by_rows = P(slots, None, "tensor", None)
    return jax.shard_map(
        on_device,
        mesh=split,
        in_specs=(by_tokens, by_tokens, by_tokens, by_tokens, P(slots), by_rows, by_rows),
        out_specs=(by_tokens, by_tokens, by_tokens),
        check_vma=False,
    )
```

```python
import functools
import math

import jax
import jax.numpy as jnp
from jax import lax
from jax.experimental import pallas as pl
from jax.experimental.pallas import tpu as pltpu
from jax.sharding import Mesh, PartitionSpec as P

HEAD_DIM = 96
CHUNKS = 4
VMEM_BYTES = 8 * 2**20
GRAD_VMEM_BYTES = 16 * 2**20
FIRST_VMEM_BYTES = 46 * 2**20
VALUE_VMEM_BYTES = 47 * 2**20
OUT_VMEM_BYTES = 42 * 2**20
ODD, EVEN, VERSION, CORE, ROW, HALF = range(6)
LANES = 128
NOTE_ROWS = 16
SMALL = pl.CostEstimate(flops=1, bytes_accessed=1, transcendentals=0)
NN = (((1,), (0,)), ((), ()))
NT = (((1,), (1,)), ((), ()))
TN = (((0,), (0,)), ((), ()))


def matmul(left_side, right_side, dims):
    return lax.dot_general(left_side, right_side, dims, preferred_element_type=jnp.float32)


def in_vmem():
    return pl.BlockSpec(memory_space=pltpu.VMEM)


def in_smem():
    return pl.BlockSpec(memory_space=pltpu.SMEM)


def in_hbm():
    return pl.BlockSpec(memory_space=pltpu.HBM)


def in_place():
    return pl.BlockSpec(memory_space=pl.ANY)


def picked_version(index, facts_ref, note_ref):
    if index == 0:
        return facts_ref[VERSION]
    return (jnp.max(note_ref[...].astype(jnp.float32)) > 0.5).astype(jnp.int32)


def project_kernel(index, spot, facts_ref, note_ref, *refs):
    tables, (tokens_ref, partial_ref) = refs[:-2], refs[-2:]
    version = picked_version(index, facts_ref, note_ref)
    flipped = tokens_ref[spot].T

    def rows_of(table_ref):
        partial_ref[...] = matmul(table_ref[0, version], flipped, NN).astype(jnp.bfloat16)

    if len(tables) == 1:
        rows_of(tables[0])
    else:
        pl.when(facts_ref[ODD] == 1)(lambda: rows_of(tables[0]))
        pl.when(facts_ref[ODD] == 0)(lambda: rows_of(tables[1]))


def project(index, spot, facts, note, tables, tokens):
    rows = tables[0].shape[2]
    return pl.pallas_call(
        functools.partial(project_kernel, index, spot),
        out_shape=jax.ShapeDtypeStruct((rows, tokens.shape[1]), jnp.bfloat16),
        in_specs=[in_smem()] + [in_vmem()] * (2 + len(tables)),
        out_specs=in_vmem(),
        compiler_params=pltpu.CompilerParams(vmem_limit_bytes=VMEM_BYTES),
        cost_estimate=SMALL,
        name="project",
    )(facts, note, *tables, tokens)


def mix_kernel(
    outer,
    natural,
    index,
    facts_ref,
    note_ref,
    value_ref,
    mine_ref,
    arrived_ref,
    probs_ref,
    result_ref,
    keep_ref,
    send_ref,
):
    version = picked_version(index, facts_ref, note_ref)
    step = value_ref.shape[3] // CHUNKS
    tokens = mine_ref.shape[1]

    def heads(dims):
        for head in range(mine_ref.shape[0] // HEAD_DIM):
            rows = pl.ds(head * HEAD_DIM, HEAD_DIM)
            total = mine_ref[rows, :].astype(jnp.float32) + arrived_ref[rows, :].astype(jnp.float32)
            probs = probs_ref[head * tokens : (head + 1) * tokens, :]
            mixed = matmul(total.astype(jnp.bfloat16), probs, dims)
            result_ref[rows, :] = mixed.astype(jnp.bfloat16)

    pl.when(facts_ref[natural] == 1)(lambda: heads(NN))
    pl.when(facts_ref[natural] == 0)(lambda: heads(NT))

    flipped = result_ref[...].T
    second_core = facts_ref[CORE] == 1
    shard = tokens // (2 * outer)
    for chunk in range(CHUNKS):
        columns = pl.ds(chunk * step, step)
        partial = matmul(flipped, value_ref[0, version, :, columns], NN)
        for place in range(outer):
            low = partial[2 * place * shard : (2 * place + 1) * shard]
            high = partial[(2 * place + 1) * shard : (2 * place + 2) * shard]
            keep_ref[place, :, columns] = jnp.where(second_core, high, low).astype(jnp.bfloat16)
            send_ref[place, :, columns] = jnp.where(second_core, low, high).astype(jnp.bfloat16)


def mix(natural, index, facts, note, message, w_value, mine, arrived, outer):
    rows, width = w_value.shape[2:]
    tokens = mine.shape[1]
    half = jax.ShapeDtypeStruct((outer, tokens // (2 * outer), width), jnp.bfloat16)
    return pl.pallas_call(
        functools.partial(mix_kernel, outer, natural, index),
        out_shape=(jax.ShapeDtypeStruct((rows, tokens), jnp.bfloat16), half, half),
        in_specs=[in_smem()] + [in_vmem()] * 5,
        out_specs=(in_vmem(), in_vmem(), in_vmem()),
        compiler_params=pltpu.CompilerParams(vmem_limit_bytes=VMEM_BYTES),
        cost_estimate=SMALL,
        name="mix",
    )(facts, note, w_value, mine, arrived, message)


def combine_kernel(outer, last, index, facts_ref, keep_ref, arrived_ref, addend_ref, *refs):
    first_refs, sent_refs = refs[:-outer], refs[-outer:]
    for delta in range(outer):
        spot = facts_ref[ROW] ^ delta
        total = keep_ref[spot].astype(jnp.float32) + arrived_ref[spot].astype(jnp.float32)
        if delta == 0:
            total = total + addend_ref[index].astype(jnp.float32)
        total = total.astype(jnp.bfloat16)
        if last:
            total = jnp.where(facts_ref[ODD] == 1, first_refs[delta][...], total)
        sent_refs[delta][...] = total


def combine(index, facts, keep, arrived, addend, first_sent=()):
    outer, shard, width = keep.shape
    piece = jax.ShapeDtypeStruct((shard, width), jnp.bfloat16)
    return pl.pallas_call(
        functools.partial(combine_kernel, outer, len(first_sent) > 0, index),
        out_shape=(piece,) * outer,
        in_specs=[in_smem()] + [in_vmem()] * (3 + len(first_sent)),
        out_specs=(in_vmem(),) * outer,
        compiler_params=pltpu.CompilerParams(vmem_limit_bytes=VMEM_BYTES),
        cost_estimate=SMALL,
        name="combine",
    )(facts, keep, arrived, addend, *first_sent)


def assemble_kernel(n_own, facts_ref, *refs):
    grad_ref = refs[-1]
    width = refs[0].shape[1]

    def total(parts):
        value = parts[0][...].astype(jnp.float32)
        for part in parts[1:]:
            value = value + part[...].astype(jnp.float32)
        return value.astype(jnp.bfloat16)

    half = facts_ref[HALF]
    own = pl.ds(pl.multiple_of(half * width, width), width)
    other = pl.ds(pl.multiple_of((1 - half) * width, width), width)
    grad_ref[0, :, other] = total(refs[n_own:-1])
    grad_ref[0, :, own] = total(refs[:n_own])


def assemble(facts, own_parts, other_parts):
    shard, width = own_parts[0].shape
    return pl.pallas_call(
        functools.partial(assemble_kernel, len(own_parts)),
        out_shape=jax.ShapeDtypeStruct((1, shard, 2 * width), jnp.bfloat16),
        in_specs=[in_smem()] + [in_vmem()] * (len(own_parts) + len(other_parts)),
        out_specs=in_vmem(),
        compiler_params=pltpu.CompilerParams(vmem_limit_bytes=VMEM_BYTES),
        name="assemble",
    )(facts, *own_parts, *other_parts)


def weight_grad_kernel(facts_ref, a0, a1, b0, b1, first, second0, second1, value_ref, out_ref):
    odd = facts_ref[ODD] == 1
    tokens = a0.shape[1]
    left_first = jnp.concatenate([a0[...], a1[...]], axis=1)
    left_second = jnp.concatenate([b0[...], b1[...]], axis=1)
    right_second = jnp.concatenate([second0[0], second1[0]], axis=0)
    right_first = first[...].reshape(2 * tokens, first.shape[2])
    grad_first = matmul(left_first, right_second, NN)
    grad_second = matmul(left_second, right_first, NN)
    value_ref[0] = jnp.where(odd, grad_first, grad_second).astype(jnp.bfloat16)
    out_ref[0] = jnp.where(odd, grad_second, grad_first).astype(jnp.bfloat16)


def weight_grads(facts, first_results, second_results, first_full, second_full):
    rows, tokens = first_results[0].shape
    width = first_full.shape[2]
    step = rows // CHUNKS
    grad = jax.ShapeDtypeStruct((1, rows, width), jnp.bfloat16)
    left = pl.BlockSpec((step, tokens), lambda i: (i, 0))
    both = pl.BlockSpec((2, tokens, width), lambda i: (0, 0, 0))
    single = pl.BlockSpec((1, tokens, width), lambda i: (0, 0, 0))
    wide = pl.BlockSpec((1, step, width), lambda i: (0, i, 0))
    return pl.pallas_call(
        weight_grad_kernel,
        grid=(CHUNKS,),
        out_shape=(grad, grad),
        in_specs=[in_smem()] + [left] * 4 + [both, single, single],
        out_specs=(wide, wide),
        compiler_params=pltpu.CompilerParams(vmem_limit_bytes=GRAD_VMEM_BYTES),
        cost_estimate=SMALL,
        name="weight_grads",
    )(facts, *first_results, *second_results, first_full, *second_full)


def load(source_ref, table_ref, sems):
    step = table_ref.shape[2] // CHUNKS
    copies = []
    for version in range(2):
        for chunk in range(CHUNKS):
            spot = (slice(None), version, pl.ds(chunk * step, step))
            copies.append(
                pltpu.make_async_copy(
                    source_ref.at[spot], table_ref.at[spot], sems.at[version * CHUNKS + chunk]
                )
            )
    return copies


def pack_kernel(
    facts_ref, stash_ref, input_ref, value_ref, out_ref, message_ref, own_ref, table_ref, sems
):
    @pl.when(facts_ref[ODD] == 1)
    def _():
        for copy in load(out_ref, table_ref, sems):
            copy.start()

    @pl.when(facts_ref[ODD] == 0)
    def _():
        for copy in load(value_ref, table_ref, sems):
            copy.start()

    tokens = stash_ref.shape[2]
    shard, width = own_ref.shape
    heads = stash_ref.shape[1] // HEAD_DIM
    causal = lax.broadcasted_iota(jnp.int32, (tokens, tokens), 1) <= lax.broadcasted_iota(
        jnp.int32, (tokens, tokens), 0
    )
    for head in range(heads):
        rows = pl.ds(head * HEAD_DIM, HEAD_DIM)
        scores = matmul(stash_ref[0, rows, :], stash_ref[1, rows, :], TN)
        scores = jnp.where(causal, scores * (1.0 / math.sqrt(HEAD_DIM)), -jnp.inf)
        expo = jnp.exp(scores - jnp.max(scores, axis=1, keepdims=True))
        probs = (expo / jnp.sum(expo, axis=1, keepdims=True)).astype(jnp.bfloat16)
        message_ref[head * tokens : (head + 1) * tokens, :] = probs
    half = facts_ref[HALF]
    own_ref[...] = input_ref[1, :, pl.ds(pl.multiple_of(half * width, width), width)]
    other = input_ref[1, :, pl.ds(pl.multiple_of((1 - half) * width, width), width)]
    for block in range(width // LANES):
        start = heads * tokens + block * shard
        message_ref[start : start + shard, :] = other[:, block * LANES : (block + 1) * LANES]
    for copy in load(value_ref, table_ref, sems):
        copy.wait()


def pack(facts, stash, inputs, w_value, w_out):
    rows, tokens = stash.shape[1:]
    shard = inputs.shape[1]
    width = inputs.shape[2] // 2
    length = rows // HEAD_DIM * tokens + width // LANES * shard
    return pl.pallas_call(
        pack_kernel,
        out_shape=(
            jax.ShapeDtypeStruct((length, LANES), jnp.bfloat16),
            jax.ShapeDtypeStruct((shard, width), jnp.bfloat16),
            jax.ShapeDtypeStruct(w_value.shape, jnp.bfloat16),
        ),
        in_specs=[in_smem(), in_vmem(), in_vmem(), in_hbm(), in_hbm()],
        out_specs=(in_vmem(), in_vmem(), in_vmem()),
        scratch_shapes=[pltpu.SemaphoreType.DMA((2 * CHUNKS,))],
        compiler_params=pltpu.CompilerParams(vmem_limit_bytes=FIRST_VMEM_BYTES),
        cost_estimate=SMALL,
        name="pack",
    )(facts, stash, inputs, w_value, w_out)


def load_kernel(source_ref, table_ref, sems):
    copies = load(source_ref, table_ref, sems)
    for copy in copies:
        copy.start()
    for copy in copies:
        copy.wait()


def load_table(table, grant):
    return pl.pallas_call(
        load_kernel,
        out_shape=jax.ShapeDtypeStruct(table.shape, jnp.bfloat16),
        in_specs=[in_hbm()],
        out_specs=in_vmem(),
        scratch_shapes=[pltpu.SemaphoreType.DMA((2 * CHUNKS,))],
        compiler_params=pltpu.CompilerParams(vmem_limit_bytes=grant),
        cost_estimate=SMALL,
        name="load_table",
    )(table)


def arrive_kernel(index, facts_ref, source_ref, *refs):
    parts, piece_ref = refs[:-1], refs[-1]
    shard, width = piece_ref.shape[1:]

    @pl.when(facts_ref[ODD] == 1)
    def _():
        if index == 0:
            piece_ref[0] = source_ref[...]
        else:
            first_row = source_ref.shape[0] - width // LANES * shard
            for block in range(width // LANES):
                start = first_row + block * shard
                columns = pl.ds(block * LANES, LANES)
                piece_ref[0, :, columns] = source_ref[start : start + shard, :]

    @pl.when(facts_ref[ODD] == 0)
    def _():
        total = parts[0][...].astype(jnp.float32)
        for part in parts[1:]:
            total = total + part[...].astype(jnp.float32)
        piece_ref[0] = total.astype(jnp.bfloat16)


def arrive(index, facts, source, parts):
    return pl.pallas_call(
        functools.partial(arrive_kernel, index),
        out_shape=jax.ShapeDtypeStruct((1,) + parts[0].shape, jnp.bfloat16),
        in_specs=[in_smem()] + [in_vmem()] * (1 + len(parts)),
        out_specs=in_vmem(),
        compiler_params=pltpu.CompilerParams(vmem_limit_bytes=VMEM_BYTES),
        cost_estimate=SMALL,
        name="arrive",
    )(facts, source, *parts)


def on_device(section_input, query, key_stash, incoming, version, w_value, w_out):
    half = lax.axis_index("half")
    odd_flag = lax.axis_index("pair") % 2
    odd = odd_flag == 1
    place = lax.axis_index("tensor")
    core, row = place % 2, place // 2
    n_pairs = lax.axis_size("pair")
    n_tensor = lax.axis_size("tensor")
    outer = n_tensor // 2
    width = w_value.shape[3]
    shard = section_input.shape[1]

    def swap_half(array):
        return lax.ppermute(array, "half", [(0, 1), (1, 0)])

    def swap_core(array):
        return lax.ppermute(array, "tensor", [(i, i ^ 1) for i in range(n_tensor)])

    def to_row(array, delta):
        return lax.ppermute(array, "tensor", [(i, i ^ (2 * delta)) for i in range(n_tensor)])

    def to_other_half(array, delta):
        pairs = [
            (h * n_tensor + i, (1 - h) * n_tensor + (i ^ (2 * delta)))
            for h in range(2)
            for i in range(n_tensor)
        ]
        return lax.ppermute(array, ("half", "tensor"), pairs)

    def swap_section(array, delta):
        pairs = [
            (p * n_tensor + i, (p ^ 1) * n_tensor + (i ^ (2 * delta)))
            for p in range(n_pairs)
            for i in range(n_tensor)
        ]
        return lax.ppermute(array, ("pair", "tensor"), pairs)

    def own_columns(array):
        return lax.dynamic_slice_in_dim(array, half * width, width, 1)

    def other_columns(array):
        return lax.dynamic_slice_in_dim(array, (1 - half) * width, width, 1)

    def gathered(pair):
        return lax.all_gather(pair, "tensor", axis=1, tiled=True)

    facts = jnp.stack([odd_flag, 1 - odd_flag, version[0], core, row, half])
    inputs = jnp.stack([jnp.where(odd, incoming[0], section_input[0]), section_input[0]])
    note = jnp.full((NOTE_ROWS, width), version[0], jnp.int32).astype(jnp.bfloat16)
    sent_piece = jnp.concatenate([other_columns(inputs[0]), note])
    other_piece = swap_half(sent_piece)
    other_note = other_piece[shard:]
    first_pair = jnp.stack([own_columns(inputs[0]), other_piece[:shard]])
    stash = jnp.concatenate([query, key_stash])
    own_message, input_own, first_table = pack(facts, stash, inputs, w_value, w_out)
    other_message = swap_half(own_message)
    first_full = gathered(first_pair)
    own_full, other_message = lax.optimization_barrier((first_full, other_message))
    messages = [own_message, other_message]

    partial = [None, None]
    for m in (1, 0):
        tokens = first_full if m else own_full
        partial[m] = project(m, m, facts, other_note, (first_table,), tokens)
    arrived = [swap_half(partial[1]), swap_half(partial[0])]
    later_value, _ = lax.optimization_barrier((w_value, partial))
    value_table = load_table(later_value, VALUE_VMEM_BYTES)
    first_result, first_sent = [None, None], [None, None]
    second_piece, second_full = [None, None], [None, None]
    for m in range(2):
        first_result[m], keep, send = mix(
            ODD, m, facts, other_note, messages[m], value_table, partial[m], arrived[m], outer
        )
        first_sent[m] = combine(m, facts, keep, swap_core(send), first_pair)
    later_out, _ = lax.optimization_barrier((w_out, first_sent))
    out_table = load_table(later_out, OUT_VMEM_BYTES)
    sources = [input_own, other_message]
    sources, _ = lax.optimization_barrier((sources, out_table))
    for m in range(2):
        received = [swap_section(part, d) for d, part in enumerate(first_sent[m])]
        second_piece[m] = arrive(m, facts, sources[m], received)
    for m in range(2):
        second_full[m] = gathered(second_piece[m])
        partial[m] = project(
            m, 0, facts, other_note, (value_table, out_table), second_full[m]
        )
    arrived = [swap_half(partial[1]), swap_half(partial[0])]
    second_result, last_sent = [None, None], [None, None]
    for m in (1, 0):
        second_result[m], keep, send = mix(
            EVEN, m, facts, other_note, messages[m], value_table, partial[m], arrived[m], outer
        )
        last_sent[m] = combine(0, facts, keep, swap_core(send), second_piece[m], first_sent[m])
    other_parts = [to_other_half(part, d) for d, part in enumerate(last_sent[1])]
    own_parts = [last_sent[0][0]] + [to_row(part, d + 1) for d, part in enumerate(last_sent[0][1:])]
    second_result, _ = lax.optimization_barrier((second_result, last_sent))
    grad_value, grad_out = weight_grads(
        facts, first_result, second_result, first_full, second_full
    )
    own_parts, other_parts, _ = lax.optimization_barrier((own_parts, other_parts, grad_value))
    input_grad = assemble(facts, own_parts, other_parts)
    return (input_grad, grad_value, grad_out)


def solution(mesh):
    sections, tensor = mesh.devices.shape
    split = Mesh(mesh.devices.reshape(sections // 2, 2, tensor), ("pair", "half", "tensor"))
    slots = ("pair", "half")
    by_tokens = P(slots, "tensor", None)
    by_rows = P(slots, None, "tensor", None)
    return jax.shard_map(
        on_device,
        mesh=split,
        in_specs=(by_tokens, by_tokens, by_tokens, by_tokens, P(slots), by_rows, by_rows),
        out_specs=(by_tokens, by_tokens, by_tokens),
        check_vma=False,
    )
```

```python
import functools
import math

import jax
import jax.numpy as jnp
from jax import lax
from jax.experimental import pallas as pl
from jax.experimental.pallas import tpu as pltpu
from jax.sharding import Mesh, PartitionSpec as P

HEAD_DIM = 96
CHUNKS = 4
VMEM_BYTES = 8 * 2**20
GRAD_VMEM_BYTES = 16 * 2**20
FIRST_VMEM_BYTES = 46 * 2**20
VALUE_VMEM_BYTES = 47 * 2**20
OUT_VMEM_BYTES = 42 * 2**20
ODD, EVEN, VERSION, CORE, ROW, HALF = range(6)
LANES = 128
NOTE_ROWS = 16
SMALL = pl.CostEstimate(flops=1, bytes_accessed=1, transcendentals=0)
NN = (((1,), (0,)), ((), ()))
NT = (((1,), (1,)), ((), ()))
TN = (((0,), (0,)), ((), ()))


def matmul(left_side, right_side, dims):
    return lax.dot_general(left_side, right_side, dims, preferred_element_type=jnp.float32)


def in_vmem():
    return pl.BlockSpec(memory_space=pltpu.VMEM)


def in_smem():
    return pl.BlockSpec(memory_space=pltpu.SMEM)


def in_hbm():
    return pl.BlockSpec(memory_space=pltpu.HBM)


def in_place():
    return pl.BlockSpec(memory_space=pl.ANY)


def picked_version(index, facts_ref, note_ref):
    if index == 0:
        return facts_ref[VERSION]
    return (jnp.max(note_ref[...].astype(jnp.float32)) > 0.5).astype(jnp.int32)


def first_project_kernel(index, facts_ref, note_ref, table_ref, tokens_ref, partial_ref):
    version = picked_version(index, facts_ref, note_ref)
    partial = matmul(table_ref[0, version], tokens_ref[index].T, NN)
    partial_ref[...] = partial.astype(jnp.bfloat16)


def first_project(index, facts, note, table, tokens):
    rows = table.shape[2]
    return pl.pallas_call(
        functools.partial(first_project_kernel, index),
        out_shape=jax.ShapeDtypeStruct((rows, tokens.shape[1]), jnp.bfloat16),
        in_specs=[in_smem()] + [in_vmem()] * 3,
        out_specs=in_vmem(),
        compiler_params=pltpu.CompilerParams(vmem_limit_bytes=VMEM_BYTES),
        cost_estimate=SMALL,
        name="first_project",
    )(facts, note, table, tokens)


def project_kernel(
    index, outer, facts_ref, note_ref, value_ref, out_ref, mine_ref, theirs_ref, partial_ref, full_ref
):
    version = picked_version(index, facts_ref, note_ref)
    first_core = facts_ref[CORE] == 0
    shard = mine_ref.shape[0] // outer
    for place in range(outer):
        mine = mine_ref[place * shard : (place + 1) * shard, :]
        theirs = theirs_ref[place * shard : (place + 1) * shard, :]
        start = 2 * place * shard
        full_ref[start : start + shard, :] = jnp.where(first_core, mine, theirs)
        full_ref[start + shard : start + 2 * shard, :] = jnp.where(first_core, theirs, mine)
    flipped = full_ref[...].T

    def rows_of(table_ref):
        partial_ref[...] = matmul(table_ref[0, version], flipped, NN).astype(jnp.bfloat16)

    pl.when(facts_ref[ODD] == 1)(lambda: rows_of(value_ref))
    pl.when(facts_ref[ODD] == 0)(lambda: rows_of(out_ref))


def project(index, outer, facts, note, tables, mine, theirs):
    rows = tables[0].shape[2]
    tokens, width = 2 * mine.shape[0], mine.shape[1]
    return pl.pallas_call(
        functools.partial(project_kernel, index, outer),
        out_shape=(
            jax.ShapeDtypeStruct((rows, tokens), jnp.bfloat16),
            jax.ShapeDtypeStruct((tokens, width), jnp.bfloat16),
        ),
        in_specs=[in_smem()] + [in_vmem()] * 5,
        out_specs=(in_vmem(), in_vmem()),
        compiler_params=pltpu.CompilerParams(vmem_limit_bytes=VMEM_BYTES),
        cost_estimate=SMALL,
        name="project",
    )(facts, note, *tables, mine, theirs)


def mix_kernel(
    outer,
    natural,
    index,
    facts_ref,
    note_ref,
    value_ref,
    mine_ref,
    arrived_ref,
    probs_ref,
    result_ref,
    keep_ref,
    send_ref,
):
    version = picked_version(index, facts_ref, note_ref)
    step = value_ref.shape[3] // CHUNKS
    tokens = mine_ref.shape[1]

    def heads(dims):
        for head in range(mine_ref.shape[0] // HEAD_DIM):
            rows = pl.ds(head * HEAD_DIM, HEAD_DIM)
            total = mine_ref[rows, :].astype(jnp.float32) + arrived_ref[rows, :].astype(jnp.float32)
            probs = probs_ref[head * tokens : (head + 1) * tokens, :]
            mixed = matmul(total.astype(jnp.bfloat16), probs, dims)
            result_ref[rows, :] = mixed.astype(jnp.bfloat16)

    pl.when(facts_ref[natural] == 1)(lambda: heads(NN))
    pl.when(facts_ref[natural] == 0)(lambda: heads(NT))

    flipped = result_ref[...].T
    second_core = facts_ref[CORE] == 1
    shard = tokens // (2 * outer)
    for chunk in range(CHUNKS):
        columns = pl.ds(chunk * step, step)
        partial = matmul(flipped, value_ref[0, version, :, columns], NN)
        for place in range(outer):
            low = partial[2 * place * shard : (2 * place + 1) * shard]
            high = partial[(2 * place + 1) * shard : (2 * place + 2) * shard]
            keep_ref[place, :, columns] = jnp.where(second_core, high, low).astype(jnp.bfloat16)
            send_ref[place, :, columns] = jnp.where(second_core, low, high).astype(jnp.bfloat16)


def mix(natural, index, facts, note, message, w_value, mine, arrived, outer):
    rows, width = w_value.shape[2:]
    tokens = mine.shape[1]
    half = jax.ShapeDtypeStruct((outer, tokens // (2 * outer), width), jnp.bfloat16)
    return pl.pallas_call(
        functools.partial(mix_kernel, outer, natural, index),
        out_shape=(jax.ShapeDtypeStruct((rows, tokens), jnp.bfloat16), half, half),
        in_specs=[in_smem()] + [in_vmem()] * 5,
        out_specs=(in_vmem(), in_vmem(), in_vmem()),
        compiler_params=pltpu.CompilerParams(vmem_limit_bytes=VMEM_BYTES),
        cost_estimate=SMALL,
        name="mix",
    )(facts, note, w_value, mine, arrived, message)


def combine_kernel(outer, last, index, facts_ref, keep_ref, arrived_ref, addend_ref, *refs):
    first_refs, sent_refs = refs[:-outer], refs[-outer:]
    for delta in range(outer):
        spot = facts_ref[ROW] ^ delta
        total = keep_ref[spot].astype(jnp.float32) + arrived_ref[spot].astype(jnp.float32)
        if delta == 0:
            addend = addend_ref[...] if index is None else addend_ref[index]
            total = total + addend.astype(jnp.float32)
        total = total.astype(jnp.bfloat16)
        if last:
            total = jnp.where(facts_ref[ODD] == 1, first_refs[delta][...], total)
        sent_refs[delta][...] = total


def combine(index, facts, keep, arrived, addend, first_sent=()):
    outer, shard, width = keep.shape
    piece = jax.ShapeDtypeStruct((shard, width), jnp.bfloat16)
    return pl.pallas_call(
        functools.partial(combine_kernel, outer, len(first_sent) > 0, index),
        out_shape=(piece,) * outer,
        in_specs=[in_smem()] + [in_vmem()] * (3 + len(first_sent)),
        out_specs=(in_vmem(),) * outer,
        compiler_params=pltpu.CompilerParams(vmem_limit_bytes=VMEM_BYTES),
        cost_estimate=SMALL,
        name="combine",
    )(facts, keep, arrived, addend, *first_sent)


def assemble_kernel(n_own, facts_ref, *refs):
    grad_ref = refs[-1]
    width = refs[0].shape[1]

    def total(parts):
        value = parts[0][...].astype(jnp.float32)
        for part in parts[1:]:
            value = value + part[...].astype(jnp.float32)
        return value.astype(jnp.bfloat16)

    half = facts_ref[HALF]
    own = pl.ds(pl.multiple_of(half * width, width), width)
    other = pl.ds(pl.multiple_of((1 - half) * width, width), width)
    grad_ref[0, :, other] = total(refs[n_own:-1])
    grad_ref[0, :, own] = total(refs[:n_own])


def assemble(facts, own_parts, other_parts):
    shard, width = own_parts[0].shape
    return pl.pallas_call(
        functools.partial(assemble_kernel, len(own_parts)),
        out_shape=jax.ShapeDtypeStruct((1, shard, 2 * width), jnp.bfloat16),
        in_specs=[in_smem()] + [in_vmem()] * (len(own_parts) + len(other_parts)),
        out_specs=in_vmem(),
        compiler_params=pltpu.CompilerParams(vmem_limit_bytes=VMEM_BYTES),
        name="assemble",
    )(facts, *own_parts, *other_parts)


def weight_grad_kernel(facts_ref, a0, a1, b0, b1, first, second0, second1, value_ref, out_ref):
    odd = facts_ref[ODD] == 1
    tokens = a0.shape[1]
    left_first = jnp.concatenate([a0[...], a1[...]], axis=1)
    left_second = jnp.concatenate([b0[...], b1[...]], axis=1)
    right_second = jnp.concatenate([second0[...], second1[...]], axis=0)
    right_first = first[...].reshape(2 * tokens, first.shape[2])
    grad_first = matmul(left_first, right_second, NN)
    grad_second = matmul(left_second, right_first, NN)
    value_ref[0] = jnp.where(odd, grad_first, grad_second).astype(jnp.bfloat16)
    out_ref[0] = jnp.where(odd, grad_second, grad_first).astype(jnp.bfloat16)


def weight_grads(facts, first_results, second_results, first_full, second_full):
    rows, tokens = first_results[0].shape
    width = first_full.shape[2]
    step = rows // CHUNKS
    grad = jax.ShapeDtypeStruct((1, rows, width), jnp.bfloat16)
    left = pl.BlockSpec((step, tokens), lambda i: (i, 0))
    both = pl.BlockSpec((2, tokens, width), lambda i: (0, 0, 0))
    single = pl.BlockSpec((tokens, width), lambda i: (0, 0))
    wide = pl.BlockSpec((1, step, width), lambda i: (0, i, 0))
    return pl.pallas_call(
        weight_grad_kernel,
        grid=(CHUNKS,),
        out_shape=(grad, grad),
        in_specs=[in_smem()] + [left] * 4 + [both, single, single],
        out_specs=(wide, wide),
        compiler_params=pltpu.CompilerParams(vmem_limit_bytes=GRAD_VMEM_BYTES),
        cost_estimate=SMALL,
        name="weight_grads",
    )(facts, *first_results, *second_results, first_full, *second_full)


def load(source_ref, table_ref, sems):
    step = table_ref.shape[2] // CHUNKS
    copies = []
    for version in range(2):
        for chunk in range(CHUNKS):
            spot = (slice(None), version, pl.ds(chunk * step, step))
            copies.append(
                pltpu.make_async_copy(
                    source_ref.at[spot], table_ref.at[spot], sems.at[version * CHUNKS + chunk]
                )
            )
    return copies


def pack_kernel(
    facts_ref, stash_ref, input_ref, value_ref, out_ref, message_ref, own_ref, table_ref, sems
):
    @pl.when(facts_ref[ODD] == 1)
    def _():
        for copy in load(out_ref, table_ref, sems):
            copy.start()

    @pl.when(facts_ref[ODD] == 0)
    def _():
        for copy in load(value_ref, table_ref, sems):
            copy.start()

    tokens = stash_ref.shape[2]
    shard, width = own_ref.shape
    heads = stash_ref.shape[1] // HEAD_DIM
    causal = lax.broadcasted_iota(jnp.int32, (tokens, tokens), 1) <= lax.broadcasted_iota(
        jnp.int32, (tokens, tokens), 0
    )
    for head in range(heads):
        rows = pl.ds(head * HEAD_DIM, HEAD_DIM)
        scores = matmul(stash_ref[0, rows, :], stash_ref[1, rows, :], TN)
        scores = jnp.where(causal, scores * (1.0 / math.sqrt(HEAD_DIM)), -jnp.inf)
        expo = jnp.exp(scores - jnp.max(scores, axis=1, keepdims=True))
        probs = (expo / jnp.sum(expo, axis=1, keepdims=True)).astype(jnp.bfloat16)
        message_ref[head * tokens : (head + 1) * tokens, :] = probs
    half = facts_ref[HALF]
    own_ref[...] = input_ref[1, :, pl.ds(pl.multiple_of(half * width, width), width)]
    other = input_ref[1, :, pl.ds(pl.multiple_of((1 - half) * width, width), width)]
    for block in range(width // LANES):
        start = heads * tokens + block * shard
        message_ref[start : start + shard, :] = other[:, block * LANES : (block + 1) * LANES]
    for copy in load(value_ref, table_ref, sems):
        copy.wait()


def pack(facts, stash, inputs, w_value, w_out):
    rows, tokens = stash.shape[1:]
    shard = inputs.shape[1]
    width = inputs.shape[2] // 2
    length = rows // HEAD_DIM * tokens + width // LANES * shard
    return pl.pallas_call(
        pack_kernel,
        out_shape=(
            jax.ShapeDtypeStruct((length, LANES), jnp.bfloat16),
            jax.ShapeDtypeStruct((shard, width), jnp.bfloat16),
            jax.ShapeDtypeStruct(w_value.shape, jnp.bfloat16),
        ),
        in_specs=[in_smem(), in_vmem(), in_vmem(), in_hbm(), in_hbm()],
        out_specs=(in_vmem(), in_vmem(), in_vmem()),
        scratch_shapes=[pltpu.SemaphoreType.DMA((2 * CHUNKS,))],
        compiler_params=pltpu.CompilerParams(vmem_limit_bytes=FIRST_VMEM_BYTES),
        cost_estimate=SMALL,
        name="pack",
    )(facts, stash, inputs, w_value, w_out)


def load_kernel(source_ref, table_ref, sems):
    copies = load(source_ref, table_ref, sems)
    for copy in copies:
        copy.start()
    for copy in copies:
        copy.wait()


def load_table(table, grant):
    return pl.pallas_call(
        load_kernel,
        out_shape=jax.ShapeDtypeStruct(table.shape, jnp.bfloat16),
        in_specs=[in_hbm()],
        out_specs=in_vmem(),
        scratch_shapes=[pltpu.SemaphoreType.DMA((2 * CHUNKS,))],
        compiler_params=pltpu.CompilerParams(vmem_limit_bytes=grant),
        cost_estimate=SMALL,
        name="load_table",
    )(table)


def arrive_kernel(index, facts_ref, source_ref, *refs):
    parts, piece_ref = refs[:-1], refs[-1]
    shard, width = piece_ref.shape

    @pl.when(facts_ref[ODD] == 1)
    def _():
        if index == 0:
            piece_ref[...] = source_ref[...]
        else:
            first_row = source_ref.shape[0] - width // LANES * shard
            for block in range(width // LANES):
                start = first_row + block * shard
                columns = pl.ds(block * LANES, LANES)
                piece_ref[:, columns] = source_ref[start : start + shard, :]

    @pl.when(facts_ref[ODD] == 0)
    def _():
        total = parts[0][...].astype(jnp.float32)
        for part in parts[1:]:
            total = total + part[...].astype(jnp.float32)
        piece_ref[...] = total.astype(jnp.bfloat16)


def arrive(index, facts, source, parts):
    return pl.pallas_call(
        functools.partial(arrive_kernel, index),
        out_shape=jax.ShapeDtypeStruct(parts[0].shape, jnp.bfloat16),
        in_specs=[in_smem()] + [in_vmem()] * (1 + len(parts)),
        out_specs=in_vmem(),
        compiler_params=pltpu.CompilerParams(vmem_limit_bytes=VMEM_BYTES),
        cost_estimate=SMALL,
        name="arrive",
    )(facts, source, *parts)


def on_device(section_input, query, key_stash, incoming, version, w_value, w_out):
    half = lax.axis_index("half")
    odd_flag = lax.axis_index("pair") % 2
    odd = odd_flag == 1
    core, row = lax.axis_index("core"), lax.axis_index("outer")
    n_pairs = lax.axis_size("pair")
    outer = lax.axis_size("outer")
    n_tensor = 2 * outer
    width = w_value.shape[3]
    shard = section_input.shape[1]

    def swap_half(array):
        return lax.ppermute(array, "half", [(0, 1), (1, 0)])

    def swap_core(array):
        return lax.ppermute(array, "core", [(0, 1), (1, 0)])

    def to_row(array, delta):
        return lax.ppermute(array, "outer", [(i, i ^ delta) for i in range(outer)])

    def to_other_half(array, delta):
        pairs = [
            (h * n_tensor + i, (1 - h) * n_tensor + (i ^ (2 * delta)))
            for h in range(2)
            for i in range(n_tensor)
        ]
        return lax.ppermute(array, ("half", "outer", "core"), pairs)

    def swap_section(array, delta):
        pairs = [
            (p * n_tensor + i, (p ^ 1) * n_tensor + (i ^ (2 * delta)))
            for p in range(n_pairs)
            for i in range(n_tensor)
        ]
        return lax.ppermute(array, ("pair", "outer", "core"), pairs)

    def own_columns(array):
        return lax.dynamic_slice_in_dim(array, half * width, width, 1)

    def other_columns(array):
        return lax.dynamic_slice_in_dim(array, (1 - half) * width, width, 1)

    def gathered(pair):
        return lax.all_gather(pair, ("outer", "core"), axis=1, tiled=True)

    facts = jnp.stack([odd_flag, 1 - odd_flag, version[0], core, row, half])
    inputs = jnp.stack([jnp.where(odd, incoming[0], section_input[0]), section_input[0]])
    note = jnp.full((NOTE_ROWS, width), version[0], jnp.int32).astype(jnp.bfloat16)
    sent_piece = jnp.concatenate([other_columns(inputs[0]), note])
    other_piece = swap_half(sent_piece)
    other_note = other_piece[shard:]
    first_pair = jnp.stack([own_columns(inputs[0]), other_piece[:shard]])
    stash = jnp.concatenate([query, key_stash])
    own_message, input_own, first_table = pack(facts, stash, inputs, w_value, w_out)
    other_message = swap_half(own_message)
    first_full = gathered(first_pair)
    own_full, other_message = lax.optimization_barrier((first_full, other_message))
    messages = [own_message, other_message]

    partial = [None, None]
    for m in (1, 0):
        tokens = first_full if m else own_full
        partial[m] = first_project(m, facts, other_note, first_table, tokens)
    arrived = [swap_half(partial[1]), swap_half(partial[0])]
    later_value, _ = lax.optimization_barrier((w_value, partial))
    value_table = load_table(later_value, VALUE_VMEM_BYTES)
    first_result, first_sent = [None, None], [None, None]
    second_piece, second_full = [None, None], [None, None]
    for m in range(2):
        first_result[m], keep, send = mix(
            ODD, m, facts, other_note, messages[m], value_table, partial[m], arrived[m], outer
        )
        first_sent[m] = combine(m, facts, keep, swap_core(send), first_pair)
    later_out, _ = lax.optimization_barrier((w_out, first_sent))
    out_table = load_table(later_out, OUT_VMEM_BYTES)
    sources = [input_own, other_message]
    sources, _ = lax.optimization_barrier((sources, out_table))
    for m in range(2):
        received = [swap_section(part, d) for d, part in enumerate(first_sent[m])]
        second_piece[m] = arrive(m, facts, sources[m], received)
    for m in range(2):
        mine = lax.all_gather(second_piece[m], "outer", axis=0, tiled=True)
        partial[m], second_full[m] = project(
            m, outer, facts, other_note, (value_table, out_table), mine, swap_core(mine)
        )
    arrived = [swap_half(partial[1]), swap_half(partial[0])]
    second_result, last_sent = [None, None], [None, None]
    for m in (1, 0):
        second_result[m], keep, send = mix(
            EVEN, m, facts, other_note, messages[m], value_table, partial[m], arrived[m], outer
        )
        last_sent[m] = combine(None, facts, keep, swap_core(send), second_piece[m], first_sent[m])
    other_parts = [to_other_half(part, d) for d, part in enumerate(last_sent[1])]
    own_parts = [last_sent[0][0]] + [to_row(part, d + 1) for d, part in enumerate(last_sent[0][1:])]
    second_result, _ = lax.optimization_barrier((second_result, last_sent))
    grad_value, grad_out = weight_grads(
        facts, first_result, second_result, first_full, second_full
    )
    own_parts, other_parts, _ = lax.optimization_barrier((own_parts, other_parts, grad_value))
    input_grad = assemble(facts, own_parts, other_parts)
    return (input_grad, grad_value, grad_out)


def solution(mesh):
    sections, tensor = mesh.devices.shape
    split = Mesh(
        mesh.devices.reshape(sections // 2, 2, tensor // 2, 2), ("pair", "half", "outer", "core")
    )
    slots, places = ("pair", "half"), ("outer", "core")
    by_tokens = P(slots, places, None)
    by_rows = P(slots, None, places, None)
    return jax.shard_map(
        on_device,
        mesh=split,
        in_specs=(by_tokens, by_tokens, by_tokens, by_tokens, P(slots), by_rows, by_rows),
        out_specs=(by_tokens, by_tokens, by_tokens),
        check_vma=False,
    )
```

```python
import functools
import math

import jax
import jax.numpy as jnp
from jax import lax
from jax.experimental import pallas as pl
from jax.experimental.pallas import tpu as pltpu
from jax.sharding import Mesh, PartitionSpec as P

HEAD_DIM = 96
CHUNKS = 4
VMEM_BYTES = 8 * 2**20
GRAD_VMEM_BYTES = 16 * 2**20
FIRST_VMEM_BYTES = 46 * 2**20
VALUE_VMEM_BYTES = 47 * 2**20
OUT_VMEM_BYTES = 42 * 2**20
ODD, EVEN, VERSION, CORE, ROW, HALF = range(6)
LANES = 128
NOTE_ROWS = 16
SMALL = pl.CostEstimate(flops=1, bytes_accessed=1, transcendentals=0)
NN = (((1,), (0,)), ((), ()))
NT = (((1,), (1,)), ((), ()))
TN = (((0,), (0,)), ((), ()))


def matmul(left_side, right_side, dims):
    return lax.dot_general(left_side, right_side, dims, preferred_element_type=jnp.float32)


def in_vmem():
    return pl.BlockSpec(memory_space=pltpu.VMEM)


def in_smem():
    return pl.BlockSpec(memory_space=pltpu.SMEM)


def in_hbm():
    return pl.BlockSpec(memory_space=pltpu.HBM)


def in_place():
    return pl.BlockSpec(memory_space=pl.ANY)


def picked_version(index, facts_ref, note_ref):
    if index == 0:
        return facts_ref[VERSION]
    return (jnp.max(note_ref[...].astype(jnp.float32)) > 0.5).astype(jnp.int32)


def first_project_kernel(index, facts_ref, note_ref, table_ref, tokens_ref, partial_ref):
    version = picked_version(index, facts_ref, note_ref)
    partial = matmul(table_ref[0, version], tokens_ref[index].T, NN)
    partial_ref[...] = partial.astype(jnp.bfloat16)


def first_project(index, facts, note, table, tokens):
    rows = table.shape[2]
    return pl.pallas_call(
        functools.partial(first_project_kernel, index),
        out_shape=jax.ShapeDtypeStruct((rows, tokens.shape[1]), jnp.bfloat16),
        in_specs=[in_smem()] + [in_vmem()] * 3,
        out_specs=in_vmem(),
        compiler_params=pltpu.CompilerParams(vmem_limit_bytes=VMEM_BYTES),
        cost_estimate=SMALL,
        name="first_project",
    )(facts, note, table, tokens)


def project_kernel(index, outer, facts_ref, note_ref, value_ref, out_ref, *refs):
    piece_refs, (partial_ref, full_ref) = refs[:-2], refs[-2:]
    version = picked_version(index, facts_ref, note_ref)
    first_core = facts_ref[CORE] == 0
    shard = piece_refs[0].shape[0]
    mine = [ref[...] for ref in piece_refs[:outer]]
    theirs = [ref[...] for ref in piece_refs[outer:]]
    for place in range(outer):
        offset = facts_ref[ROW] ^ place
        own, other = mine[0], theirs[0]
        for delta in range(1, outer):
            own = jnp.where(offset == delta, mine[delta], own)
            other = jnp.where(offset == delta, theirs[delta], other)
        start = 2 * place * shard
        full_ref[start : start + shard, :] = jnp.where(first_core, own, other)
        full_ref[start + shard : start + 2 * shard, :] = jnp.where(first_core, other, own)
    flipped = full_ref[...].T

    def rows_of(table_ref):
        partial_ref[...] = matmul(table_ref[0, version], flipped, NN).astype(jnp.bfloat16)

    pl.when(facts_ref[ODD] == 1)(lambda: rows_of(value_ref))
    pl.when(facts_ref[ODD] == 0)(lambda: rows_of(out_ref))


def project(index, facts, note, tables, mine, theirs):
    outer = len(mine)
    rows, width = tables[0].shape[2:]
    tokens = 2 * outer * mine[0].shape[0]
    return pl.pallas_call(
        functools.partial(project_kernel, index, outer),
        out_shape=(
            jax.ShapeDtypeStruct((rows, tokens), jnp.bfloat16),
            jax.ShapeDtypeStruct((tokens, width), jnp.bfloat16),
        ),
        in_specs=[in_smem()] + [in_vmem()] * (3 + 2 * outer),
        out_specs=(in_vmem(), in_vmem()),
        compiler_params=pltpu.CompilerParams(vmem_limit_bytes=VMEM_BYTES),
        cost_estimate=SMALL,
        name="project",
    )(facts, note, *tables, *mine, *theirs)


def mix_kernel(
    outer,
    natural,
    index,
    facts_ref,
    note_ref,
    value_ref,
    mine_ref,
    arrived_ref,
    probs_ref,
    result_ref,
    keep_ref,
    send_ref,
):
    version = picked_version(index, facts_ref, note_ref)
    step = value_ref.shape[3] // CHUNKS
    tokens = mine_ref.shape[1]

    def heads(dims):
        for head in range(mine_ref.shape[0] // HEAD_DIM):
            rows = pl.ds(head * HEAD_DIM, HEAD_DIM)
            total = mine_ref[rows, :].astype(jnp.float32) + arrived_ref[rows, :].astype(jnp.float32)
            probs = probs_ref[head * tokens : (head + 1) * tokens, :]
            mixed = matmul(total.astype(jnp.bfloat16), probs, dims)
            result_ref[rows, :] = mixed.astype(jnp.bfloat16)

    pl.when(facts_ref[natural] == 1)(lambda: heads(NN))
    pl.when(facts_ref[natural] == 0)(lambda: heads(NT))

    flipped = result_ref[...].T
    second_core = facts_ref[CORE] == 1
    shard = tokens // (2 * outer)
    for chunk in range(CHUNKS):
        columns = pl.ds(chunk * step, step)
        partial = matmul(flipped, value_ref[0, version, :, columns], NN)
        for place in range(outer):
            low = partial[2 * place * shard : (2 * place + 1) * shard]
            high = partial[(2 * place + 1) * shard : (2 * place + 2) * shard]
            keep_ref[place, :, columns] = jnp.where(second_core, high, low).astype(jnp.bfloat16)
            send_ref[place, :, columns] = jnp.where(second_core, low, high).astype(jnp.bfloat16)


def mix(natural, index, facts, note, message, w_value, mine, arrived, outer):
    rows, width = w_value.shape[2:]
    tokens = mine.shape[1]
    half = jax.ShapeDtypeStruct((outer, tokens // (2 * outer), width), jnp.bfloat16)
    return pl.pallas_call(
        functools.partial(mix_kernel, outer, natural, index),
        out_shape=(jax.ShapeDtypeStruct((rows, tokens), jnp.bfloat16), half, half),
        in_specs=[in_smem()] + [in_vmem()] * 5,
        out_specs=(in_vmem(), in_vmem(), in_vmem()),
        compiler_params=pltpu.CompilerParams(vmem_limit_bytes=VMEM_BYTES),
        cost_estimate=SMALL,
        name="mix",
    )(facts, note, w_value, mine, arrived, message)


def combine_kernel(outer, last, index, facts_ref, keep_ref, arrived_ref, addend_ref, *refs):
    first_refs, sent_refs = refs[:-outer], refs[-outer:]
    for delta in range(outer):
        spot = facts_ref[ROW] ^ delta
        total = keep_ref[spot].astype(jnp.float32) + arrived_ref[spot].astype(jnp.float32)
        if delta == 0:
            addend = addend_ref[...] if index is None else addend_ref[index]
            total = total + addend.astype(jnp.float32)
        total = total.astype(jnp.bfloat16)
        if last:
            total = jnp.where(facts_ref[ODD] == 1, first_refs[delta][...], total)
        sent_refs[delta][...] = total


def combine(index, facts, keep, arrived, addend, first_sent=()):
    outer, shard, width = keep.shape
    piece = jax.ShapeDtypeStruct((shard, width), jnp.bfloat16)
    return pl.pallas_call(
        functools.partial(combine_kernel, outer, len(first_sent) > 0, index),
        out_shape=(piece,) * outer,
        in_specs=[in_smem()] + [in_vmem()] * (3 + len(first_sent)),
        out_specs=(in_vmem(),) * outer,
        compiler_params=pltpu.CompilerParams(vmem_limit_bytes=VMEM_BYTES),
        cost_estimate=SMALL,
        name="combine",
    )(facts, keep, arrived, addend, *first_sent)


def assemble_kernel(n_own, facts_ref, *refs):
    grad_ref = refs[-1]
    width = refs[0].shape[1]

    def total(parts):
        value = parts[0][...].astype(jnp.float32)
        for part in parts[1:]:
            value = value + part[...].astype(jnp.float32)
        return value.astype(jnp.bfloat16)

    half = facts_ref[HALF]
    own = pl.ds(pl.multiple_of(half * width, width), width)
    other = pl.ds(pl.multiple_of((1 - half) * width, width), width)
    grad_ref[0, :, other] = total(refs[n_own:-1])
    grad_ref[0, :, own] = total(refs[:n_own])


def assemble(facts, own_parts, other_parts):
    shard, width = own_parts[0].shape
    return pl.pallas_call(
        functools.partial(assemble_kernel, len(own_parts)),
        out_shape=jax.ShapeDtypeStruct((1, shard, 2 * width), jnp.bfloat16),
        in_specs=[in_smem()] + [in_vmem()] * (len(own_parts) + len(other_parts)),
        out_specs=in_vmem(),
        compiler_params=pltpu.CompilerParams(vmem_limit_bytes=VMEM_BYTES),
        name="assemble",
    )(facts, *own_parts, *other_parts)


def weight_grad_kernel(facts_ref, a0, a1, b0, b1, first, second0, second1, value_ref, out_ref):
    odd = facts_ref[ODD] == 1
    tokens = a0.shape[1]
    left_first = jnp.concatenate([a0[...], a1[...]], axis=1)
    left_second = jnp.concatenate([b0[...], b1[...]], axis=1)
    right_second = jnp.concatenate([second0[...], second1[...]], axis=0)
    right_first = first[...].reshape(2 * tokens, first.shape[2])
    grad_first = matmul(left_first, right_second, NN)
    grad_second = matmul(left_second, right_first, NN)
    value_ref[0] = jnp.where(odd, grad_first, grad_second).astype(jnp.bfloat16)
    out_ref[0] = jnp.where(odd, grad_second, grad_first).astype(jnp.bfloat16)


def weight_grads(facts, first_results, second_results, first_full, second_full):
    rows, tokens = first_results[0].shape
    width = first_full.shape[2]
    step = rows // CHUNKS
    grad = jax.ShapeDtypeStruct((1, rows, width), jnp.bfloat16)
    left = pl.BlockSpec((step, tokens), lambda i: (i, 0))
    both = pl.BlockSpec((2, tokens, width), lambda i: (0, 0, 0))
    single = pl.BlockSpec((tokens, width), lambda i: (0, 0))
    wide = pl.BlockSpec((1, step, width), lambda i: (0, i, 0))
    return pl.pallas_call(
        weight_grad_kernel,
        grid=(CHUNKS,),
        out_shape=(grad, grad),
        in_specs=[in_smem()] + [left] * 4 + [both, single, single],
        out_specs=(wide, wide),
        compiler_params=pltpu.CompilerParams(vmem_limit_bytes=GRAD_VMEM_BYTES),
        cost_estimate=SMALL,
        name="weight_grads",
    )(facts, *first_results, *second_results, first_full, *second_full)


def load(source_ref, table_ref, sems):
    step = table_ref.shape[2] // CHUNKS
    copies = []
    for version in range(2):
        for chunk in range(CHUNKS):
            spot = (slice(None), version, pl.ds(chunk * step, step))
            copies.append(
                pltpu.make_async_copy(
                    source_ref.at[spot], table_ref.at[spot], sems.at[version * CHUNKS + chunk]
                )
            )
    return copies


def pack_kernel(
    facts_ref, stash_ref, input_ref, value_ref, out_ref, message_ref, own_ref, table_ref, sems
):
    @pl.when(facts_ref[ODD] == 1)
    def _():
        for copy in load(out_ref, table_ref, sems):
            copy.start()

    @pl.when(facts_ref[ODD] == 0)
    def _():
        for copy in load(value_ref, table_ref, sems):
            copy.start()

    tokens = stash_ref.shape[2]
    shard, width = own_ref.shape
    heads = stash_ref.shape[1] // HEAD_DIM
    causal = lax.broadcasted_iota(jnp.int32, (tokens, tokens), 1) <= lax.broadcasted_iota(
        jnp.int32, (tokens, tokens), 0
    )
    for head in range(heads):
        rows = pl.ds(head * HEAD_DIM, HEAD_DIM)
        scores = matmul(stash_ref[0, rows, :], stash_ref[1, rows, :], TN)
        scores = jnp.where(causal, scores * (1.0 / math.sqrt(HEAD_DIM)), -jnp.inf)
        expo = jnp.exp(scores - jnp.max(scores, axis=1, keepdims=True))
        probs = (expo / jnp.sum(expo, axis=1, keepdims=True)).astype(jnp.bfloat16)
        message_ref[head * tokens : (head + 1) * tokens, :] = probs
    half = facts_ref[HALF]
    own_ref[...] = input_ref[1, :, pl.ds(pl.multiple_of(half * width, width), width)]
    other = input_ref[1, :, pl.ds(pl.multiple_of((1 - half) * width, width), width)]
    for block in range(width // LANES):
        start = heads * tokens + block * shard
        message_ref[start : start + shard, :] = other[:, block * LANES : (block + 1) * LANES]
    for copy in load(value_ref, table_ref, sems):
        copy.wait()


def pack(facts, stash, inputs, w_value, w_out):
    rows, tokens = stash.shape[1:]
    shard = inputs.shape[1]
    width = inputs.shape[2] // 2
    length = rows // HEAD_DIM * tokens + width // LANES * shard
    return pl.pallas_call(
        pack_kernel,
        out_shape=(
            jax.ShapeDtypeStruct((length, LANES), jnp.bfloat16),
            jax.ShapeDtypeStruct((shard, width), jnp.bfloat16),
            jax.ShapeDtypeStruct(w_value.shape, jnp.bfloat16),
        ),
        in_specs=[in_smem(), in_vmem(), in_vmem(), in_hbm(), in_hbm()],
        out_specs=(in_vmem(), in_vmem(), in_vmem()),
        scratch_shapes=[pltpu.SemaphoreType.DMA((2 * CHUNKS,))],
        compiler_params=pltpu.CompilerParams(vmem_limit_bytes=FIRST_VMEM_BYTES),
        cost_estimate=SMALL,
        name="pack",
    )(facts, stash, inputs, w_value, w_out)


def load_kernel(source_ref, table_ref, sems):
    copies = load(source_ref, table_ref, sems)
    for copy in copies:
        copy.start()
    for copy in copies:
        copy.wait()


def load_table(table, grant):
    return pl.pallas_call(
        load_kernel,
        out_shape=jax.ShapeDtypeStruct(table.shape, jnp.bfloat16),
        in_specs=[in_hbm()],
        out_specs=in_vmem(),
        scratch_shapes=[pltpu.SemaphoreType.DMA((2 * CHUNKS,))],
        compiler_params=pltpu.CompilerParams(vmem_limit_bytes=grant),
        cost_estimate=SMALL,
        name="load_table",
    )(table)


def arrive_kernel(index, facts_ref, source_ref, *refs):
    parts, piece_ref = refs[:-1], refs[-1]
    shard, width = piece_ref.shape

    @pl.when(facts_ref[ODD] == 1)
    def _():
        if index == 0:
            piece_ref[...] = source_ref[...]
        else:
            first_row = source_ref.shape[0] - width // LANES * shard
            for block in range(width // LANES):
                start = first_row + block * shard
                columns = pl.ds(block * LANES, LANES)
                piece_ref[:, columns] = source_ref[start : start + shard, :]

    @pl.when(facts_ref[ODD] == 0)
    def _():
        total = parts[0][...].astype(jnp.float32)
        for part in parts[1:]:
            total = total + part[...].astype(jnp.float32)
        piece_ref[...] = total.astype(jnp.bfloat16)


def arrive(index, facts, source, parts):
    return pl.pallas_call(
        functools.partial(arrive_kernel, index),
        out_shape=jax.ShapeDtypeStruct(parts[0].shape, jnp.bfloat16),
        in_specs=[in_smem()] + [in_vmem()] * (1 + len(parts)),
        out_specs=in_vmem(),
        compiler_params=pltpu.CompilerParams(vmem_limit_bytes=VMEM_BYTES),
        cost_estimate=SMALL,
        name="arrive",
    )(facts, source, *parts)


def on_device(section_input, query, key_stash, incoming, version, w_value, w_out):
    half = lax.axis_index("half")
    odd_flag = lax.axis_index("pair") % 2
    odd = odd_flag == 1
    core, row = lax.axis_index("core"), lax.axis_index("outer")
    n_pairs = lax.axis_size("pair")
    outer = lax.axis_size("outer")
    n_tensor = 2 * outer
    width = w_value.shape[3]
    shard = section_input.shape[1]

    def swap_half(array):
        return lax.ppermute(array, "half", [(0, 1), (1, 0)])

    def swap_core(array):
        return lax.ppermute(array, "core", [(0, 1), (1, 0)])

    def to_row(array, delta):
        return lax.ppermute(array, "outer", [(i, i ^ delta) for i in range(outer)])

    def to_other_half(array, delta):
        pairs = [
            (h * n_tensor + i, (1 - h) * n_tensor + (i ^ (2 * delta)))
            for h in range(2)
            for i in range(n_tensor)
        ]
        return lax.ppermute(array, ("half", "outer", "core"), pairs)

    def swap_section(array, delta):
        pairs = [
            (p * n_tensor + i, (p ^ 1) * n_tensor + (i ^ (2 * delta)))
            for p in range(n_pairs)
            for i in range(n_tensor)
        ]
        return lax.ppermute(array, ("pair", "outer", "core"), pairs)

    def own_columns(array):
        return lax.dynamic_slice_in_dim(array, half * width, width, 1)

    def other_columns(array):
        return lax.dynamic_slice_in_dim(array, (1 - half) * width, width, 1)

    def gathered(pair):
        return lax.all_gather(pair, ("outer", "core"), axis=1, tiled=True)

    facts = jnp.stack([odd_flag, 1 - odd_flag, version[0], core, row, half])
    inputs = jnp.stack([jnp.where(odd, incoming[0], section_input[0]), section_input[0]])
    note = jnp.full((NOTE_ROWS, width), version[0], jnp.int32).astype(jnp.bfloat16)
    sent_piece = jnp.concatenate([other_columns(inputs[0]), note])
    other_piece = swap_half(sent_piece)
    other_note = other_piece[shard:]
    first_pair = jnp.stack([own_columns(inputs[0]), other_piece[:shard]])
    stash = jnp.concatenate([query, key_stash])
    own_message, input_own, first_table = pack(facts, stash, inputs, w_value, w_out)
    other_message = swap_half(own_message)
    first_full = gathered(first_pair)
    own_full, other_message = lax.optimization_barrier((first_full, other_message))
    messages = [own_message, other_message]

    partial = [None, None]
    for m in (1, 0):
        tokens = first_full if m else own_full
        partial[m] = first_project(m, facts, other_note, first_table, tokens)
    arrived = [swap_half(partial[1]), swap_half(partial[0])]
    later_value, _ = lax.optimization_barrier((w_value, partial))
    value_table = load_table(later_value, VALUE_VMEM_BYTES)
    first_result, first_sent = [None, None], [None, None]
    second_piece, second_full = [None, None], [None, None]
    for m in range(2):
        first_result[m], keep, send = mix(
            ODD, m, facts, other_note, messages[m], value_table, partial[m], arrived[m], outer
        )
        first_sent[m] = combine(m, facts, keep, swap_core(send), first_pair)
    later_out, _ = lax.optimization_barrier((w_out, first_sent))
    out_table = load_table(later_out, OUT_VMEM_BYTES)
    sources = [input_own, other_message]
    sources, _ = lax.optimization_barrier((sources, out_table))
    for m in range(2):
        received = [swap_section(part, d) for d, part in enumerate(first_sent[m])]
        second_piece[m] = arrive(m, facts, sources[m], received)
    for m in range(2):
        mine = [second_piece[m]] + [to_row(second_piece[m], d) for d in range(1, outer)]
        theirs = [swap_core(piece) for piece in mine]
        partial[m], second_full[m] = project(
            m, facts, other_note, (value_table, out_table), mine, theirs
        )
    arrived = [swap_half(partial[1]), swap_half(partial[0])]
    second_result, last_sent = [None, None], [None, None]
    for m in (1, 0):
        second_result[m], keep, send = mix(
            EVEN, m, facts, other_note, messages[m], value_table, partial[m], arrived[m], outer
        )
        if m == 0:
            keep, _ = lax.optimization_barrier((keep, last_sent[1]))
        last_sent[m] = combine(None, facts, keep, swap_core(send), second_piece[m], first_sent[m])
    other_parts = [to_other_half(part, d) for d, part in enumerate(last_sent[1])]
    own_parts = [last_sent[0][0]] + [to_row(part, d + 1) for d, part in enumerate(last_sent[0][1:])]
    second_result, _ = lax.optimization_barrier((second_result, last_sent))
    grad_value, grad_out = weight_grads(
        facts, first_result, second_result, first_full, second_full
    )
    own_parts, other_parts, _ = lax.optimization_barrier((own_parts, other_parts, grad_value))
    input_grad = assemble(facts, own_parts, other_parts)
    return (input_grad, grad_value, grad_out)


def solution(mesh):
    sections, tensor = mesh.devices.shape
    split = Mesh(
        mesh.devices.reshape(sections // 2, 2, tensor // 2, 2), ("pair", "half", "outer", "core")
    )
    slots, places = ("pair", "half"), ("outer", "core")
    by_tokens = P(slots, places, None)
    by_rows = P(slots, None, places, None)
    return jax.shard_map(
        on_device,
        mesh=split,
        in_specs=(by_tokens, by_tokens, by_tokens, by_tokens, P(slots), by_rows, by_rows),
        out_specs=(by_tokens, by_tokens, by_tokens),
        check_vma=False,
    )
```

```python
import functools
import math

import jax
import jax.numpy as jnp
from jax import lax
from jax.experimental import pallas as pl
from jax.experimental.pallas import tpu as pltpu
from jax.sharding import Mesh, PartitionSpec as P

HEAD_DIM = 96
CHUNKS = 4
VMEM_BYTES = 8 * 2**20
GRAD_VMEM_BYTES = 16 * 2**20
FIRST_VMEM_BYTES = 46 * 2**20
VALUE_VMEM_BYTES = 47 * 2**20
OUT_VMEM_BYTES = 42 * 2**20
ODD, EVEN, VERSION, CORE, ROW, HALF = range(6)
LANES = 128
NOTE_ROWS = 16
SMALL = pl.CostEstimate(flops=1, bytes_accessed=1, transcendentals=0)
NN = (((1,), (0,)), ((), ()))
NT = (((1,), (1,)), ((), ()))
TN = (((0,), (0,)), ((), ()))


def matmul(left_side, right_side, dims):
    return lax.dot_general(left_side, right_side, dims, preferred_element_type=jnp.float32)


def in_vmem():
    return pl.BlockSpec(memory_space=pltpu.VMEM)


def in_smem():
    return pl.BlockSpec(memory_space=pltpu.SMEM)


def in_hbm():
    return pl.BlockSpec(memory_space=pltpu.HBM)


def in_place():
    return pl.BlockSpec(memory_space=pl.ANY)


def picked_version(index, facts_ref, note_ref):
    if index == 0:
        return facts_ref[VERSION]
    note = note_ref[note_ref.shape[0] - NOTE_ROWS :, :]
    return (jnp.max(note.astype(jnp.float32)) > 0.5).astype(jnp.int32)


def project_kernel(index, outer, shard, n_tables, facts_ref, note_ref, *refs):
    table_refs, piece_refs = refs[:n_tables], refs[n_tables:-2]
    partial_ref, full_ref = refs[-2:]
    version = picked_version(index, facts_ref, note_ref)
    first_core = facts_ref[CORE] == 0
    mine = [ref[:shard, :] for ref in piece_refs[:outer]]
    theirs = [ref[:shard, :] for ref in piece_refs[outer:]]
    for place in range(outer):
        offset = facts_ref[ROW] ^ place
        own, other = mine[0], theirs[0]
        for delta in range(1, outer):
            own = jnp.where(offset == delta, mine[delta], own)
            other = jnp.where(offset == delta, theirs[delta], other)
        start = 2 * place * shard
        full_ref[start : start + shard, :] = jnp.where(first_core, own, other)
        full_ref[start + shard : start + 2 * shard, :] = jnp.where(first_core, other, own)
    flipped = full_ref[...].T

    def rows_of(table_ref):
        partial_ref[...] = matmul(table_ref[0, version], flipped, NN).astype(jnp.bfloat16)

    if n_tables == 1:
        rows_of(table_refs[0])
    else:
        pl.when(facts_ref[ODD] == 1)(lambda: rows_of(table_refs[0]))
        pl.when(facts_ref[ODD] == 0)(lambda: rows_of(table_refs[1]))


def project(index, shard, facts, note, tables, mine, theirs):
    outer = len(mine)
    rows, width = tables[0].shape[2:]
    tokens = 2 * outer * shard
    return pl.pallas_call(
        functools.partial(project_kernel, index, outer, shard, len(tables)),
        out_shape=(
            jax.ShapeDtypeStruct((rows, tokens), jnp.bfloat16),
            jax.ShapeDtypeStruct((tokens, width), jnp.bfloat16),
        ),
        in_specs=[in_smem()] + [in_vmem()] * (1 + len(tables) + 2 * outer),
        out_specs=(in_vmem(), in_vmem()),
        compiler_params=pltpu.CompilerParams(vmem_limit_bytes=VMEM_BYTES),
        cost_estimate=SMALL,
        name="project",
    )(facts, note, *tables, *mine, *theirs)


def mix_kernel(
    outer,
    natural,
    index,
    facts_ref,
    note_ref,
    value_ref,
    mine_ref,
    arrived_ref,
    probs_ref,
    result_ref,
    keep_ref,
    send_ref,
):
    version = picked_version(index, facts_ref, note_ref)
    step = value_ref.shape[3] // CHUNKS
    tokens = mine_ref.shape[1]

    def heads(dims):
        for head in range(mine_ref.shape[0] // HEAD_DIM):
            rows = pl.ds(head * HEAD_DIM, HEAD_DIM)
            total = mine_ref[rows, :].astype(jnp.float32) + arrived_ref[rows, :].astype(jnp.float32)
            probs = probs_ref[head * tokens : (head + 1) * tokens, :]
            mixed = matmul(total.astype(jnp.bfloat16), probs, dims)
            result_ref[rows, :] = mixed.astype(jnp.bfloat16)

    pl.when(facts_ref[natural] == 1)(lambda: heads(NN))
    pl.when(facts_ref[natural] == 0)(lambda: heads(NT))

    flipped = result_ref[...].T
    second_core = facts_ref[CORE] == 1
    shard = tokens // (2 * outer)
    for chunk in range(CHUNKS):
        columns = pl.ds(chunk * step, step)
        partial = matmul(flipped, value_ref[0, version, :, columns], NN)
        for place in range(outer):
            low = partial[2 * place * shard : (2 * place + 1) * shard]
            high = partial[(2 * place + 1) * shard : (2 * place + 2) * shard]
            keep_ref[place, :, columns] = jnp.where(second_core, high, low).astype(jnp.bfloat16)
            send_ref[place, :, columns] = jnp.where(second_core, low, high).astype(jnp.bfloat16)


def mix(natural, index, facts, note, message, w_value, mine, arrived, outer):
    rows, width = w_value.shape[2:]
    tokens = mine.shape[1]
    half = jax.ShapeDtypeStruct((outer, tokens // (2 * outer), width), jnp.bfloat16)
    return pl.pallas_call(
        functools.partial(mix_kernel, outer, natural, index),
        out_shape=(jax.ShapeDtypeStruct((rows, tokens), jnp.bfloat16), half, half),
        in_specs=[in_smem()] + [in_vmem()] * 5,
        out_specs=(in_vmem(), in_vmem(), in_vmem()),
        compiler_params=pltpu.CompilerParams(vmem_limit_bytes=VMEM_BYTES),
        cost_estimate=SMALL,
        name="mix",
    )(facts, note, w_value, mine, arrived, message)


def combine_kernel(outer, last, facts_ref, keep_ref, arrived_ref, addend_ref, *refs):
    first_refs, sent_refs = refs[:-outer], refs[-outer:]
    for delta in range(outer):
        spot = facts_ref[ROW] ^ delta
        total = keep_ref[spot].astype(jnp.float32) + arrived_ref[spot].astype(jnp.float32)
        if delta == 0:
            total = total + addend_ref[: total.shape[0], :].astype(jnp.float32)
        total = total.astype(jnp.bfloat16)
        if last:
            total = jnp.where(facts_ref[ODD] == 1, first_refs[delta][...], total)
        sent_refs[delta][...] = total


def combine(facts, keep, arrived, addend, first_sent=()):
    outer, shard, width = keep.shape
    piece = jax.ShapeDtypeStruct((shard, width), jnp.bfloat16)
    return pl.pallas_call(
        functools.partial(combine_kernel, outer, len(first_sent) > 0),
        out_shape=(piece,) * outer,
        in_specs=[in_smem()] + [in_vmem()] * (3 + len(first_sent)),
        out_specs=(in_vmem(),) * outer,
        compiler_params=pltpu.CompilerParams(vmem_limit_bytes=VMEM_BYTES),
        cost_estimate=SMALL,
        name="combine",
    )(facts, keep, arrived, addend, *first_sent)


def assemble_kernel(n_own, facts_ref, *refs):
    grad_ref = refs[-1]
    width = refs[0].shape[1]

    def total(parts):
        value = parts[0][...].astype(jnp.float32)
        for part in parts[1:]:
            value = value + part[...].astype(jnp.float32)
        return value.astype(jnp.bfloat16)

    half = facts_ref[HALF]
    own = pl.ds(pl.multiple_of(half * width, width), width)
    other = pl.ds(pl.multiple_of((1 - half) * width, width), width)
    grad_ref[0, :, other] = total(refs[n_own:-1])
    grad_ref[0, :, own] = total(refs[:n_own])


def assemble(facts, own_parts, other_parts):
    shard, width = own_parts[0].shape
    return pl.pallas_call(
        functools.partial(assemble_kernel, len(own_parts)),
        out_shape=jax.ShapeDtypeStruct((1, shard, 2 * width), jnp.bfloat16),
        in_specs=[in_smem()] + [in_vmem()] * (len(own_parts) + len(other_parts)),
        out_specs=in_vmem(),
        compiler_params=pltpu.CompilerParams(vmem_limit_bytes=VMEM_BYTES),
        name="assemble",
    )(facts, *own_parts, *other_parts)


def weight_grad_kernel(
    facts_ref, a0, a1, b0, b1, first0, first1, second0, second1, value_ref, out_ref
):
    odd = facts_ref[ODD] == 1
    left_first = jnp.concatenate([a0[...], a1[...]], axis=1)
    left_second = jnp.concatenate([b0[...], b1[...]], axis=1)
    right_second = jnp.concatenate([second0[...], second1[...]], axis=0)
    right_first = jnp.concatenate([first0[...], first1[...]], axis=0)
    grad_first = matmul(left_first, right_second, NN)
    grad_second = matmul(left_second, right_first, NN)
    value_ref[0] = jnp.where(odd, grad_first, grad_second).astype(jnp.bfloat16)
    out_ref[0] = jnp.where(odd, grad_second, grad_first).astype(jnp.bfloat16)


def weight_grads(facts, first_results, second_results, first_full, second_full):
    rows, tokens = first_results[0].shape
    width = first_full[0].shape[1]
    step = rows // CHUNKS
    grad = jax.ShapeDtypeStruct((1, rows, width), jnp.bfloat16)
    left = pl.BlockSpec((step, tokens), lambda i: (i, 0))
    single = pl.BlockSpec((tokens, width), lambda i: (0, 0))
    wide = pl.BlockSpec((1, step, width), lambda i: (0, i, 0))
    return pl.pallas_call(
        weight_grad_kernel,
        grid=(CHUNKS,),
        out_shape=(grad, grad),
        in_specs=[in_smem()] + [left] * 4 + [single] * 4,
        out_specs=(wide, wide),
        compiler_params=pltpu.CompilerParams(vmem_limit_bytes=GRAD_VMEM_BYTES),
        cost_estimate=SMALL,
        name="weight_grads",
    )(facts, *first_results, *second_results, *first_full, *second_full)


def load(source_ref, table_ref, sems):
    step = table_ref.shape[2] // CHUNKS
    copies = []
    for version in range(2):
        for chunk in range(CHUNKS):
            spot = (slice(None), version, pl.ds(chunk * step, step))
            copies.append(
                pltpu.make_async_copy(
                    source_ref.at[spot], table_ref.at[spot], sems.at[version * CHUNKS + chunk]
                )
            )
    return copies


def probs_kernel(stash_ref, probs_ref):
    tokens = stash_ref.shape[2]
    causal = lax.broadcasted_iota(jnp.int32, (tokens, tokens), 1) <= lax.broadcasted_iota(
        jnp.int32, (tokens, tokens), 0
    )
    for head in range(stash_ref.shape[1] // HEAD_DIM):
        rows = pl.ds(head * HEAD_DIM, HEAD_DIM)
        scores = matmul(stash_ref[0, rows, :], stash_ref[1, rows, :], TN)
        scores = jnp.where(causal, scores * (1.0 / math.sqrt(HEAD_DIM)), -jnp.inf)
        expo = jnp.exp(scores - jnp.max(scores, axis=1, keepdims=True))
        probs = (expo / jnp.sum(expo, axis=1, keepdims=True)).astype(jnp.bfloat16)
        probs_ref[head * tokens : (head + 1) * tokens, :] = probs


def attention_probs(stash):
    rows, tokens = stash.shape[1:]
    return pl.pallas_call(
        probs_kernel,
        out_shape=jax.ShapeDtypeStruct((rows // HEAD_DIM * tokens, tokens), jnp.bfloat16),
        in_specs=[in_vmem()],
        out_specs=in_vmem(),
        compiler_params=pltpu.CompilerParams(vmem_limit_bytes=VMEM_BYTES),
        cost_estimate=SMALL,
        name="probs",
    )(stash)


def load_kernel(source_ref, table_ref, sems):
    copies = load(source_ref, table_ref, sems)
    for copy in copies:
        copy.start()
    for copy in copies:
        copy.wait()


def load_first_kernel(facts_ref, value_ref, out_ref, table_ref, sems):
    def start(source_ref):
        for copy in load(source_ref, table_ref, sems):
            copy.start()

    pl.when(facts_ref[ODD] == 1)(lambda: start(out_ref))
    pl.when(facts_ref[ODD] == 0)(lambda: start(value_ref))
    for copy in load(value_ref, table_ref, sems):
        copy.wait()


def load_first(facts, w_value, w_out):
    return pl.pallas_call(
        load_first_kernel,
        out_shape=jax.ShapeDtypeStruct(w_value.shape, jnp.bfloat16),
        in_specs=[in_smem(), in_hbm(), in_hbm()],
        out_specs=in_vmem(),
        scratch_shapes=[pltpu.SemaphoreType.DMA((2 * CHUNKS,))],
        compiler_params=pltpu.CompilerParams(vmem_limit_bytes=FIRST_VMEM_BYTES),
        cost_estimate=SMALL,
        name="load_first",
    )(facts, w_value, w_out)


def load_table(table, grant):
    return pl.pallas_call(
        load_kernel,
        out_shape=jax.ShapeDtypeStruct(table.shape, jnp.bfloat16),
        in_specs=[in_hbm()],
        out_specs=in_vmem(),
        scratch_shapes=[pltpu.SemaphoreType.DMA((2 * CHUNKS,))],
        compiler_params=pltpu.CompilerParams(vmem_limit_bytes=grant),
        cost_estimate=SMALL,
        name="load_table",
    )(table)


def arrive_kernel(facts_ref, input_ref, *refs):
    parts, piece_ref = refs[:-1], refs[-1]

    @pl.when(facts_ref[ODD] == 1)
    def _():
        piece_ref[...] = input_ref[...]

    @pl.when(facts_ref[ODD] == 0)
    def _():
        total = parts[0][...].astype(jnp.float32)
        for part in parts[1:]:
            total = total + part[...].astype(jnp.float32)
        piece_ref[...] = total.astype(jnp.bfloat16)


def arrive(facts, input_piece, parts):
    return pl.pallas_call(
        arrive_kernel,
        out_shape=jax.ShapeDtypeStruct(parts[0].shape, jnp.bfloat16),
        in_specs=[in_smem()] + [in_vmem()] * (1 + len(parts)),
        out_specs=in_vmem(),
        compiler_params=pltpu.CompilerParams(vmem_limit_bytes=VMEM_BYTES),
        cost_estimate=SMALL,
        name="arrive",
    )(facts, input_piece, *parts)


def on_device(section_input, query, key_stash, incoming, version, w_value, w_out):
    half = lax.axis_index("half")
    odd_flag = lax.axis_index("pair") % 2
    odd = odd_flag == 1
    core, row = lax.axis_index("core"), lax.axis_index("outer")
    n_pairs = lax.axis_size("pair")
    outer = lax.axis_size("outer")
    n_tensor = 2 * outer
    width = w_value.shape[3]
    shard = section_input.shape[1]

    def swap_half(array):
        return lax.ppermute(array, "half", [(0, 1), (1, 0)])

    def swap_core(array):
        return lax.ppermute(array, "core", [(0, 1), (1, 0)])

    def to_row(array, delta):
        return lax.ppermute(array, "outer", [(i, i ^ delta) for i in range(outer)])

    def to_other_half(array, delta):
        pairs = [
            (h * n_tensor + i, (1 - h) * n_tensor + (i ^ (2 * delta)))
            for h in range(2)
            for i in range(n_tensor)
        ]
        return lax.ppermute(array, ("half", "outer", "core"), pairs)

    def swap_section(array, delta):
        pairs = [
            (p * n_tensor + i, (p ^ 1) * n_tensor + (i ^ (2 * delta)))
            for p in range(n_pairs)
            for i in range(n_tensor)
        ]
        return lax.ppermute(array, ("pair", "outer", "core"), pairs)

    def own_columns(array):
        return lax.dynamic_slice_in_dim(array, half * width, width, 1)

    def other_columns(array):
        return lax.dynamic_slice_in_dim(array, (1 - half) * width, width, 1)

    def spread_rows(piece):
        return [piece] + [to_row(piece, delta) for delta in range(1, outer)]

    facts = jnp.stack([odd_flag, 1 - odd_flag, version[0], core, row, half])
    first = jnp.where(odd, incoming[0], section_input[0])
    own_piece, sent_piece = own_columns(first), other_columns(first)
    note = jnp.full((NOTE_ROWS, width), version[0], jnp.int32).astype(jnp.bfloat16)
    noted_piece = jnp.concatenate([sent_piece, note])
    other_note = swap_half(noted_piece)
    first_piece = [own_piece, other_note[:shard]]
    first_mine = [spread_rows(piece) for piece in first_piece]
    own_probs = attention_probs(jnp.concatenate([query, key_stash]))
    late_value, late_out, _ = lax.optimization_barrier((w_value, w_out, own_probs))
    first_table = load_first(facts, late_value, late_out)
    other_probs = swap_half(own_probs)
    swapped, _ = lax.optimization_barrier((first_mine, first_table))
    first_theirs = [[swap_core(piece) for piece in pieces] for pieces in swapped]

    probs = [own_probs, other_probs]
    partial, first_full = [None, None], [None, None]
    for m in (1, 0):
        mine = first_mine[m]
        if m == 0:
            mine, probs, _ = lax.optimization_barrier((mine, probs, partial[1]))
        partial[m], first_full[m] = project(
            m, shard, facts, other_note, (first_table,), mine, first_theirs[m]
        )
    arrived = [swap_half(partial[1]), swap_half(partial[0])]
    later_value, _ = lax.optimization_barrier((w_value, partial))
    value_table = load_table(later_value, VALUE_VMEM_BYTES)
    first_result, first_sent = [None, None], [None, None]
    second_piece, second_full = [None, None], [None, None]
    for m in range(2):
        first_result[m], keep, send = mix(
            ODD, m, facts, other_note, probs[m], value_table, partial[m], arrived[m], outer
        )
        first_sent[m] = combine(facts, keep, swap_core(send), first_piece[m])
    later_out, _ = lax.optimization_barrier((w_out, first_sent))
    out_table = load_table(later_out, OUT_VMEM_BYTES)
    later_input, _ = lax.optimization_barrier((section_input[0], out_table))
    input_piece = [own_columns(later_input), swap_half(other_columns(later_input))]
    for m in range(2):
        received = [swap_section(part, d) for d, part in enumerate(first_sent[m])]
        second_piece[m] = arrive(facts, input_piece[m], received)
    for m in range(2):
        mine = spread_rows(second_piece[m])
        theirs = [swap_core(piece) for piece in mine]
        partial[m], second_full[m] = project(
            m, shard, facts, other_note, (value_table, out_table), mine, theirs
        )
    arrived = [swap_half(partial[1]), swap_half(partial[0])]
    second_result, last_sent = [None, None], [None, None]
    for m in (1, 0):
        second_result[m], keep, send = mix(
            EVEN, m, facts, other_note, probs[m], value_table, partial[m], arrived[m], outer
        )
        if m == 0:
            keep, _ = lax.optimization_barrier((keep, last_sent[1]))
        last_sent[m] = combine(facts, keep, swap_core(send), second_piece[m], first_sent[m])
    other_parts = [to_other_half(part, d) for d, part in enumerate(last_sent[1])]
    own_parts = [last_sent[0][0]] + [to_row(part, d + 1) for d, part in enumerate(last_sent[0][1:])]
    second_result, _ = lax.optimization_barrier((second_result, last_sent))
    grad_value, grad_out = weight_grads(
        facts, first_result, second_result, first_full, second_full
    )
    own_parts, other_parts, _ = lax.optimization_barrier((own_parts, other_parts, grad_value))
    input_grad = assemble(facts, own_parts, other_parts)
    return (input_grad, grad_value, grad_out)


def solution(mesh):
    sections, tensor = mesh.devices.shape
    split = Mesh(
        mesh.devices.reshape(sections // 2, 2, tensor // 2, 2), ("pair", "half", "outer", "core")
    )
    slots, places = ("pair", "half"), ("outer", "core")
    by_tokens = P(slots, places, None)
    by_rows = P(slots, None, places, None)
    return jax.shard_map(
        on_device,
        mesh=split,
        in_specs=(by_tokens, by_tokens, by_tokens, by_tokens, P(slots), by_rows, by_rows),
        out_specs=(by_tokens, by_tokens, by_tokens),
        check_vma=False,
    )
```

```python
import functools
import math

import jax
import jax.numpy as jnp
from jax import lax
from jax.experimental import pallas as pl
from jax.experimental.pallas import tpu as pltpu
from jax.sharding import Mesh, PartitionSpec as P

HEAD_DIM = 96
CHUNKS = 4
VMEM_BYTES = 8 * 2**20
GRAD_VMEM_BYTES = 16 * 2**20
FIRST_VMEM_BYTES = 46 * 2**20
VALUE_VMEM_BYTES = 47 * 2**20
OUT_VMEM_BYTES = 42 * 2**20
ODD, EVEN, VERSION, CORE, ROW, HALF = range(6)
LANES = 128
NOTE_ROWS = 16
SMALL = pl.CostEstimate(flops=1, bytes_accessed=1, transcendentals=0)
NN = (((1,), (0,)), ((), ()))
NT = (((1,), (1,)), ((), ()))
TN = (((0,), (0,)), ((), ()))


def matmul(left_side, right_side, dims):
    return lax.dot_general(left_side, right_side, dims, preferred_element_type=jnp.float32)


def in_vmem():
    return pl.BlockSpec(memory_space=pltpu.VMEM)


def in_smem():
    return pl.BlockSpec(memory_space=pltpu.SMEM)


def in_hbm():
    return pl.BlockSpec(memory_space=pltpu.HBM)


def in_place():
    return pl.BlockSpec(memory_space=pl.ANY)


def picked_version(index, facts_ref, note_ref):
    if index == 0:
        return facts_ref[VERSION]
    note = note_ref[note_ref.shape[0] - NOTE_ROWS :, :]
    return (jnp.max(note.astype(jnp.float32)) > 0.5).astype(jnp.int32)


def project_kernel(index, outer, shard, n_tables, facts_ref, note_ref, *refs):
    table_refs, piece_refs = refs[:n_tables], refs[n_tables:-2]
    partial_ref, full_ref = refs[-2:]
    version = picked_version(index, facts_ref, note_ref)
    first_core = facts_ref[CORE] == 0
    mine = [ref[:shard, :] for ref in piece_refs[:outer]]
    theirs = [ref[:shard, :] for ref in piece_refs[outer:]]
    for place in range(outer):
        offset = facts_ref[ROW] ^ place
        own, other = mine[0], theirs[0]
        for delta in range(1, outer):
            own = jnp.where(offset == delta, mine[delta], own)
            other = jnp.where(offset == delta, theirs[delta], other)
        start = 2 * place * shard
        full_ref[start : start + shard, :] = jnp.where(first_core, own, other)
        full_ref[start + shard : start + 2 * shard, :] = jnp.where(first_core, other, own)
    flipped = full_ref[...].T

    def rows_of(table_ref):
        partial_ref[...] = matmul(table_ref[0, version], flipped, NN).astype(jnp.bfloat16)

    if n_tables == 1:
        rows_of(table_refs[0])
    else:
        pl.when(facts_ref[ODD] == 1)(lambda: rows_of(table_refs[0]))
        pl.when(facts_ref[ODD] == 0)(lambda: rows_of(table_refs[1]))


def project(index, shard, facts, note, tables, mine, theirs):
    outer = len(mine)
    rows, width = tables[0].shape[2:]
    tokens = 2 * outer * shard
    return pl.pallas_call(
        functools.partial(project_kernel, index, outer, shard, len(tables)),
        out_shape=(
            jax.ShapeDtypeStruct((rows, tokens), jnp.bfloat16),
            jax.ShapeDtypeStruct((tokens, width), jnp.bfloat16),
        ),
        in_specs=[in_smem()] + [in_vmem()] * (1 + len(tables) + 2 * outer),
        out_specs=(in_vmem(), in_vmem()),
        compiler_params=pltpu.CompilerParams(vmem_limit_bytes=VMEM_BYTES),
        cost_estimate=SMALL,
        name="project",
    )(facts, note, *tables, *mine, *theirs)


def mix_kernel(
    outer,
    natural,
    index,
    facts_ref,
    note_ref,
    value_ref,
    mine_ref,
    arrived_ref,
    probs_ref,
    result_ref,
    keep_ref,
    send_ref,
):
    version = picked_version(index, facts_ref, note_ref)
    step = value_ref.shape[3] // CHUNKS
    tokens = mine_ref.shape[1]

    def heads(dims):
        for head in range(mine_ref.shape[0] // HEAD_DIM):
            rows = pl.ds(head * HEAD_DIM, HEAD_DIM)
            total = mine_ref[rows, :].astype(jnp.float32) + arrived_ref[rows, :].astype(jnp.float32)
            probs = probs_ref[head * tokens : (head + 1) * tokens, :]
            mixed = matmul(total.astype(jnp.bfloat16), probs, dims)
            result_ref[rows, :] = mixed.astype(jnp.bfloat16)

    pl.when(facts_ref[natural] == 1)(lambda: heads(NN))
    pl.when(facts_ref[natural] == 0)(lambda: heads(NT))

    flipped = result_ref[...].T
    second_core = facts_ref[CORE] == 1
    shard = tokens // (2 * outer)
    for chunk in range(CHUNKS):
        columns = pl.ds(chunk * step, step)
        partial = matmul(flipped, value_ref[0, version, :, columns], NN)
        for place in range(outer):
            low = partial[2 * place * shard : (2 * place + 1) * shard]
            high = partial[(2 * place + 1) * shard : (2 * place + 2) * shard]
            keep_ref[place, :, columns] = jnp.where(second_core, high, low).astype(jnp.bfloat16)
            send_ref[place, :, columns] = jnp.where(second_core, low, high).astype(jnp.bfloat16)


def mix(natural, index, facts, note, message, w_value, mine, arrived, outer):
    rows, width = w_value.shape[2:]
    tokens = mine.shape[1]
    half = jax.ShapeDtypeStruct((outer, tokens // (2 * outer), width), jnp.bfloat16)
    return pl.pallas_call(
        functools.partial(mix_kernel, outer, natural, index),
        out_shape=(jax.ShapeDtypeStruct((rows, tokens), jnp.bfloat16), half, half),
        in_specs=[in_smem()] + [in_vmem()] * 5,
        out_specs=(in_vmem(), in_vmem(), in_vmem()),
        compiler_params=pltpu.CompilerParams(vmem_limit_bytes=VMEM_BYTES),
        cost_estimate=SMALL,
        name="mix",
    )(facts, note, w_value, mine, arrived, message)


def combine_kernel(outer, last, facts_ref, keep_ref, arrived_ref, addend_ref, *refs):
    first_refs, sent_refs = refs[:-outer], refs[-outer:]
    for delta in range(outer):
        spot = facts_ref[ROW] ^ delta
        total = keep_ref[spot].astype(jnp.float32) + arrived_ref[spot].astype(jnp.float32)
        if delta == 0:
            total = total + addend_ref[: total.shape[0], :].astype(jnp.float32)
        total = total.astype(jnp.bfloat16)
        if last:
            total = jnp.where(facts_ref[ODD] == 1, first_refs[delta][...], total)
        sent_refs[delta][...] = total


def combine(facts, keep, arrived, addend, first_sent=()):
    outer, shard, width = keep.shape
    piece = jax.ShapeDtypeStruct((shard, width), jnp.bfloat16)
    return pl.pallas_call(
        functools.partial(combine_kernel, outer, len(first_sent) > 0),
        out_shape=(piece,) * outer,
        in_specs=[in_smem()] + [in_vmem()] * (3 + len(first_sent)),
        out_specs=(in_vmem(),) * outer,
        compiler_params=pltpu.CompilerParams(vmem_limit_bytes=VMEM_BYTES),
        cost_estimate=SMALL,
        name="combine",
    )(facts, keep, arrived, addend, *first_sent)


def weight_grad_kernel(
    facts_ref, a0, a1, b0, b1, first0, first1, second0, second1, value_ref, out_ref
):
    odd = facts_ref[ODD] == 1
    left_first = jnp.concatenate([a0[...], a1[...]], axis=1)
    left_second = jnp.concatenate([b0[...], b1[...]], axis=1)
    right_second = jnp.concatenate([second0[...], second1[...]], axis=0)
    right_first = jnp.concatenate([first0[...], first1[...]], axis=0)
    grad_first = matmul(left_first, right_second, NN)
    grad_second = matmul(left_second, right_first, NN)
    value_ref[0] = jnp.where(odd, grad_first, grad_second).astype(jnp.bfloat16)
    out_ref[0] = jnp.where(odd, grad_second, grad_first).astype(jnp.bfloat16)


def weight_grads(facts, first_results, second_results, first_full, second_full):
    rows, tokens = first_results[0].shape
    width = first_full[0].shape[1]
    step = rows // CHUNKS
    grad = jax.ShapeDtypeStruct((1, rows, width), jnp.bfloat16)
    left = pl.BlockSpec((step, tokens), lambda i: (i, 0))
    single = pl.BlockSpec((tokens, width), lambda i: (0, 0))
    wide = pl.BlockSpec((1, step, width), lambda i: (0, i, 0))
    return pl.pallas_call(
        weight_grad_kernel,
        grid=(CHUNKS,),
        out_shape=(grad, grad),
        in_specs=[in_smem()] + [left] * 4 + [single] * 4,
        out_specs=(wide, wide),
        compiler_params=pltpu.CompilerParams(vmem_limit_bytes=GRAD_VMEM_BYTES),
        cost_estimate=SMALL,
        name="weight_grads",
    )(facts, *first_results, *second_results, *first_full, *second_full)


def load(source_ref, table_ref, sems):
    step = table_ref.shape[2] // CHUNKS
    copies = []
    for version in range(2):
        for chunk in range(CHUNKS):
            spot = (slice(None), version, pl.ds(chunk * step, step))
            copies.append(
                pltpu.make_async_copy(
                    source_ref.at[spot], table_ref.at[spot], sems.at[version * CHUNKS + chunk]
                )
            )
    return copies


def probs_kernel(stash_ref, probs_ref):
    tokens = stash_ref.shape[2]
    causal = lax.broadcasted_iota(jnp.int32, (tokens, tokens), 1) <= lax.broadcasted_iota(
        jnp.int32, (tokens, tokens), 0
    )
    for head in range(stash_ref.shape[1] // HEAD_DIM):
        rows = pl.ds(head * HEAD_DIM, HEAD_DIM)
        scores = matmul(stash_ref[0, rows, :], stash_ref[1, rows, :], TN)
        scores = jnp.where(causal, scores * (1.0 / math.sqrt(HEAD_DIM)), -jnp.inf)
        expo = jnp.exp(scores - jnp.max(scores, axis=1, keepdims=True))
        probs = (expo / jnp.sum(expo, axis=1, keepdims=True)).astype(jnp.bfloat16)
        probs_ref[head * tokens : (head + 1) * tokens, :] = probs


def attention_probs(stash):
    rows, tokens = stash.shape[1:]
    return pl.pallas_call(
        probs_kernel,
        out_shape=jax.ShapeDtypeStruct((rows // HEAD_DIM * tokens, tokens), jnp.bfloat16),
        in_specs=[in_vmem()],
        out_specs=in_vmem(),
        compiler_params=pltpu.CompilerParams(vmem_limit_bytes=VMEM_BYTES),
        cost_estimate=SMALL,
        name="probs",
    )(stash)


def load_kernel(source_ref, table_ref, sems):
    copies = load(source_ref, table_ref, sems)
    for copy in copies:
        copy.start()
    for copy in copies:
        copy.wait()


def load_first_kernel(facts_ref, value_ref, out_ref, table_ref, sems):
    def start(source_ref):
        for copy in load(source_ref, table_ref, sems):
            copy.start()

    pl.when(facts_ref[ODD] == 1)(lambda: start(out_ref))
    pl.when(facts_ref[ODD] == 0)(lambda: start(value_ref))
    for copy in load(value_ref, table_ref, sems):
        copy.wait()


def load_first(facts, w_value, w_out):
    return pl.pallas_call(
        load_first_kernel,
        out_shape=jax.ShapeDtypeStruct(w_value.shape, jnp.bfloat16),
        in_specs=[in_smem(), in_hbm(), in_hbm()],
        out_specs=in_vmem(),
        scratch_shapes=[pltpu.SemaphoreType.DMA((2 * CHUNKS,))],
        compiler_params=pltpu.CompilerParams(vmem_limit_bytes=FIRST_VMEM_BYTES),
        cost_estimate=SMALL,
        name="load_first",
    )(facts, w_value, w_out)


def load_table(table, grant):
    return pl.pallas_call(
        load_kernel,
        out_shape=jax.ShapeDtypeStruct(table.shape, jnp.bfloat16),
        in_specs=[in_hbm()],
        out_specs=in_vmem(),
        scratch_shapes=[pltpu.SemaphoreType.DMA((2 * CHUNKS,))],
        compiler_params=pltpu.CompilerParams(vmem_limit_bytes=grant),
        cost_estimate=SMALL,
        name="load_table",
    )(table)


def on_device(section_input, query, key_stash, incoming, version, w_value, w_out):
    half = lax.axis_index("half")
    odd_flag = lax.axis_index("pair") % 2
    odd = odd_flag == 1
    core, row = lax.axis_index("core"), lax.axis_index("outer")
    n_pairs = lax.axis_size("pair")
    outer = lax.axis_size("outer")
    n_tensor = 2 * outer
    width = w_value.shape[3]
    shard = section_input.shape[1]

    def swap_half(array):
        return lax.ppermute(array, "half", [(0, 1), (1, 0)])

    def swap_core(array):
        return lax.ppermute(array, "core", [(0, 1), (1, 0)])

    def to_row(array, delta):
        return lax.ppermute(array, "outer", [(i, i ^ delta) for i in range(outer)])

    def to_other_half(array, delta):
        pairs = [
            (h * n_tensor + i, (1 - h) * n_tensor + (i ^ (2 * delta)))
            for h in range(2)
            for i in range(n_tensor)
        ]
        return lax.ppermute(array, ("half", "outer", "core"), pairs)

    def swap_section(array, delta):
        pairs = [
            (p * n_tensor + i, (p ^ 1) * n_tensor + (i ^ (2 * delta)))
            for p in range(n_pairs)
            for i in range(n_tensor)
        ]
        return lax.ppermute(array, ("pair", "outer", "core"), pairs)

    def own_columns(array):
        return lax.dynamic_slice_in_dim(array, half * width, width, 1)

    def other_columns(array):
        return lax.dynamic_slice_in_dim(array, (1 - half) * width, width, 1)

    def total(parts):
        value = parts[0].astype(jnp.float32)
        for part in parts[1:]:
            value = value + part.astype(jnp.float32)
        return value

    def spread_rows(piece):
        return [piece] + [to_row(piece, delta) for delta in range(1, outer)]

    facts = jnp.stack([odd_flag, 1 - odd_flag, version[0], core, row, half])
    first = jnp.where(odd, incoming[0], section_input[0])
    own_piece, sent_piece = own_columns(first), other_columns(first)
    other_piece = swap_half(sent_piece)
    first_piece = [own_piece, other_piece]
    later_own, _ = lax.optimization_barrier((own_piece, other_piece))
    first_mine = [spread_rows(later_own), spread_rows(other_piece)]
    own_probs = attention_probs(jnp.concatenate([query, key_stash]))
    note = jnp.full((NOTE_ROWS, LANES), version[0], jnp.int32).astype(jnp.bfloat16)
    own_probs = jnp.concatenate([own_probs, note])
    other_probs = swap_half(own_probs)
    other_note = other_probs
    late_value, late_out, _ = lax.optimization_barrier((w_value, w_out, own_probs))
    first_table = load_first(facts, late_value, late_out)
    swapped, _ = lax.optimization_barrier((first_mine, first_table))
    first_theirs = [[swap_core(piece) for piece in pieces] for pieces in swapped]

    probs = [own_probs, other_probs]
    partial, first_full = [None, None], [None, None]
    for m in (1, 0):
        mine = first_mine[m]
        if m == 0:
            mine, probs, _ = lax.optimization_barrier((mine, probs, partial[1]))
        partial[m], first_full[m] = project(
            m, shard, facts, other_note, (first_table,), mine, first_theirs[m]
        )
    arrived = [swap_half(partial[1]), swap_half(partial[0])]
    later_value, _ = lax.optimization_barrier((w_value, partial))
    value_table = load_table(later_value, VALUE_VMEM_BYTES)
    first_result, first_sent = [None, None], [None, None]
    second_piece, second_full = [None, None], [None, None]
    for m in range(2):
        first_result[m], keep, send = mix(
            ODD, m, facts, other_note, probs[m], value_table, partial[m], arrived[m], outer
        )
        first_sent[m] = combine(facts, keep, swap_core(send), first_piece[m])
    later_out, _ = lax.optimization_barrier((w_out, first_sent))
    out_table = load_table(later_out, OUT_VMEM_BYTES)
    later_input, _ = lax.optimization_barrier((section_input[0], out_table))
    input_piece = [own_columns(later_input), swap_half(other_columns(later_input))]
    for m in range(2):
        received = [swap_section(part, d) for d, part in enumerate(first_sent[m])]
        second_piece[m] = jnp.where(odd, input_piece[m], total(received).astype(jnp.bfloat16))
    for m in range(2):
        mine = spread_rows(second_piece[m])
        theirs = [swap_core(piece) for piece in mine]
        partial[m], second_full[m] = project(
            m, shard, facts, other_note, (value_table, out_table), mine, theirs
        )
    arrived = [swap_half(partial[1]), swap_half(partial[0])]
    second_result, last_sent = [None, None], [None, None]
    for m in (1, 0):
        second_result[m], keep, send = mix(
            EVEN, m, facts, other_note, probs[m], value_table, partial[m], arrived[m], outer
        )
        if m == 0:
            keep, _ = lax.optimization_barrier((keep, last_sent[1]))
        last_sent[m] = combine(facts, keep, swap_core(send), second_piece[m], first_sent[m])
    other_parts = [to_other_half(part, d) for d, part in enumerate(last_sent[1])]
    own_parts = [last_sent[0][0]] + [to_row(part, d + 1) for d, part in enumerate(last_sent[0][1:])]
    second_result, _ = lax.optimization_barrier((second_result, last_sent))
    grad_value, grad_out = weight_grads(
        facts, first_result, second_result, first_full, second_full
    )
    own_parts, other_parts, _ = lax.optimization_barrier((own_parts, other_parts, grad_value))
    own_grad = total(own_parts).astype(jnp.bfloat16)
    other_grad = total(other_parts).astype(jnp.bfloat16)
    input_grad = jnp.concatenate(
        [jnp.where(half == 0, own_grad, other_grad), jnp.where(half == 0, other_grad, own_grad)],
        axis=1,
    )
    return (input_grad[None], grad_value, grad_out)


def solution(mesh):
    sections, tensor = mesh.devices.shape
    split = Mesh(
        mesh.devices.reshape(sections // 2, 2, tensor // 2, 2), ("pair", "half", "outer", "core")
    )
    slots, places = ("pair", "half"), ("outer", "core")
    by_tokens = P(slots, places, None)
    by_rows = P(slots, None, places, None)
    return jax.shard_map(
        on_device,
        mesh=split,
        in_specs=(by_tokens, by_tokens, by_tokens, by_tokens, P(slots), by_rows, by_rows),
        out_specs=(by_tokens, by_tokens, by_tokens),
        check_vma=False,
    )
```

```python
import functools
import math

import jax
import jax.numpy as jnp
from jax import lax
from jax.experimental import pallas as pl
from jax.experimental.pallas import tpu as pltpu
from jax.sharding import Mesh, PartitionSpec as P

HEAD_DIM = 96
CHUNKS = 4
VMEM_BYTES = 8 * 2**20
GRAD_VMEM_BYTES = 16 * 2**20
FIRST_VMEM_BYTES = 46 * 2**20
VALUE_VMEM_BYTES = 47 * 2**20
OUT_VMEM_BYTES = 42 * 2**20
ODD, EVEN, VERSION, CORE, ROW, HALF = range(6)
LANES = 128
NOTE_ROWS = 16
SMALL = pl.CostEstimate(flops=1, bytes_accessed=1, transcendentals=0)
NN = (((1,), (0,)), ((), ()))
NT = (((1,), (1,)), ((), ()))
TN = (((0,), (0,)), ((), ()))


def matmul(left_side, right_side, dims):
    return lax.dot_general(left_side, right_side, dims, preferred_element_type=jnp.float32)


def in_vmem():
    return pl.BlockSpec(memory_space=pltpu.VMEM)


def in_smem():
    return pl.BlockSpec(memory_space=pltpu.SMEM)


def in_hbm():
    return pl.BlockSpec(memory_space=pltpu.HBM)


def in_place():
    return pl.BlockSpec(memory_space=pl.ANY)


def picked_version(index, facts_ref, note_ref):
    if index == 0:
        return facts_ref[VERSION]
    note = note_ref[note_ref.shape[0] - NOTE_ROWS :, :]
    return (jnp.max(note.astype(jnp.float32)) > 0.5).astype(jnp.int32)


def project_kernel(index, outer, shard, n_tables, facts_ref, note_ref, *refs):
    table_refs, piece_refs = refs[:n_tables], refs[n_tables:-2]
    partial_ref, full_ref = refs[-2:]
    version = picked_version(index, facts_ref, note_ref)
    first_core = facts_ref[CORE] == 0
    mine = [ref[:shard, :] for ref in piece_refs[:outer]]
    theirs = [ref[:shard, :] for ref in piece_refs[outer:]]
    for place in range(outer):
        offset = facts_ref[ROW] ^ place
        own, other = mine[0], theirs[0]
        for delta in range(1, outer):
            own = jnp.where(offset == delta, mine[delta], own)
            other = jnp.where(offset == delta, theirs[delta], other)
        start = 2 * place * shard
        full_ref[start : start + shard, :] = jnp.where(first_core, own, other)
        full_ref[start + shard : start + 2 * shard, :] = jnp.where(first_core, other, own)
    flipped = full_ref[...].T

    def rows_of(table_ref):
        partial_ref[...] = matmul(table_ref[0, version], flipped, NN).astype(jnp.bfloat16)

    if n_tables == 1:
        rows_of(table_refs[0])
    else:
        pl.when(facts_ref[ODD] == 1)(lambda: rows_of(table_refs[0]))
        pl.when(facts_ref[ODD] == 0)(lambda: rows_of(table_refs[1]))


def project(index, shard, facts, note, tables, mine, theirs):
    outer = len(mine)
    rows, width = tables[0].shape[2:]
    tokens = 2 * outer * shard
    return pl.pallas_call(
        functools.partial(project_kernel, index, outer, shard, len(tables)),
        out_shape=(
            jax.ShapeDtypeStruct((rows, tokens), jnp.bfloat16),
            jax.ShapeDtypeStruct((tokens, width), jnp.bfloat16),
        ),
        in_specs=[in_smem()] + [in_vmem()] * (1 + len(tables) + 2 * outer),
        out_specs=(in_vmem(), in_vmem()),
        compiler_params=pltpu.CompilerParams(vmem_limit_bytes=VMEM_BYTES),
        cost_estimate=SMALL,
        name="project",
    )(facts, note, *tables, *mine, *theirs)


def mix_kernel(
    outer,
    natural,
    index,
    facts_ref,
    note_ref,
    value_ref,
    mine_ref,
    arrived_ref,
    probs_ref,
    result_ref,
    keep_ref,
    send_ref,
):
    version = picked_version(index, facts_ref, note_ref)
    step = value_ref.shape[3] // CHUNKS
    tokens = mine_ref.shape[1]

    def heads(dims):
        for head in range(mine_ref.shape[0] // HEAD_DIM):
            rows = pl.ds(head * HEAD_DIM, HEAD_DIM)
            total = mine_ref[rows, :].astype(jnp.float32) + arrived_ref[rows, :].astype(jnp.float32)
            probs = probs_ref[head * tokens : (head + 1) * tokens, :]
            mixed = matmul(total.astype(jnp.bfloat16), probs, dims)
            result_ref[rows, :] = mixed.astype(jnp.bfloat16)

    pl.when(facts_ref[natural] == 1)(lambda: heads(NN))
    pl.when(facts_ref[natural] == 0)(lambda: heads(NT))

    flipped = result_ref[...].T
    second_core = facts_ref[CORE] == 1
    shard = tokens // (2 * outer)
    for chunk in range(CHUNKS):
        columns = pl.ds(chunk * step, step)
        partial = matmul(flipped, value_ref[0, version, :, columns], NN)
        for place in range(outer):
            low = partial[2 * place * shard : (2 * place + 1) * shard]
            high = partial[(2 * place + 1) * shard : (2 * place + 2) * shard]
            keep_ref[place, :, columns] = jnp.where(second_core, high, low).astype(jnp.bfloat16)
            send_ref[place, :, columns] = jnp.where(second_core, low, high).astype(jnp.bfloat16)


def mix(natural, index, facts, note, message, w_value, mine, arrived, outer):
    rows, width = w_value.shape[2:]
    tokens = mine.shape[1]
    half = jax.ShapeDtypeStruct((outer, tokens // (2 * outer), width), jnp.bfloat16)
    return pl.pallas_call(
        functools.partial(mix_kernel, outer, natural, index),
        out_shape=(jax.ShapeDtypeStruct((rows, tokens), jnp.bfloat16), half, half),
        in_specs=[in_smem()] + [in_vmem()] * 5,
        out_specs=(in_vmem(), in_vmem(), in_vmem()),
        compiler_params=pltpu.CompilerParams(vmem_limit_bytes=VMEM_BYTES),
        cost_estimate=SMALL,
        name="mix",
    )(facts, note, w_value, mine, arrived, message)


def combine_kernel(outer, last, facts_ref, keep_ref, arrived_ref, addend_ref, *refs):
    first_refs, sent_refs = refs[:-outer], refs[-outer:]
    for delta in range(outer):
        spot = facts_ref[ROW] ^ delta
        total = keep_ref[spot].astype(jnp.float32) + arrived_ref[spot].astype(jnp.float32)
        if delta == 0:
            total = total + addend_ref[: total.shape[0], :].astype(jnp.float32)
        total = total.astype(jnp.bfloat16)
        if last:
            total = jnp.where(facts_ref[ODD] == 1, first_refs[delta][...], total)
        sent_refs[delta][...] = total


def combine(facts, keep, arrived, addend, first_sent=()):
    outer, shard, width = keep.shape
    piece = jax.ShapeDtypeStruct((shard, width), jnp.bfloat16)
    return pl.pallas_call(
        functools.partial(combine_kernel, outer, len(first_sent) > 0),
        out_shape=(piece,) * outer,
        in_specs=[in_smem()] + [in_vmem()] * (3 + len(first_sent)),
        out_specs=(in_vmem(),) * outer,
        compiler_params=pltpu.CompilerParams(vmem_limit_bytes=VMEM_BYTES),
        cost_estimate=SMALL,
        name="combine",
    )(facts, keep, arrived, addend, *first_sent)


def weight_grad_kernel(
    facts_ref, a0, a1, b0, b1, first0, first1, second0, second1, value_ref, out_ref
):
    odd = facts_ref[ODD] == 1
    left_first = jnp.concatenate([a0[...], a1[...]], axis=1)
    left_second = jnp.concatenate([b0[...], b1[...]], axis=1)
    right_second = jnp.concatenate([second0[...], second1[...]], axis=0)
    right_first = jnp.concatenate([first0[...], first1[...]], axis=0)
    grad_first = matmul(left_first, right_second, NN)
    grad_second = matmul(left_second, right_first, NN)
    value_ref[0] = jnp.where(odd, grad_first, grad_second).astype(jnp.bfloat16)
    out_ref[0] = jnp.where(odd, grad_second, grad_first).astype(jnp.bfloat16)


def weight_grads(facts, first_results, second_results, first_full, second_full):
    rows, tokens = first_results[0].shape
    width = first_full[0].shape[1]
    step = rows // CHUNKS
    grad = jax.ShapeDtypeStruct((1, rows, width), jnp.bfloat16)
    left = pl.BlockSpec((step, tokens), lambda i: (i, 0))
    single = pl.BlockSpec((tokens, width), lambda i: (0, 0))
    wide = pl.BlockSpec((1, step, width), lambda i: (0, i, 0))
    return pl.pallas_call(
        weight_grad_kernel,
        grid=(CHUNKS,),
        out_shape=(grad, grad),
        in_specs=[in_smem()] + [left] * 4 + [single] * 4,
        out_specs=(wide, wide),
        compiler_params=pltpu.CompilerParams(vmem_limit_bytes=GRAD_VMEM_BYTES),
        cost_estimate=SMALL,
        name="weight_grads",
    )(facts, *first_results, *second_results, *first_full, *second_full)


def load(source_ref, table_ref, sems):
    step = table_ref.shape[2] // CHUNKS
    copies = []
    for version in range(2):
        for chunk in range(CHUNKS):
            spot = (slice(None), version, pl.ds(chunk * step, step))
            copies.append(
                pltpu.make_async_copy(
                    source_ref.at[spot], table_ref.at[spot], sems.at[version * CHUNKS + chunk]
                )
            )
    return copies


def probs_kernel(stash_ref, probs_ref):
    tokens = stash_ref.shape[2]
    causal = lax.broadcasted_iota(jnp.int32, (tokens, tokens), 1) <= lax.broadcasted_iota(
        jnp.int32, (tokens, tokens), 0
    )
    for head in range(stash_ref.shape[1] // HEAD_DIM):
        rows = pl.ds(head * HEAD_DIM, HEAD_DIM)
        scores = matmul(stash_ref[0, rows, :], stash_ref[1, rows, :], TN)
        scores = jnp.where(causal, scores * (1.0 / math.sqrt(HEAD_DIM)), -jnp.inf)
        expo = jnp.exp(scores - jnp.max(scores, axis=1, keepdims=True))
        probs = (expo / jnp.sum(expo, axis=1, keepdims=True)).astype(jnp.bfloat16)
        probs_ref[head * tokens : (head + 1) * tokens, :] = probs


def attention_probs(stash):
    rows, tokens = stash.shape[1:]
    return pl.pallas_call(
        probs_kernel,
        out_shape=jax.ShapeDtypeStruct((rows // HEAD_DIM * tokens, tokens), jnp.bfloat16),
        in_specs=[in_vmem()],
        out_specs=in_vmem(),
        compiler_params=pltpu.CompilerParams(vmem_limit_bytes=VMEM_BYTES),
        cost_estimate=SMALL,
        name="probs",
    )(stash)


def load_kernel(source_ref, table_ref, sems):
    copies = load(source_ref, table_ref, sems)
    for copy in copies:
        copy.start()
    for copy in copies:
        copy.wait()


def load_first_kernel(facts_ref, value_ref, out_ref, table_ref, sems):
    def start(source_ref):
        for copy in load(source_ref, table_ref, sems):
            copy.start()

    pl.when(facts_ref[ODD] == 1)(lambda: start(out_ref))
    pl.when(facts_ref[ODD] == 0)(lambda: start(value_ref))
    for copy in load(value_ref, table_ref, sems):
        copy.wait()


def load_first(facts, w_value, w_out):
    return pl.pallas_call(
        load_first_kernel,
        out_shape=jax.ShapeDtypeStruct(w_value.shape, jnp.bfloat16),
        in_specs=[in_smem(), in_hbm(), in_hbm()],
        out_specs=in_vmem(),
        scratch_shapes=[pltpu.SemaphoreType.DMA((2 * CHUNKS,))],
        compiler_params=pltpu.CompilerParams(vmem_limit_bytes=FIRST_VMEM_BYTES),
        cost_estimate=SMALL,
        name="load_first",
    )(facts, w_value, w_out)


def load_table(table, grant):
    return pl.pallas_call(
        load_kernel,
        out_shape=jax.ShapeDtypeStruct(table.shape, jnp.bfloat16),
        in_specs=[in_hbm()],
        out_specs=in_vmem(),
        scratch_shapes=[pltpu.SemaphoreType.DMA((2 * CHUNKS,))],
        compiler_params=pltpu.CompilerParams(vmem_limit_bytes=grant),
        cost_estimate=SMALL,
        name="load_table",
    )(table)


def on_device(section_input, query, key_stash, incoming, version, w_value, w_out):
    half = lax.axis_index("half")
    odd_flag = lax.axis_index("pair") % 2
    odd = odd_flag == 1
    core, row = lax.axis_index("core"), lax.axis_index("outer")
    n_pairs = lax.axis_size("pair")
    outer = lax.axis_size("outer")
    n_tensor = 2 * outer
    width = w_value.shape[3]
    shard = section_input.shape[1]

    def swap_half(array):
        return lax.ppermute(array, "half", [(0, 1), (1, 0)])

    def swap_core(array):
        return lax.ppermute(array, "core", [(0, 1), (1, 0)])

    def to_row(array, delta):
        return lax.ppermute(array, "outer", [(i, i ^ delta) for i in range(outer)])

    def to_other_half(array, delta):
        pairs = [
            (h * n_tensor + i, (1 - h) * n_tensor + (i ^ (2 * delta)))
            for h in range(2)
            for i in range(n_tensor)
        ]
        return lax.ppermute(array, ("half", "outer", "core"), pairs)

    def swap_section(array, delta):
        pairs = [
            (p * n_tensor + i, (p ^ 1) * n_tensor + (i ^ (2 * delta)))
            for p in range(n_pairs)
            for i in range(n_tensor)
        ]
        return lax.ppermute(array, ("pair", "outer", "core"), pairs)

    def own_columns(array):
        return lax.dynamic_slice_in_dim(array, half * width, width, 1)

    def other_columns(array):
        return lax.dynamic_slice_in_dim(array, (1 - half) * width, width, 1)

    def total(parts):
        value = parts[0].astype(jnp.float32)
        for part in parts[1:]:
            value = value + part.astype(jnp.float32)
        return value

    def spread_rows(piece):
        return [piece] + [to_row(piece, delta) for delta in range(1, outer)]

    facts = jnp.stack([odd_flag, 1 - odd_flag, version[0], core, row, half])
    first = jnp.where(odd, incoming[0], section_input[0])
    own_piece, sent_piece = own_columns(first), other_columns(first)
    other_piece = swap_half(sent_piece)
    first_piece = [own_piece, other_piece]
    later_own, _ = lax.optimization_barrier((own_piece, other_piece))
    first_mine = [spread_rows(later_own), spread_rows(other_piece)]
    own_probs = attention_probs(jnp.concatenate([query, key_stash]))
    note = jnp.full((NOTE_ROWS, LANES), version[0], jnp.int32).astype(jnp.bfloat16)
    own_probs = jnp.concatenate([own_probs, note])
    other_probs = swap_half(own_probs)
    other_note = other_probs
    late_value, late_out, _ = lax.optimization_barrier((w_value, w_out, own_probs))
    first_table = load_first(facts, late_value, late_out)
    first_theirs = []
    for pieces in first_mine:
        later, _ = lax.optimization_barrier((pieces, first_table))
        first_theirs.append([swap_core(piece) for piece in later])

    probs = [own_probs, other_probs]
    partial, first_full = [None, None], [None, None]
    for m in (1, 0):
        mine = first_mine[m]
        if m == 0:
            mine, probs, _ = lax.optimization_barrier((mine, probs, partial[1]))
        partial[m], first_full[m] = project(
            m, shard, facts, other_note, (first_table,), mine, first_theirs[m]
        )
    arrived = [swap_half(partial[1]), swap_half(partial[0])]
    later_value, _ = lax.optimization_barrier((w_value, partial))
    value_table = load_table(later_value, VALUE_VMEM_BYTES)
    first_result, first_sent = [None, None], [None, None]
    second_piece, second_full = [None, None], [None, None]
    for m in range(2):
        first_result[m], keep, send = mix(
            ODD, m, facts, other_note, probs[m], value_table, partial[m], arrived[m], outer
        )
        first_sent[m] = combine(facts, keep, swap_core(send), first_piece[m])
    later_out, _ = lax.optimization_barrier((w_out, first_sent))
    out_table = load_table(later_out, OUT_VMEM_BYTES)
    later_input, _ = lax.optimization_barrier((section_input[0], out_table))
    input_own, input_sent = lax.optimization_barrier(
        (own_columns(later_input), other_columns(later_input))
    )
    input_piece = [input_own, swap_half(input_sent)]
    for m in range(2):
        received = [swap_section(part, d) for d, part in enumerate(first_sent[m])]
        second_piece[m] = jnp.where(odd, input_piece[m], total(received).astype(jnp.bfloat16))
    for m in range(2):
        mine = spread_rows(second_piece[m])
        theirs = [swap_core(piece) for piece in mine]
        partial[m], second_full[m] = project(
            m, shard, facts, other_note, (value_table, out_table), mine, theirs
        )
    arrived = [swap_half(partial[1]), swap_half(partial[0])]
    second_result, last_sent = [None, None], [None, None]
    for m in (1, 0):
        second_result[m], keep, send = mix(
            EVEN, m, facts, other_note, probs[m], value_table, partial[m], arrived[m], outer
        )
        if m == 0:
            keep, _ = lax.optimization_barrier((keep, last_sent[1]))
        last_sent[m] = combine(facts, keep, swap_core(send), second_piece[m], first_sent[m])
    other_parts = [to_other_half(part, d) for d, part in enumerate(last_sent[1])]
    own_parts = [last_sent[0][0]] + [to_row(part, d + 1) for d, part in enumerate(last_sent[0][1:])]
    second_result, _ = lax.optimization_barrier((second_result, last_sent))
    grad_value, grad_out = weight_grads(
        facts, first_result, second_result, first_full, second_full
    )
    own_parts, other_parts, _ = lax.optimization_barrier((own_parts, other_parts, grad_value))
    own_grad = total(own_parts).astype(jnp.bfloat16)
    other_grad = total(other_parts).astype(jnp.bfloat16)
    input_grad = jnp.concatenate(
        [jnp.where(half == 0, own_grad, other_grad), jnp.where(half == 0, other_grad, own_grad)],
        axis=1,
    )
    return (input_grad[None], grad_value, grad_out)


def solution(mesh):
    sections, tensor = mesh.devices.shape
    split = Mesh(
        mesh.devices.reshape(sections // 2, 2, tensor // 2, 2), ("pair", "half", "outer", "core")
    )
    slots, places = ("pair", "half"), ("outer", "core")
    by_tokens = P(slots, places, None)
    by_rows = P(slots, None, places, None)
    return jax.shard_map(
        on_device,
        mesh=split,
        in_specs=(by_tokens, by_tokens, by_tokens, by_tokens, P(slots), by_rows, by_rows),
        out_specs=(by_tokens, by_tokens, by_tokens),
        check_vma=False,
    )
```

```python
import functools
import math

import jax
import jax.numpy as jnp
from jax import lax
from jax.experimental import pallas as pl
from jax.experimental.pallas import tpu as pltpu
from jax.sharding import Mesh, PartitionSpec as P

HEAD_DIM = 96
CHUNKS = 4
VMEM_BYTES = 8 * 2**20
GRAD_VMEM_BYTES = 16 * 2**20
FIRST_VMEM_BYTES = 46 * 2**20
VALUE_VMEM_BYTES = 47 * 2**20
OUT_VMEM_BYTES = 42 * 2**20
LANES = 128
NOTE_ROWS = 16
SMALL = pl.CostEstimate(flops=1, bytes_accessed=1, transcendentals=0)
NN = (((1,), (0,)), ((), ()))
NT = (((1,), (1,)), ((), ()))
TN = (((0,), (0,)), ((), ()))


def matmul(left_side, right_side, dims):
    return lax.dot_general(left_side, right_side, dims, preferred_element_type=jnp.float32)


def in_vmem():
    return pl.BlockSpec(memory_space=pltpu.VMEM)


def in_hbm():
    return pl.BlockSpec(memory_space=pltpu.HBM)


def in_place():
    return pl.BlockSpec(memory_space=pl.ANY)


def is_odd():
    return (lax.axis_index("pair") & 1) == 1


def noted_version(message_ref):
    note = message_ref[message_ref.shape[0] - NOTE_ROWS :, :]
    return (jnp.max(note.astype(jnp.float32)) > 0.5).astype(jnp.int32)


def project_kernel(outer, shard, n_tables, message_ref, *refs):
    table_refs, piece_refs = refs[:n_tables], refs[n_tables:-2]
    partial_ref, full_ref = refs[-2:]
    version = noted_version(message_ref)
    first_core = lax.axis_index("core") == 0
    mine = [ref[:shard, :] for ref in piece_refs[:outer]]
    theirs = [ref[:shard, :] for ref in piece_refs[outer:]]
    for place in range(outer):
        offset = lax.axis_index("outer") ^ place
        own, other = mine[0], theirs[0]
        for delta in range(1, outer):
            own = jnp.where(offset == delta, mine[delta], own)
            other = jnp.where(offset == delta, theirs[delta], other)
        start = 2 * place * shard
        full_ref[start : start + shard, :] = jnp.where(first_core, own, other)
        full_ref[start + shard : start + 2 * shard, :] = jnp.where(first_core, other, own)
    flipped = full_ref[...].T

    def rows_of(table_ref):
        partial_ref[...] = matmul(table_ref[0, version], flipped, NN).astype(jnp.bfloat16)

    if n_tables == 1:
        rows_of(table_refs[0])
    else:
        pl.when(is_odd())(lambda: rows_of(table_refs[0]))
        pl.when(jnp.logical_not(is_odd()))(lambda: rows_of(table_refs[1]))


def project(shard, message, tables, mine, theirs):
    outer = len(mine)
    rows, width = tables[0].shape[2:]
    tokens = 2 * outer * shard
    return pl.pallas_call(
        functools.partial(project_kernel, outer, shard, len(tables)),
        out_shape=(
            jax.ShapeDtypeStruct((rows, tokens), jnp.bfloat16),
            jax.ShapeDtypeStruct((tokens, width), jnp.bfloat16),
        ),
        in_specs=[in_vmem()] * (1 + len(tables) + 2 * outer),
        out_specs=(in_vmem(), in_vmem()),
        compiler_params=pltpu.CompilerParams(vmem_limit_bytes=VMEM_BYTES),
        cost_estimate=SMALL,
        name="project",
    )(message, *tables, *mine, *theirs)


def mix_kernel(
    outer,
    odd_phase,
    message_ref,
    value_ref,
    mine_ref,
    arrived_ref,
    result_ref,
    keep_ref,
    send_ref,
):
    version = noted_version(message_ref)
    step = value_ref.shape[3] // CHUNKS
    tokens = mine_ref.shape[1]

    def heads(dims):
        for head in range(mine_ref.shape[0] // HEAD_DIM):
            rows = pl.ds(head * HEAD_DIM, HEAD_DIM)
            total = mine_ref[rows, :].astype(jnp.float32) + arrived_ref[rows, :].astype(jnp.float32)
            probs = message_ref[head * tokens : (head + 1) * tokens, :]
            mixed = matmul(total.astype(jnp.bfloat16), probs, dims)
            result_ref[rows, :] = mixed.astype(jnp.bfloat16)

    natural = is_odd() == odd_phase
    pl.when(natural)(lambda: heads(NN))
    pl.when(jnp.logical_not(natural))(lambda: heads(NT))

    flipped = result_ref[...].T
    second_core = lax.axis_index("core") == 1
    shard = tokens // (2 * outer)
    for chunk in range(CHUNKS):
        columns = pl.ds(chunk * step, step)
        partial = matmul(flipped, value_ref[0, version, :, columns], NN)
        for place in range(outer):
            low = partial[2 * place * shard : (2 * place + 1) * shard]
            high = partial[(2 * place + 1) * shard : (2 * place + 2) * shard]
            keep_ref[place, :, columns] = jnp.where(second_core, high, low).astype(jnp.bfloat16)
            send_ref[place, :, columns] = jnp.where(second_core, low, high).astype(jnp.bfloat16)


def mix(odd_phase, message, w_value, mine, arrived, outer):
    rows, width = w_value.shape[2:]
    tokens = mine.shape[1]
    half = jax.ShapeDtypeStruct((outer, tokens // (2 * outer), width), jnp.bfloat16)
    return pl.pallas_call(
        functools.partial(mix_kernel, outer, odd_phase),
        out_shape=(jax.ShapeDtypeStruct((rows, tokens), jnp.bfloat16), half, half),
        in_specs=[in_vmem()] * 4,
        out_specs=(in_vmem(), in_vmem(), in_vmem()),
        compiler_params=pltpu.CompilerParams(vmem_limit_bytes=VMEM_BYTES),
        cost_estimate=SMALL,
        name="mix",
    )(message, w_value, mine, arrived)


def combine_kernel(outer, last, keep_ref, arrived_ref, addend_ref, *refs):
    first_refs, sent_refs = refs[:-outer], refs[-outer:]
    for delta in range(outer):
        spot = lax.axis_index("outer") ^ delta
        total = keep_ref[spot].astype(jnp.float32) + arrived_ref[spot].astype(jnp.float32)
        if delta == 0:
            total = total + addend_ref[: total.shape[0], :].astype(jnp.float32)
        total = total.astype(jnp.bfloat16)
        if last:
            total = jnp.where(is_odd(), first_refs[delta][...], total)
        sent_refs[delta][...] = total


def combine(keep, arrived, addend, first_sent=()):
    outer, shard, width = keep.shape
    piece = jax.ShapeDtypeStruct((shard, width), jnp.bfloat16)
    return pl.pallas_call(
        functools.partial(combine_kernel, outer, len(first_sent) > 0),
        out_shape=(piece,) * outer,
        in_specs=[in_vmem()] * (3 + len(first_sent)),
        out_specs=(in_vmem(),) * outer,
        compiler_params=pltpu.CompilerParams(vmem_limit_bytes=VMEM_BYTES),
        cost_estimate=SMALL,
        name="combine",
    )(keep, arrived, addend, *first_sent)


def weight_grad_kernel(
    a0, a1, b0, b1, first0, first1, second0, second1, value_ref, out_ref
):
    odd = is_odd()
    left_first = jnp.concatenate([a0[...], a1[...]], axis=1)
    left_second = jnp.concatenate([b0[...], b1[...]], axis=1)
    right_second = jnp.concatenate([second0[...], second1[...]], axis=0)
    right_first = jnp.concatenate([first0[...], first1[...]], axis=0)
    grad_first = matmul(left_first, right_second, NN)
    grad_second = matmul(left_second, right_first, NN)
    value_ref[0] = jnp.where(odd, grad_first, grad_second).astype(jnp.bfloat16)
    out_ref[0] = jnp.where(odd, grad_second, grad_first).astype(jnp.bfloat16)


def weight_grads(first_results, second_results, first_full, second_full):
    rows, tokens = first_results[0].shape
    width = first_full[0].shape[1]
    step = rows // CHUNKS
    grad = jax.ShapeDtypeStruct((1, rows, width), jnp.bfloat16)
    left = pl.BlockSpec((step, tokens), lambda i: (i, 0))
    single = pl.BlockSpec((tokens, width), lambda i: (0, 0))
    wide = pl.BlockSpec((1, step, width), lambda i: (0, i, 0))
    return pl.pallas_call(
        weight_grad_kernel,
        grid=(CHUNKS,),
        out_shape=(grad, grad),
        in_specs=[left] * 4 + [single] * 4,
        out_specs=(wide, wide),
        compiler_params=pltpu.CompilerParams(vmem_limit_bytes=GRAD_VMEM_BYTES),
        cost_estimate=SMALL,
        name="weight_grads",
    )(*first_results, *second_results, *first_full, *second_full)


def load(source_ref, table_ref, sems):
    step = table_ref.shape[2] // CHUNKS
    copies = []
    for version in range(2):
        for chunk in range(CHUNKS):
            spot = (slice(None), version, pl.ds(chunk * step, step))
            copies.append(
                pltpu.make_async_copy(
                    source_ref.at[spot], table_ref.at[spot], sems.at[version * CHUNKS + chunk]
                )
            )
    return copies


def probs_kernel(stash_ref, probs_ref):
    tokens = stash_ref.shape[2]
    causal = lax.broadcasted_iota(jnp.int32, (tokens, tokens), 1) <= lax.broadcasted_iota(
        jnp.int32, (tokens, tokens), 0
    )
    for head in range(stash_ref.shape[1] // HEAD_DIM):
        rows = pl.ds(head * HEAD_DIM, HEAD_DIM)
        scores = matmul(stash_ref[0, rows, :], stash_ref[1, rows, :], TN)
        scores = jnp.where(causal, scores * (1.0 / math.sqrt(HEAD_DIM)), -jnp.inf)
        expo = jnp.exp(scores - jnp.max(scores, axis=1, keepdims=True))
        probs = (expo / jnp.sum(expo, axis=1, keepdims=True)).astype(jnp.bfloat16)
        probs_ref[head * tokens : (head + 1) * tokens, :] = probs


def attention_probs(stash):
    rows, tokens = stash.shape[1:]
    return pl.pallas_call(
        probs_kernel,
        out_shape=jax.ShapeDtypeStruct((rows // HEAD_DIM * tokens, tokens), jnp.bfloat16),
        in_specs=[in_vmem()],
        out_specs=in_vmem(),
        compiler_params=pltpu.CompilerParams(vmem_limit_bytes=VMEM_BYTES),
        cost_estimate=SMALL,
        name="probs",
    )(stash)


def load_kernel(source_ref, table_ref, sems):
    copies = load(source_ref, table_ref, sems)
    for copy in copies:
        copy.start()
    for copy in copies:
        copy.wait()


def load_first_kernel(value_ref, out_ref, table_ref, sems):
    def start(source_ref):
        for copy in load(source_ref, table_ref, sems):
            copy.start()

    pl.when(is_odd())(lambda: start(out_ref))
    pl.when(jnp.logical_not(is_odd()))(lambda: start(value_ref))
    for copy in load(value_ref, table_ref, sems):
        copy.wait()


def load_first(w_value, w_out):
    return pl.pallas_call(
        load_first_kernel,
        out_shape=jax.ShapeDtypeStruct(w_value.shape, jnp.bfloat16),
        in_specs=[in_hbm(), in_hbm()],
        out_specs=in_vmem(),
        scratch_shapes=[pltpu.SemaphoreType.DMA((2 * CHUNKS,))],
        compiler_params=pltpu.CompilerParams(vmem_limit_bytes=FIRST_VMEM_BYTES),
        cost_estimate=SMALL,
        name="load_first",
    )(w_value, w_out)


def load_table(table, grant):
    return pl.pallas_call(
        load_kernel,
        out_shape=jax.ShapeDtypeStruct(table.shape, jnp.bfloat16),
        in_specs=[in_hbm()],
        out_specs=in_vmem(),
        scratch_shapes=[pltpu.SemaphoreType.DMA((2 * CHUNKS,))],
        compiler_params=pltpu.CompilerParams(vmem_limit_bytes=grant),
        cost_estimate=SMALL,
        name="load_table",
    )(table)


def on_device(section_input, query, key_stash, incoming, version, w_value, w_out):
    half = lax.axis_index("half")
    odd = is_odd()
    n_pairs = lax.axis_size("pair")
    outer = lax.axis_size("outer")
    n_tensor = 2 * outer
    width = w_value.shape[3]
    shard = section_input.shape[1]

    def swap_half(array):
        return lax.ppermute(array, "half", [(0, 1), (1, 0)])

    def swap_core(array):
        return lax.ppermute(array, "core", [(0, 1), (1, 0)])

    def to_row(array, delta):
        return lax.ppermute(array, "outer", [(i, i ^ delta) for i in range(outer)])

    def to_other_half(array, delta):
        pairs = [
            (h * n_tensor + i, (1 - h) * n_tensor + (i ^ (2 * delta)))
            for h in range(2)
            for i in range(n_tensor)
        ]
        return lax.ppermute(array, ("half", "outer", "core"), pairs)

    def swap_section(array, delta):
        pairs = [
            (p * n_tensor + i, (p ^ 1) * n_tensor + (i ^ (2 * delta)))
            for p in range(n_pairs)
            for i in range(n_tensor)
        ]
        return lax.ppermute(array, ("pair", "outer", "core"), pairs)

    def own_columns(array):
        return lax.dynamic_slice_in_dim(array, half * width, width, 1)

    def other_columns(array):
        return lax.dynamic_slice_in_dim(array, (1 - half) * width, width, 1)

    def total(parts):
        value = parts[0].astype(jnp.float32)
        for part in parts[1:]:
            value = value + part.astype(jnp.float32)
        return value

    def spread_rows(piece):
        return [piece] + [to_row(piece, delta) for delta in range(1, outer)]

    first = jnp.where(odd, incoming[0], section_input[0])
    own_piece, sent_piece = own_columns(first), other_columns(first)
    other_piece = swap_half(sent_piece)
    first_piece = [own_piece, other_piece]
    later_own, _ = lax.optimization_barrier((own_piece, other_piece))
    first_mine = [spread_rows(later_own), spread_rows(other_piece)]
    own_probs = attention_probs(jnp.concatenate([query, key_stash]))
    note = jnp.full((NOTE_ROWS, LANES), version[0], jnp.int32).astype(jnp.bfloat16)
    own_probs = jnp.concatenate([own_probs, note])
    other_probs = swap_half(own_probs)
    late_value, late_out, _ = lax.optimization_barrier((w_value, w_out, own_probs))
    first_table = load_first(late_value, late_out)
    first_theirs = []
    for pieces in first_mine:
        later, _ = lax.optimization_barrier((pieces, first_table))
        first_theirs.append([swap_core(piece) for piece in later])

    probs = [own_probs, other_probs]
    partial, first_full = [None, None], [None, None]
    for m in (1, 0):
        mine = first_mine[m]
        if m == 0:
            mine, probs, _ = lax.optimization_barrier((mine, probs, partial[1]))
        partial[m], first_full[m] = project(
            shard, probs[m], (first_table,), mine, first_theirs[m]
        )
    arrived = [swap_half(partial[1]), swap_half(partial[0])]
    later_value, _ = lax.optimization_barrier((w_value, partial))
    value_table = load_table(later_value, VALUE_VMEM_BYTES)
    first_result, first_sent = [None, None], [None, None]
    second_piece, second_full = [None, None], [None, None]
    for m in range(2):
        first_result[m], keep, send = mix(
            True, probs[m], value_table, partial[m], arrived[m], outer
        )
        first_sent[m] = combine(keep, swap_core(send), first_piece[m])
    later_out, _ = lax.optimization_barrier((w_out, first_sent))
    out_table = load_table(later_out, OUT_VMEM_BYTES)
    later_input, _ = lax.optimization_barrier((section_input[0], out_table))
    input_own, input_sent = lax.optimization_barrier(
        (own_columns(later_input), other_columns(later_input))
    )
    input_piece = [input_own, swap_half(input_sent)]
    for m in range(2):
        received = [swap_section(part, d) for d, part in enumerate(first_sent[m])]
        second_piece[m] = jnp.where(odd, input_piece[m], total(received).astype(jnp.bfloat16))
    for m in range(2):
        mine = spread_rows(second_piece[m])
        theirs = [swap_core(piece) for piece in mine]
        partial[m], second_full[m] = project(
            shard, probs[m], (value_table, out_table), mine, theirs
        )
    arrived = [swap_half(partial[1]), swap_half(partial[0])]
    second_result, last_sent = [None, None], [None, None]
    for m in (1, 0):
        second_result[m], keep, send = mix(
            False, probs[m], value_table, partial[m], arrived[m], outer
        )
        if m == 0:
            keep, _ = lax.optimization_barrier((keep, last_sent[1]))
        last_sent[m] = combine(keep, swap_core(send), second_piece[m], first_sent[m])
    other_parts = [to_other_half(part, d) for d, part in enumerate(last_sent[1])]
    own_parts = [last_sent[0][0]] + [to_row(part, d + 1) for d, part in enumerate(last_sent[0][1:])]
    second_result, _ = lax.optimization_barrier((second_result, last_sent))
    grad_value, grad_out = weight_grads(
        first_result, second_result, first_full, second_full
    )
    own_parts, other_parts, _ = lax.optimization_barrier((own_parts, other_parts, grad_value))
    own_grad = total(own_parts).astype(jnp.bfloat16)
    other_grad = total(other_parts).astype(jnp.bfloat16)
    input_grad = jnp.concatenate(
        [jnp.where(half == 0, own_grad, other_grad), jnp.where(half == 0, other_grad, own_grad)],
        axis=1,
    )
    return (input_grad[None], grad_value, grad_out)


def solution(mesh):
    sections, tensor = mesh.devices.shape
    split = Mesh(
        mesh.devices.reshape(sections // 2, 2, tensor // 2, 2), ("pair", "half", "outer", "core")
    )
    slots, places = ("pair", "half"), ("outer", "core")
    by_tokens = P(slots, places, None)
    by_rows = P(slots, None, places, None)
    return jax.shard_map(
        on_device,
        mesh=split,
        in_specs=(by_tokens, by_tokens, by_tokens, by_tokens, P(slots), by_rows, by_rows),
        out_specs=(by_tokens, by_tokens, by_tokens),
        check_vma=False,
    )
```

```python
import functools
import math

import jax
import jax.numpy as jnp
from jax import lax
from jax.experimental import pallas as pl
from jax.experimental.pallas import tpu as pltpu
from jax.sharding import Mesh, PartitionSpec as P

HEAD_DIM = 96
CHUNKS = 4
VMEM_BYTES = 8 * 2**20
GRAD_VMEM_BYTES = 16 * 2**20
FIRST_VMEM_BYTES = 46 * 2**20
VALUE_VMEM_BYTES = 47 * 2**20
OUT_VMEM_BYTES = 42 * 2**20
LANES = 128
NOTE_ROWS = 16
SMALL = pl.CostEstimate(flops=1, bytes_accessed=1, transcendentals=0)
NN = (((1,), (0,)), ((), ()))
NT = (((1,), (1,)), ((), ()))
TN = (((0,), (0,)), ((), ()))


def matmul(left_side, right_side, dims):
    return lax.dot_general(left_side, right_side, dims, preferred_element_type=jnp.float32)


def in_vmem():
    return pl.BlockSpec(memory_space=pltpu.VMEM)


def in_hbm():
    return pl.BlockSpec(memory_space=pltpu.HBM)


def in_place():
    return pl.BlockSpec(memory_space=pl.ANY)


def is_odd():
    return (lax.axis_index("pair") & 1) == 1


def noted_version(message_ref):
    note = message_ref[message_ref.shape[0] - NOTE_ROWS :, :]
    return (jnp.max(note.astype(jnp.float32)) > 0.5).astype(jnp.int32)


def project_kernel(outer, shard, n_tables, message_ref, *refs):
    table_refs, piece_refs = refs[:n_tables], refs[n_tables:-2]
    partial_ref, full_ref = refs[-2:]
    version = noted_version(message_ref)
    first_core = lax.axis_index("core") == 0
    mine = [ref[:shard, :] for ref in piece_refs[:outer]]
    theirs = [ref[:shard, :] for ref in piece_refs[outer:]]
    for place in range(outer):
        offset = lax.axis_index("outer") ^ place
        own, other = mine[0], theirs[0]
        for delta in range(1, outer):
            own = jnp.where(offset == delta, mine[delta], own)
            other = jnp.where(offset == delta, theirs[delta], other)
        start = 2 * place * shard
        full_ref[start : start + shard, :] = jnp.where(first_core, own, other)
        full_ref[start + shard : start + 2 * shard, :] = jnp.where(first_core, other, own)
    flipped = full_ref[...].T

    def rows_of(table_ref):
        partial_ref[...] = matmul(table_ref[0, version], flipped, NN).astype(jnp.bfloat16)

    if n_tables == 1:
        rows_of(table_refs[0])
    else:
        pl.when(is_odd())(lambda: rows_of(table_refs[0]))
        pl.when(jnp.logical_not(is_odd()))(lambda: rows_of(table_refs[1]))


def project(shard, message, tables, mine, theirs):
    outer = len(mine)
    rows, width = tables[0].shape[2:]
    tokens = 2 * outer * shard
    return pl.pallas_call(
        functools.partial(project_kernel, outer, shard, len(tables)),
        out_shape=(
            jax.ShapeDtypeStruct((rows, tokens), jnp.bfloat16),
            jax.ShapeDtypeStruct((tokens, width), jnp.bfloat16),
        ),
        in_specs=[in_vmem()] * (1 + len(tables) + 2 * outer),
        out_specs=(in_vmem(), in_vmem()),
        compiler_params=pltpu.CompilerParams(vmem_limit_bytes=VMEM_BYTES),
        cost_estimate=SMALL,
        name="project",
    )(message, *tables, *mine, *theirs)


def mix_kernel(
    outer,
    odd_phase,
    message_ref,
    value_ref,
    mine_ref,
    arrived_ref,
    result_ref,
    keep_ref,
    send_ref,
):
    version = noted_version(message_ref)
    step = value_ref.shape[3] // CHUNKS
    tokens = mine_ref.shape[1]

    def heads(dims):
        for head in range(mine_ref.shape[0] // HEAD_DIM):
            rows = pl.ds(head * HEAD_DIM, HEAD_DIM)
            total = mine_ref[rows, :].astype(jnp.float32) + arrived_ref[rows, :].astype(jnp.float32)
            probs = message_ref[head * tokens : (head + 1) * tokens, :]
            mixed = matmul(total.astype(jnp.bfloat16), probs, dims)
            result_ref[rows, :] = mixed.astype(jnp.bfloat16)

    natural = is_odd() == odd_phase
    pl.when(natural)(lambda: heads(NN))
    pl.when(jnp.logical_not(natural))(lambda: heads(NT))

    flipped = result_ref[...].T
    second_core = lax.axis_index("core") == 1
    shard = tokens // (2 * outer)
    for chunk in range(CHUNKS):
        columns = pl.ds(chunk * step, step)
        partial = matmul(flipped, value_ref[0, version, :, columns], NN)
        for place in range(outer):
            low = partial[2 * place * shard : (2 * place + 1) * shard]
            high = partial[(2 * place + 1) * shard : (2 * place + 2) * shard]
            keep_ref[place, :, columns] = jnp.where(second_core, high, low).astype(jnp.bfloat16)
            send_ref[place, :, columns] = jnp.where(second_core, low, high).astype(jnp.bfloat16)


def mix(odd_phase, message, w_value, mine, arrived, outer):
    rows, width = w_value.shape[2:]
    tokens = mine.shape[1]
    half = jax.ShapeDtypeStruct((outer, tokens // (2 * outer), width), jnp.bfloat16)
    return pl.pallas_call(
        functools.partial(mix_kernel, outer, odd_phase),
        out_shape=(jax.ShapeDtypeStruct((rows, tokens), jnp.bfloat16), half, half),
        in_specs=[in_vmem()] * 4,
        out_specs=(in_vmem(), in_vmem(), in_vmem()),
        compiler_params=pltpu.CompilerParams(vmem_limit_bytes=VMEM_BYTES),
        cost_estimate=SMALL,
        name="mix",
    )(message, w_value, mine, arrived)


def combine_kernel(outer, last, keep_ref, arrived_ref, addend_ref, *refs):
    first_refs, sent_refs = refs[:-outer], refs[-outer:]
    for delta in range(outer):
        spot = lax.axis_index("outer") ^ delta
        total = keep_ref[spot].astype(jnp.float32) + arrived_ref[spot].astype(jnp.float32)
        if delta == 0:
            total = total + addend_ref[: total.shape[0], :].astype(jnp.float32)
        total = total.astype(jnp.bfloat16)
        if last:
            total = jnp.where(is_odd(), first_refs[delta][...], total)
        sent_refs[delta][...] = total


def combine(keep, arrived, addend, first_sent=()):
    outer, shard, width = keep.shape
    piece = jax.ShapeDtypeStruct((shard, width), jnp.bfloat16)
    return pl.pallas_call(
        functools.partial(combine_kernel, outer, len(first_sent) > 0),
        out_shape=(piece,) * outer,
        in_specs=[in_vmem()] * (3 + len(first_sent)),
        out_specs=(in_vmem(),) * outer,
        compiler_params=pltpu.CompilerParams(vmem_limit_bytes=VMEM_BYTES),
        cost_estimate=SMALL,
        name="combine",
    )(keep, arrived, addend, *first_sent)


def weight_grad_kernel(
    a0, a1, b0, b1, first0, first1, second0, second1, value_ref, out_ref
):
    odd = is_odd()
    left_first = jnp.concatenate([a0[...], a1[...]], axis=1)
    left_second = jnp.concatenate([b0[...], b1[...]], axis=1)
    right_second = jnp.concatenate([second0[...], second1[...]], axis=0)
    right_first = jnp.concatenate([first0[...], first1[...]], axis=0)
    grad_first = matmul(left_first, right_second, NN)
    grad_second = matmul(left_second, right_first, NN)
    value_ref[0] = jnp.where(odd, grad_first, grad_second).astype(jnp.bfloat16)
    out_ref[0] = jnp.where(odd, grad_second, grad_first).astype(jnp.bfloat16)


def weight_grads(first_results, second_results, first_full, second_full):
    rows, tokens = first_results[0].shape
    width = first_full[0].shape[1]
    step = rows // CHUNKS
    grad = jax.ShapeDtypeStruct((1, rows, width), jnp.bfloat16)
    left = pl.BlockSpec((step, tokens), lambda i: (i, 0))
    single = pl.BlockSpec((tokens, width), lambda i: (0, 0))
    wide = pl.BlockSpec((1, step, width), lambda i: (0, i, 0))
    return pl.pallas_call(
        weight_grad_kernel,
        grid=(CHUNKS,),
        out_shape=(grad, grad),
        in_specs=[left] * 4 + [single] * 4,
        out_specs=(wide, wide),
        compiler_params=pltpu.CompilerParams(vmem_limit_bytes=GRAD_VMEM_BYTES),
        cost_estimate=SMALL,
        name="weight_grads",
    )(*first_results, *second_results, *first_full, *second_full)


def load(source_ref, table_ref, sems):
    step = table_ref.shape[2] // CHUNKS
    copies = []
    for version in range(2):
        for chunk in range(CHUNKS):
            spot = (slice(None), version, pl.ds(chunk * step, step))
            copies.append(
                pltpu.make_async_copy(
                    source_ref.at[spot], table_ref.at[spot], sems.at[version * CHUNKS + chunk]
                )
            )
    return copies


def probs_kernel(stash_ref, probs_ref):
    tokens = stash_ref.shape[2]
    causal = lax.broadcasted_iota(jnp.int32, (tokens, tokens), 1) <= lax.broadcasted_iota(
        jnp.int32, (tokens, tokens), 0
    )
    for head in range(stash_ref.shape[1] // HEAD_DIM):
        rows = pl.ds(head * HEAD_DIM, HEAD_DIM)
        scores = matmul(stash_ref[0, rows, :], stash_ref[1, rows, :], TN)
        scores = jnp.where(causal, scores * (1.0 / math.sqrt(HEAD_DIM)), -jnp.inf)
        expo = jnp.exp(scores - jnp.max(scores, axis=1, keepdims=True))
        probs = (expo / jnp.sum(expo, axis=1, keepdims=True)).astype(jnp.bfloat16)
        probs_ref[head * tokens : (head + 1) * tokens, :] = probs


def attention_probs(stash):
    rows, tokens = stash.shape[1:]
    return pl.pallas_call(
        probs_kernel,
        out_shape=jax.ShapeDtypeStruct((rows // HEAD_DIM * tokens, tokens), jnp.bfloat16),
        in_specs=[in_vmem()],
        out_specs=in_vmem(),
        compiler_params=pltpu.CompilerParams(vmem_limit_bytes=VMEM_BYTES),
        cost_estimate=SMALL,
        name="probs",
    )(stash)


def load_kernel(source_ref, table_ref, sems):
    copies = load(source_ref, table_ref, sems)
    for copy in copies:
        copy.start()
    for copy in copies:
        copy.wait()


def load_first_kernel(value_ref, out_ref, table_ref, sems):
    def start(source_ref):
        for copy in load(source_ref, table_ref, sems):
            copy.start()

    pl.when(is_odd())(lambda: start(out_ref))
    pl.when(jnp.logical_not(is_odd()))(lambda: start(value_ref))
    for copy in load(value_ref, table_ref, sems):
        copy.wait()


def load_first(w_value, w_out):
    return pl.pallas_call(
        load_first_kernel,
        out_shape=jax.ShapeDtypeStruct(w_value.shape, jnp.bfloat16),
        in_specs=[in_hbm(), in_hbm()],
        out_specs=in_vmem(),
        scratch_shapes=[pltpu.SemaphoreType.DMA((2 * CHUNKS,))],
        compiler_params=pltpu.CompilerParams(vmem_limit_bytes=FIRST_VMEM_BYTES),
        cost_estimate=SMALL,
        name="load_first",
    )(w_value, w_out)


def load_table(table, grant):
    return pl.pallas_call(
        load_kernel,
        out_shape=jax.ShapeDtypeStruct(table.shape, jnp.bfloat16),
        in_specs=[in_hbm()],
        out_specs=in_vmem(),
        scratch_shapes=[pltpu.SemaphoreType.DMA((2 * CHUNKS,))],
        compiler_params=pltpu.CompilerParams(vmem_limit_bytes=grant),
        cost_estimate=SMALL,
        name="load_table",
    )(table)


def on_device(section_input, query, key_stash, incoming, version, w_value, w_out):
    half = lax.axis_index("half")
    odd = is_odd()
    n_pairs = lax.axis_size("pair")
    outer = lax.axis_size("outer")
    n_tensor = 2 * outer
    width = w_value.shape[3]
    shard = section_input.shape[1]

    def swap_half(array):
        return lax.ppermute(array, "half", [(0, 1), (1, 0)])

    def swap_core(array):
        return lax.ppermute(array, "core", [(0, 1), (1, 0)])

    def to_row(array, delta):
        return lax.ppermute(array, "outer", [(i, i ^ delta) for i in range(outer)])

    def to_other_half(array, delta):
        pairs = [
            (h * n_tensor + i, (1 - h) * n_tensor + (i ^ (2 * delta)))
            for h in range(2)
            for i in range(n_tensor)
        ]
        return lax.ppermute(array, ("half", "outer", "core"), pairs)

    def swap_section(array, delta):
        pairs = [
            (p * n_tensor + i, (p ^ 1) * n_tensor + (i ^ (2 * delta)))
            for p in range(n_pairs)
            for i in range(n_tensor)
        ]
        return lax.ppermute(array, ("pair", "outer", "core"), pairs)

    def own_columns(array):
        return lax.dynamic_slice_in_dim(array, half * width, width, 1)

    def other_columns(array):
        return lax.dynamic_slice_in_dim(array, (1 - half) * width, width, 1)

    def total(parts):
        value = parts[0].astype(jnp.float32)
        for part in parts[1:]:
            value = value + part.astype(jnp.float32)
        return value

    def spread_rows(piece):
        return [piece] + [to_row(piece, delta) for delta in range(1, outer)]

    first = jnp.where(odd, incoming[0], section_input[0])
    own_piece, sent_piece = own_columns(first), other_columns(first)
    other_piece = swap_half(sent_piece)
    first_piece = [own_piece, other_piece]
    later_own, _ = lax.optimization_barrier((own_piece, other_piece))
    first_mine = [spread_rows(later_own), spread_rows(other_piece)]
    own_probs = attention_probs(jnp.concatenate([query, key_stash]))
    note = jnp.full((NOTE_ROWS, LANES), version[0], jnp.int32).astype(jnp.bfloat16)
    own_probs = jnp.concatenate([own_probs, note])
    other_probs = swap_half(own_probs)
    late_value, late_out, _ = lax.optimization_barrier((w_value, w_out, own_probs))
    first_table = load_first(late_value, late_out)
    first_theirs = []
    for pieces in first_mine:
        later, _ = lax.optimization_barrier((pieces, first_table))
        first_theirs.append([swap_core(piece) for piece in later])

    probs = [own_probs, other_probs]
    partial, first_full = [None, None], [None, None]
    for m in (1, 0):
        mine = first_mine[m]
        if m == 0:
            mine, probs, _ = lax.optimization_barrier((mine, probs, partial[1]))
        partial[m], first_full[m] = project(
            shard, probs[m], (first_table,), mine, first_theirs[m]
        )
    arrived = [swap_half(partial[1]), swap_half(partial[0])]
    later_value, _ = lax.optimization_barrier((w_value, partial))
    value_table = load_table(later_value, VALUE_VMEM_BYTES)
    first_result, first_sent = [None, None], [None, None]
    second_piece, second_full = [None, None], [None, None]
    for m in range(2):
        first_result[m], keep, send = mix(
            True, probs[m], value_table, partial[m], arrived[m], outer
        )
        first_sent[m] = combine(keep, swap_core(send), first_piece[m])
    later_out, _ = lax.optimization_barrier((w_out, first_sent))
    out_table = load_table(later_out, OUT_VMEM_BYTES)
    later_input, _ = lax.optimization_barrier((section_input[0], out_table))
    input_own, input_sent = lax.optimization_barrier(
        (own_columns(later_input), other_columns(later_input))
    )
    input_piece = [input_own, swap_half(input_sent)]
    for m in range(2):
        received = [swap_section(part, d) for d, part in enumerate(first_sent[m])]
        second_piece[m] = jnp.where(odd, input_piece[m], total(received).astype(jnp.bfloat16))
    for m in range(2):
        mine = spread_rows(second_piece[m])
        theirs = [swap_core(piece) for piece in mine]
        partial[m], second_full[m] = project(
            shard, probs[m], (value_table, out_table), mine, theirs
        )
    arrived = [swap_half(partial[1]), swap_half(partial[0])]
    second_result, last_sent = [None, None], [None, None]
    for m in (1, 0):
        second_result[m], keep, send = mix(
            False, probs[m], value_table, partial[m], arrived[m], outer
        )
        if m == 0:
            keep, _ = lax.optimization_barrier((keep, last_sent[1]))
        last_sent[m] = combine(keep, swap_core(send), second_piece[m], first_sent[m])
    other_parts = [to_other_half(part, d) for d, part in enumerate(last_sent[1])]
    own_parts = [last_sent[0][0]] + [to_row(part, d + 1) for d, part in enumerate(last_sent[0][1:])]
    second_result, _ = lax.optimization_barrier((second_result, last_sent))
    grad_value, grad_out = weight_grads(
        first_result, second_result, first_full, second_full
    )
    other_grad = lax.optimization_barrier(total(other_parts).astype(jnp.bfloat16))
    own_parts, _ = lax.optimization_barrier((own_parts, grad_value))
    own_grad = total(own_parts).astype(jnp.bfloat16)
    input_grad = jnp.concatenate(
        [jnp.where(half == 0, own_grad, other_grad), jnp.where(half == 0, other_grad, own_grad)],
        axis=1,
    )
    return (input_grad[None], grad_value, grad_out)


def solution(mesh):
    sections, tensor = mesh.devices.shape
    split = Mesh(
        mesh.devices.reshape(sections // 2, 2, tensor // 2, 2), ("pair", "half", "outer", "core")
    )
    slots, places = ("pair", "half"), ("outer", "core")
    by_tokens = P(slots, places, None)
    by_rows = P(slots, None, places, None)
    return jax.shard_map(
        on_device,
        mesh=split,
        in_specs=(by_tokens, by_tokens, by_tokens, by_tokens, P(slots), by_rows, by_rows),
        out_specs=(by_tokens, by_tokens, by_tokens),
        check_vma=False,
    )
```

```python
import functools
import math

import jax
import jax.numpy as jnp
from jax import lax
from jax.experimental import pallas as pl
from jax.experimental.pallas import tpu as pltpu
from jax.sharding import Mesh, PartitionSpec as P

HEAD_DIM = 96
CHUNKS = 4
VMEM_BYTES = 8 * 2**20
GRAD_VMEM_BYTES = 16 * 2**20
FIRST_VMEM_BYTES = 46 * 2**20
VALUE_VMEM_BYTES = 47 * 2**20
OUT_VMEM_BYTES = 42 * 2**20
LANES = 128
NOTE_ROWS = 16
SMALL = pl.CostEstimate(flops=1, bytes_accessed=1, transcendentals=0)
NN = (((1,), (0,)), ((), ()))
NT = (((1,), (1,)), ((), ()))
TN = (((0,), (0,)), ((), ()))


def matmul(left_side, right_side, dims):
    return lax.dot_general(left_side, right_side, dims, preferred_element_type=jnp.float32)


def in_vmem():
    return pl.BlockSpec(memory_space=pltpu.VMEM)


def in_hbm():
    return pl.BlockSpec(memory_space=pltpu.HBM)


def in_place():
    return pl.BlockSpec(memory_space=pl.ANY)


def is_odd():
    return (lax.axis_index("pair") & 1) == 1


def noted_version(message_ref):
    note = message_ref[message_ref.shape[0] - NOTE_ROWS :, :]
    return (jnp.max(note.astype(jnp.float32)) > 0.5).astype(jnp.int32)


def project_kernel(outer, shard, n_tables, message_ref, *refs):
    table_refs, piece_refs = refs[:n_tables], refs[n_tables:-2]
    partial_ref, full_ref = refs[-2:]
    version = noted_version(message_ref)
    first_core = lax.axis_index("core") == 0
    mine = [ref[:shard, :] for ref in piece_refs[:outer]]
    theirs = [ref[:shard, :] for ref in piece_refs[outer:]]
    for place in range(outer):
        offset = lax.axis_index("outer") ^ place
        own, other = mine[0], theirs[0]
        for delta in range(1, outer):
            own = jnp.where(offset == delta, mine[delta], own)
            other = jnp.where(offset == delta, theirs[delta], other)
        start = 2 * place * shard
        full_ref[start : start + shard, :] = jnp.where(first_core, own, other)
        full_ref[start + shard : start + 2 * shard, :] = jnp.where(first_core, other, own)
    flipped = full_ref[...].T

    def rows_of(table_ref):
        partial_ref[...] = matmul(table_ref[0, version], flipped, NN).astype(jnp.bfloat16)

    if n_tables == 1:
        rows_of(table_refs[0])
    else:
        pl.when(is_odd())(lambda: rows_of(table_refs[0]))
        pl.when(jnp.logical_not(is_odd()))(lambda: rows_of(table_refs[1]))


def project(shard, message, tables, mine, theirs):
    outer = len(mine)
    rows, width = tables[0].shape[2:]
    tokens = 2 * outer * shard
    return pl.pallas_call(
        functools.partial(project_kernel, outer, shard, len(tables)),
        out_shape=(
            jax.ShapeDtypeStruct((rows, tokens), jnp.bfloat16),
            jax.ShapeDtypeStruct((tokens, width), jnp.bfloat16),
        ),
        in_specs=[in_vmem()] * (1 + len(tables) + 2 * outer),
        out_specs=(in_vmem(), in_vmem()),
        compiler_params=pltpu.CompilerParams(vmem_limit_bytes=VMEM_BYTES),
        cost_estimate=SMALL,
        name="project",
    )(message, *tables, *mine, *theirs)


def mix_kernel(
    outer,
    odd_phase,
    message_ref,
    value_ref,
    mine_ref,
    arrived_ref,
    result_ref,
    keep_ref,
    send_ref,
):
    version = noted_version(message_ref)
    step = value_ref.shape[3] // CHUNKS
    tokens = mine_ref.shape[1]

    def heads(dims):
        for head in range(mine_ref.shape[0] // HEAD_DIM):
            rows = pl.ds(head * HEAD_DIM, HEAD_DIM)
            total = mine_ref[rows, :].astype(jnp.float32) + arrived_ref[rows, :].astype(jnp.float32)
            probs = message_ref[head * tokens : (head + 1) * tokens, :]
            mixed = matmul(total.astype(jnp.bfloat16), probs, dims)
            result_ref[rows, :] = mixed.astype(jnp.bfloat16)

    natural = is_odd() == odd_phase
    pl.when(natural)(lambda: heads(NN))
    pl.when(jnp.logical_not(natural))(lambda: heads(NT))

    flipped = result_ref[...].T
    second_core = lax.axis_index("core") == 1
    shard = tokens // (2 * outer)
    for chunk in range(CHUNKS):
        columns = pl.ds(chunk * step, step)
        partial = matmul(flipped, value_ref[0, version, :, columns], NN)
        for place in range(outer):
            low = partial[2 * place * shard : (2 * place + 1) * shard]
            high = partial[(2 * place + 1) * shard : (2 * place + 2) * shard]
            keep_ref[place, :, columns] = jnp.where(second_core, high, low).astype(jnp.bfloat16)
            send_ref[place, :, columns] = jnp.where(second_core, low, high).astype(jnp.bfloat16)


def mix(odd_phase, message, w_value, mine, arrived, outer):
    rows, width = w_value.shape[2:]
    tokens = mine.shape[1]
    half = jax.ShapeDtypeStruct((outer, tokens // (2 * outer), width), jnp.bfloat16)
    return pl.pallas_call(
        functools.partial(mix_kernel, outer, odd_phase),
        out_shape=(jax.ShapeDtypeStruct((rows, tokens), jnp.bfloat16), half, half),
        in_specs=[in_vmem()] * 4,
        out_specs=(in_vmem(), in_vmem(), in_vmem()),
        compiler_params=pltpu.CompilerParams(vmem_limit_bytes=VMEM_BYTES),
        cost_estimate=SMALL,
        name="mix",
    )(message, w_value, mine, arrived)


def combine_kernel(outer, last, keep_ref, arrived_ref, addend_ref, *refs):
    first_refs, sent_refs = refs[:-outer], refs[-outer:]
    for delta in range(outer):
        spot = lax.axis_index("outer") ^ delta
        total = keep_ref[spot].astype(jnp.float32) + arrived_ref[spot].astype(jnp.float32)
        if delta == 0:
            total = total + addend_ref[: total.shape[0], :].astype(jnp.float32)
        total = total.astype(jnp.bfloat16)
        if last:
            total = jnp.where(is_odd(), first_refs[delta][...], total)
        sent_refs[delta][...] = total


def combine(keep, arrived, addend, first_sent=()):
    outer, shard, width = keep.shape
    piece = jax.ShapeDtypeStruct((shard, width), jnp.bfloat16)
    return pl.pallas_call(
        functools.partial(combine_kernel, outer, len(first_sent) > 0),
        out_shape=(piece,) * outer,
        in_specs=[in_vmem()] * (3 + len(first_sent)),
        out_specs=(in_vmem(),) * outer,
        compiler_params=pltpu.CompilerParams(vmem_limit_bytes=VMEM_BYTES),
        cost_estimate=SMALL,
        name="combine",
    )(keep, arrived, addend, *first_sent)


def weight_grad_kernel(
    a0, a1, b0, b1, first0, first1, second0, second1, value_ref, out_ref
):
    odd = is_odd()
    left_first = jnp.concatenate([a0[...], a1[...]], axis=1)
    left_second = jnp.concatenate([b0[...], b1[...]], axis=1)
    right_second = jnp.concatenate([second0[...], second1[...]], axis=0)
    right_first = jnp.concatenate([first0[...], first1[...]], axis=0)
    grad_first = matmul(left_first, right_second, NN)
    grad_second = matmul(left_second, right_first, NN)
    value_ref[0] = jnp.where(odd, grad_first, grad_second).astype(jnp.bfloat16)
    out_ref[0] = jnp.where(odd, grad_second, grad_first).astype(jnp.bfloat16)


def weight_grads(first_results, second_results, first_full, second_full):
    rows, tokens = first_results[0].shape
    width = first_full[0].shape[1]
    step = rows // CHUNKS
    grad = jax.ShapeDtypeStruct((1, rows, width), jnp.bfloat16)
    left = pl.BlockSpec((step, tokens), lambda i: (i, 0))
    single = pl.BlockSpec((tokens, width), lambda i: (0, 0))
    wide = pl.BlockSpec((1, step, width), lambda i: (0, i, 0))
    return pl.pallas_call(
        weight_grad_kernel,
        grid=(CHUNKS,),
        out_shape=(grad, grad),
        in_specs=[left] * 4 + [single] * 4,
        out_specs=(wide, wide),
        compiler_params=pltpu.CompilerParams(vmem_limit_bytes=GRAD_VMEM_BYTES),
        cost_estimate=SMALL,
        name="weight_grads",
    )(*first_results, *second_results, *first_full, *second_full)


def load(source_ref, table_ref, sems):
    step = table_ref.shape[2] // CHUNKS
    copies = []
    for version in range(2):
        for chunk in range(CHUNKS):
            spot = (slice(None), version, pl.ds(chunk * step, step))
            copies.append(
                pltpu.make_async_copy(
                    source_ref.at[spot], table_ref.at[spot], sems.at[version * CHUNKS + chunk]
                )
            )
    return copies


def probs_kernel(stash_ref, probs_ref):
    tokens = stash_ref.shape[2]
    causal = lax.broadcasted_iota(jnp.int32, (tokens, tokens), 1) <= lax.broadcasted_iota(
        jnp.int32, (tokens, tokens), 0
    )
    for head in range(stash_ref.shape[1] // HEAD_DIM):
        rows = pl.ds(head * HEAD_DIM, HEAD_DIM)
        scores = matmul(stash_ref[0, rows, :], stash_ref[1, rows, :], TN)
        scores = jnp.where(causal, scores * (1.0 / math.sqrt(HEAD_DIM)), -jnp.inf)
        expo = jnp.exp(scores - jnp.max(scores, axis=1, keepdims=True))
        probs = (expo / jnp.sum(expo, axis=1, keepdims=True)).astype(jnp.bfloat16)
        probs_ref[head * tokens : (head + 1) * tokens, :] = probs


def attention_probs(stash):
    rows, tokens = stash.shape[1:]
    return pl.pallas_call(
        probs_kernel,
        out_shape=jax.ShapeDtypeStruct((rows // HEAD_DIM * tokens, tokens), jnp.bfloat16),
        in_specs=[in_vmem()],
        out_specs=in_vmem(),
        compiler_params=pltpu.CompilerParams(vmem_limit_bytes=VMEM_BYTES),
        cost_estimate=SMALL,
        name="probs",
    )(stash)


def load_kernel(source_ref, table_ref, sems):
    copies = load(source_ref, table_ref, sems)
    for copy in copies:
        copy.start()
    for copy in copies:
        copy.wait()


def load_first_kernel(value_ref, out_ref, table_ref, sems):
    def start(source_ref):
        for copy in load(source_ref, table_ref, sems):
            copy.start()

    pl.when(is_odd())(lambda: start(out_ref))
    pl.when(jnp.logical_not(is_odd()))(lambda: start(value_ref))
    for copy in load(value_ref, table_ref, sems):
        copy.wait()


def load_first(w_value, w_out):
    return pl.pallas_call(
        load_first_kernel,
        out_shape=jax.ShapeDtypeStruct(w_value.shape, jnp.bfloat16),
        in_specs=[in_hbm(), in_hbm()],
        out_specs=in_vmem(),
        scratch_shapes=[pltpu.SemaphoreType.DMA((2 * CHUNKS,))],
        compiler_params=pltpu.CompilerParams(vmem_limit_bytes=FIRST_VMEM_BYTES),
        cost_estimate=SMALL,
        name="load_first",
    )(w_value, w_out)


def load_table(table, grant):
    return pl.pallas_call(
        load_kernel,
        out_shape=jax.ShapeDtypeStruct(table.shape, jnp.bfloat16),
        in_specs=[in_hbm()],
        out_specs=in_vmem(),
        scratch_shapes=[pltpu.SemaphoreType.DMA((2 * CHUNKS,))],
        compiler_params=pltpu.CompilerParams(vmem_limit_bytes=grant),
        cost_estimate=SMALL,
        name="load_table",
    )(table)


def on_device(section_input, query, key_stash, incoming, version, w_value, w_out):
    half = lax.axis_index("half")
    odd = is_odd()
    n_pairs = lax.axis_size("pair")
    outer = lax.axis_size("outer")
    n_tensor = 2 * outer
    width = w_value.shape[3]
    shard = section_input.shape[1]

    def swap_half(array):
        return lax.ppermute(array, "half", [(0, 1), (1, 0)])

    def swap_core(array):
        return lax.ppermute(array, "core", [(0, 1), (1, 0)])

    def to_row(array, delta, other_core=0):
        pairs = [
            (2 * i + c, 2 * (i ^ delta) + (c ^ other_core)) for i in range(outer) for c in range(2)
        ]
        return lax.ppermute(array, ("outer", "core"), pairs)

    def to_other_half(array, delta):
        pairs = [
            (h * n_tensor + i, (1 - h) * n_tensor + (i ^ (2 * delta)))
            for h in range(2)
            for i in range(n_tensor)
        ]
        return lax.ppermute(array, ("half", "outer", "core"), pairs)

    def swap_section(array, delta):
        pairs = [
            (p * n_tensor + i, (p ^ 1) * n_tensor + (i ^ (2 * delta)))
            for p in range(n_pairs)
            for i in range(n_tensor)
        ]
        return lax.ppermute(array, ("pair", "outer", "core"), pairs)

    def own_columns(array):
        return lax.dynamic_slice_in_dim(array, half * width, width, 1)

    def other_columns(array):
        return lax.dynamic_slice_in_dim(array, (1 - half) * width, width, 1)

    def total(parts):
        value = parts[0].astype(jnp.float32)
        for part in parts[1:]:
            value = value + part.astype(jnp.float32)
        return value

    def spread_rows(piece):
        return [piece] + [to_row(piece, delta) for delta in range(1, outer)]

    first = jnp.where(odd, incoming[0], section_input[0])
    own_piece, sent_piece = own_columns(first), other_columns(first)
    other_piece = swap_half(sent_piece)
    first_piece = [own_piece, other_piece]
    later_own, _ = lax.optimization_barrier((own_piece, other_piece))
    first_mine = [spread_rows(later_own), spread_rows(other_piece)]
    own_probs = attention_probs(jnp.concatenate([query, key_stash]))
    note = jnp.full((NOTE_ROWS, LANES), version[0], jnp.int32).astype(jnp.bfloat16)
    own_probs = jnp.concatenate([own_probs, note])
    other_probs = swap_half(own_probs)
    late_value, late_out, _ = lax.optimization_barrier((w_value, w_out, own_probs))
    first_table = load_first(late_value, late_out)
    first_theirs = []
    for pieces in first_mine:
        later, _ = lax.optimization_barrier((pieces, first_table))
        first_theirs.append([swap_core(piece) for piece in later])

    probs = [own_probs, other_probs]
    partial, first_full = [None, None], [None, None]
    for m in (1, 0):
        mine = first_mine[m]
        if m == 0:
            mine, probs, _ = lax.optimization_barrier((mine, probs, partial[1]))
        partial[m], first_full[m] = project(
            shard, probs[m], (first_table,), mine, first_theirs[m]
        )
    arrived = [swap_half(partial[1]), swap_half(partial[0])]
    later_value, _ = lax.optimization_barrier((w_value, partial))
    value_table = load_table(later_value, VALUE_VMEM_BYTES)
    first_result, first_sent = [None, None], [None, None]
    second_piece, second_full = [None, None], [None, None]
    for m in range(2):
        first_result[m], keep, send = mix(
            True, probs[m], value_table, partial[m], arrived[m], outer
        )
        first_sent[m] = combine(keep, swap_core(send), first_piece[m])
    later_out, _ = lax.optimization_barrier((w_out, first_sent))
    out_table = load_table(later_out, OUT_VMEM_BYTES)
    later_input, _ = lax.optimization_barrier((section_input[0], out_table))
    input_own, input_sent = lax.optimization_barrier(
        (own_columns(later_input), other_columns(later_input))
    )
    input_piece = [input_own, swap_half(input_sent)]
    for m in range(2):
        received = [swap_section(part, d) for d, part in enumerate(first_sent[m])]
        second_piece[m] = jnp.where(odd, input_piece[m], total(received).astype(jnp.bfloat16))
    for m in range(2):
        mine = spread_rows(second_piece[m])
        theirs = [swap_core(second_piece[m])]
        theirs += [to_row(second_piece[m], delta, 1) for delta in range(1, outer)]
        partial[m], second_full[m] = project(
            shard, probs[m], (value_table, out_table), mine, theirs
        )
    arrived = [swap_half(partial[1]), swap_half(partial[0])]
    second_result, last_sent = [None, None], [None, None]
    for m in (1, 0):
        second_result[m], keep, send = mix(
            False, probs[m], value_table, partial[m], arrived[m], outer
        )
        if m == 0:
            keep, _ = lax.optimization_barrier((keep, last_sent[1]))
        last_sent[m] = combine(keep, swap_core(send), second_piece[m], first_sent[m])
    other_parts = [to_other_half(part, d) for d, part in enumerate(last_sent[1])]
    own_parts = [last_sent[0][0]] + [to_row(part, d + 1) for d, part in enumerate(last_sent[0][1:])]
    second_result, _ = lax.optimization_barrier((second_result, last_sent))
    grad_value, grad_out = weight_grads(
        first_result, second_result, first_full, second_full
    )
    other_grad = lax.optimization_barrier(total(other_parts).astype(jnp.bfloat16))
    own_parts, _ = lax.optimization_barrier((own_parts, grad_value))
    own_grad = total(own_parts).astype(jnp.bfloat16)
    input_grad = jnp.concatenate(
        [jnp.where(half == 0, own_grad, other_grad), jnp.where(half == 0, other_grad, own_grad)],
        axis=1,
    )
    return (input_grad[None], grad_value, grad_out)


def solution(mesh):
    sections, tensor = mesh.devices.shape
    split = Mesh(
        mesh.devices.reshape(sections // 2, 2, tensor // 2, 2), ("pair", "half", "outer", "core")
    )
    slots, places = ("pair", "half"), ("outer", "core")
    by_tokens = P(slots, places, None)
    by_rows = P(slots, None, places, None)
    return jax.shard_map(
        on_device,
        mesh=split,
        in_specs=(by_tokens, by_tokens, by_tokens, by_tokens, P(slots), by_rows, by_rows),
        out_specs=(by_tokens, by_tokens, by_tokens),
        check_vma=False,
    )
```

```python
import functools
import math

import jax
import jax.numpy as jnp
from jax import lax
from jax.experimental import pallas as pl
from jax.experimental.pallas import tpu as pltpu
from jax.sharding import Mesh, PartitionSpec as P

HEAD_DIM = 96
CHUNKS = 4
VMEM_BYTES = 8 * 2**20
GRAD_VMEM_BYTES = 16 * 2**20
FIRST_VMEM_BYTES = 46 * 2**20
VALUE_VMEM_BYTES = 47 * 2**20
OUT_VMEM_BYTES = 42 * 2**20
LANES = 128
NOTE_ROWS = 16
SMALL = pl.CostEstimate(flops=1, bytes_accessed=1, transcendentals=0)
NN = (((1,), (0,)), ((), ()))
NT = (((1,), (1,)), ((), ()))
TN = (((0,), (0,)), ((), ()))


def matmul(left_side, right_side, dims):
    return lax.dot_general(left_side, right_side, dims, preferred_element_type=jnp.float32)


def in_vmem():
    return pl.BlockSpec(memory_space=pltpu.VMEM)


def in_hbm():
    return pl.BlockSpec(memory_space=pltpu.HBM)


def in_place():
    return pl.BlockSpec(memory_space=pl.ANY)


def is_odd():
    return (lax.axis_index("pair") & 1) == 1


def noted_version(message_ref):
    note = message_ref[message_ref.shape[0] - NOTE_ROWS :, :]
    return (jnp.max(note.astype(jnp.float32)) > 0.5).astype(jnp.int32)


def project_kernel(outer, shard, n_tables, message_ref, *refs):
    table_refs, piece_refs = refs[:n_tables], refs[n_tables:-2]
    partial_ref, full_ref = refs[-2:]
    version = noted_version(message_ref)
    first_core = lax.axis_index("core") == 0
    mine = [ref[:shard, :] for ref in piece_refs[:outer]]
    theirs = [ref[:shard, :] for ref in piece_refs[outer:]]
    for place in range(outer):
        offset = lax.axis_index("outer") ^ place
        own, other = mine[0], theirs[0]
        for delta in range(1, outer):
            own = jnp.where(offset == delta, mine[delta], own)
            other = jnp.where(offset == delta, theirs[delta], other)
        start = 2 * place * shard
        full_ref[start : start + shard, :] = jnp.where(first_core, own, other)
        full_ref[start + shard : start + 2 * shard, :] = jnp.where(first_core, other, own)
    flipped = full_ref[...].T

    def rows_of(table_ref):
        partial_ref[...] = matmul(table_ref[0, version], flipped, NN).astype(jnp.bfloat16)

    if n_tables == 1:
        rows_of(table_refs[0])
    else:
        pl.when(is_odd())(lambda: rows_of(table_refs[0]))
        pl.when(jnp.logical_not(is_odd()))(lambda: rows_of(table_refs[1]))


def project(shard, message, tables, mine, theirs):
    outer = len(mine)
    rows, width = tables[0].shape[2:]
    tokens = 2 * outer * shard
    return pl.pallas_call(
        functools.partial(project_kernel, outer, shard, len(tables)),
        out_shape=(
            jax.ShapeDtypeStruct((rows, tokens), jnp.bfloat16),
            jax.ShapeDtypeStruct((tokens, width), jnp.bfloat16),
        ),
        in_specs=[in_vmem()] * (1 + len(tables) + 2 * outer),
        out_specs=(in_vmem(), in_vmem()),
        compiler_params=pltpu.CompilerParams(vmem_limit_bytes=VMEM_BYTES),
        cost_estimate=SMALL,
        name="project",
    )(message, *tables, *mine, *theirs)


def mix_kernel(
    outer,
    odd_phase,
    message_ref,
    value_ref,
    mine_ref,
    arrived_ref,
    result_ref,
    keep_ref,
    send_ref,
):
    version = noted_version(message_ref)
    step = value_ref.shape[3] // CHUNKS
    tokens = mine_ref.shape[1]

    def heads(dims):
        for head in range(mine_ref.shape[0] // HEAD_DIM):
            rows = pl.ds(head * HEAD_DIM, HEAD_DIM)
            total = mine_ref[rows, :].astype(jnp.float32) + arrived_ref[rows, :].astype(jnp.float32)
            probs = message_ref[head * tokens : (head + 1) * tokens, :]
            mixed = matmul(total.astype(jnp.bfloat16), probs, dims)
            result_ref[rows, :] = mixed.astype(jnp.bfloat16)

    natural = is_odd() == odd_phase
    pl.when(natural)(lambda: heads(NN))
    pl.when(jnp.logical_not(natural))(lambda: heads(NT))

    flipped = result_ref[...].T
    second_core = lax.axis_index("core") == 1
    shard = tokens // (2 * outer)
    for chunk in range(CHUNKS):
        columns = pl.ds(chunk * step, step)
        partial = matmul(flipped, value_ref[0, version, :, columns], NN)
        for place in range(outer):
            low = partial[2 * place * shard : (2 * place + 1) * shard]
            high = partial[(2 * place + 1) * shard : (2 * place + 2) * shard]
            keep_ref[place, :, columns] = jnp.where(second_core, high, low).astype(jnp.bfloat16)
            send_ref[place, :, columns] = jnp.where(second_core, low, high).astype(jnp.bfloat16)


def mix(odd_phase, message, w_value, mine, arrived, outer):
    rows, width = w_value.shape[2:]
    tokens = mine.shape[1]
    half = jax.ShapeDtypeStruct((outer, tokens // (2 * outer), width), jnp.bfloat16)
    return pl.pallas_call(
        functools.partial(mix_kernel, outer, odd_phase),
        out_shape=(jax.ShapeDtypeStruct((rows, tokens), jnp.bfloat16), half, half),
        in_specs=[in_vmem()] * 4,
        out_specs=(in_vmem(), in_vmem(), in_vmem()),
        compiler_params=pltpu.CompilerParams(vmem_limit_bytes=VMEM_BYTES),
        cost_estimate=SMALL,
        name="mix",
    )(message, w_value, mine, arrived)


def combine_kernel(outer, last, keep_ref, arrived_ref, addend_ref, *refs):
    first_refs, sent_refs = refs[:-outer], refs[-outer:]
    for delta in range(outer):
        spot = lax.axis_index("outer") ^ delta
        total = keep_ref[spot].astype(jnp.float32) + arrived_ref[spot].astype(jnp.float32)
        if delta == 0:
            total = total + addend_ref[: total.shape[0], :].astype(jnp.float32)
        total = total.astype(jnp.bfloat16)
        if last:
            total = jnp.where(is_odd(), first_refs[delta][...], total)
        sent_refs[delta][...] = total


def combine(keep, arrived, addend, first_sent=()):
    outer, shard, width = keep.shape
    piece = jax.ShapeDtypeStruct((shard, width), jnp.bfloat16)
    return pl.pallas_call(
        functools.partial(combine_kernel, outer, len(first_sent) > 0),
        out_shape=(piece,) * outer,
        in_specs=[in_vmem()] * (3 + len(first_sent)),
        out_specs=(in_vmem(),) * outer,
        compiler_params=pltpu.CompilerParams(vmem_limit_bytes=VMEM_BYTES),
        cost_estimate=SMALL,
        name="combine",
    )(keep, arrived, addend, *first_sent)


def weight_grad_kernel(
    a0, a1, b0, b1, first0, first1, second0, second1, value_ref, out_ref
):
    odd = is_odd()
    left_first = jnp.concatenate([a0[...], a1[...]], axis=1)
    left_second = jnp.concatenate([b0[...], b1[...]], axis=1)
    right_second = jnp.concatenate([second0[...], second1[...]], axis=0)
    right_first = jnp.concatenate([first0[...], first1[...]], axis=0)
    grad_first = matmul(left_first, right_second, NN)
    grad_second = matmul(left_second, right_first, NN)
    value_ref[0] = jnp.where(odd, grad_first, grad_second).astype(jnp.bfloat16)
    out_ref[0] = jnp.where(odd, grad_second, grad_first).astype(jnp.bfloat16)


def weight_grads(first_results, second_results, first_full, second_full):
    rows, tokens = first_results[0].shape
    width = first_full[0].shape[1]
    step = rows // CHUNKS
    grad = jax.ShapeDtypeStruct((1, rows, width), jnp.bfloat16)
    left = pl.BlockSpec((step, tokens), lambda i: (i, 0))
    single = pl.BlockSpec((tokens, width), lambda i: (0, 0))
    wide = pl.BlockSpec((1, step, width), lambda i: (0, i, 0))
    return pl.pallas_call(
        weight_grad_kernel,
        grid=(CHUNKS,),
        out_shape=(grad, grad),
        in_specs=[left] * 4 + [single] * 4,
        out_specs=(wide, wide),
        compiler_params=pltpu.CompilerParams(vmem_limit_bytes=GRAD_VMEM_BYTES),
        cost_estimate=SMALL,
        name="weight_grads",
    )(*first_results, *second_results, *first_full, *second_full)


def load(source_ref, table_ref, sems):
    step = table_ref.shape[2] // CHUNKS
    copies = []
    for version in range(2):
        for chunk in range(CHUNKS):
            spot = (slice(None), version, pl.ds(chunk * step, step))
            copies.append(
                pltpu.make_async_copy(
                    source_ref.at[spot], table_ref.at[spot], sems.at[version * CHUNKS + chunk]
                )
            )
    return copies


def probs_kernel(stash_ref, probs_ref):
    tokens = stash_ref.shape[2]
    causal = lax.broadcasted_iota(jnp.int32, (tokens, tokens), 1) <= lax.broadcasted_iota(
        jnp.int32, (tokens, tokens), 0
    )
    for head in range(stash_ref.shape[1] // HEAD_DIM):
        rows = pl.ds(head * HEAD_DIM, HEAD_DIM)
        scores = matmul(stash_ref[0, rows, :], stash_ref[1, rows, :], TN)
        scores = jnp.where(causal, scores * (1.0 / math.sqrt(HEAD_DIM)), -jnp.inf)
        expo = jnp.exp(scores - jnp.max(scores, axis=1, keepdims=True))
        probs = (expo / jnp.sum(expo, axis=1, keepdims=True)).astype(jnp.bfloat16)
        probs_ref[head * tokens : (head + 1) * tokens, :] = probs


def attention_probs(stash):
    rows, tokens = stash.shape[1:]
    return pl.pallas_call(
        probs_kernel,
        out_shape=jax.ShapeDtypeStruct((rows // HEAD_DIM * tokens, tokens), jnp.bfloat16),
        in_specs=[in_vmem()],
        out_specs=in_vmem(),
        compiler_params=pltpu.CompilerParams(vmem_limit_bytes=VMEM_BYTES),
        cost_estimate=SMALL,
        name="probs",
    )(stash)


def load_kernel(source_ref, table_ref, sems):
    copies = load(source_ref, table_ref, sems)
    for copy in copies:
        copy.start()
    for copy in copies:
        copy.wait()


def load_first_kernel(value_ref, out_ref, table_ref, sems):
    def start(source_ref):
        for copy in load(source_ref, table_ref, sems):
            copy.start()

    pl.when(is_odd())(lambda: start(out_ref))
    pl.when(jnp.logical_not(is_odd()))(lambda: start(value_ref))
    for copy in load(value_ref, table_ref, sems):
        copy.wait()


def load_first(w_value, w_out):
    return pl.pallas_call(
        load_first_kernel,
        out_shape=jax.ShapeDtypeStruct(w_value.shape, jnp.bfloat16),
        in_specs=[in_hbm(), in_hbm()],
        out_specs=in_vmem(),
        scratch_shapes=[pltpu.SemaphoreType.DMA((2 * CHUNKS,))],
        compiler_params=pltpu.CompilerParams(vmem_limit_bytes=FIRST_VMEM_BYTES),
        cost_estimate=SMALL,
        name="load_first",
    )(w_value, w_out)


def load_table(table, grant):
    return pl.pallas_call(
        load_kernel,
        out_shape=jax.ShapeDtypeStruct(table.shape, jnp.bfloat16),
        in_specs=[in_hbm()],
        out_specs=in_vmem(),
        scratch_shapes=[pltpu.SemaphoreType.DMA((2 * CHUNKS,))],
        compiler_params=pltpu.CompilerParams(vmem_limit_bytes=grant),
        cost_estimate=SMALL,
        name="load_table",
    )(table)


def on_device(section_input, query, key_stash, incoming, version, w_value, w_out):
    half = lax.axis_index("half")
    odd = is_odd()
    n_pairs = lax.axis_size("pair")
    outer = lax.axis_size("outer")
    n_tensor = 2 * outer
    width = w_value.shape[3]
    shard = section_input.shape[1]

    def swap_half(array):
        return lax.ppermute(array, "half", [(0, 1), (1, 0)])

    def swap_core(array):
        return lax.ppermute(array, "core", [(0, 1), (1, 0)])

    def to_row(array, delta, other_core=0):
        pairs = [
            (2 * i + c, 2 * (i ^ delta) + (c ^ other_core)) for i in range(outer) for c in range(2)
        ]
        return lax.ppermute(array, ("outer", "core"), pairs)

    def to_other_half(array, delta):
        pairs = [
            (h * n_tensor + i, (1 - h) * n_tensor + (i ^ (2 * delta)))
            for h in range(2)
            for i in range(n_tensor)
        ]
        return lax.ppermute(array, ("half", "outer", "core"), pairs)

    def swap_section(array, delta):
        pairs = [
            (p * n_tensor + i, (p ^ 1) * n_tensor + (i ^ (2 * delta)))
            for p in range(n_pairs)
            for i in range(n_tensor)
        ]
        return lax.ppermute(array, ("pair", "outer", "core"), pairs)

    def own_columns(array):
        return lax.dynamic_slice_in_dim(array, half * width, width, 1)

    def other_columns(array):
        return lax.dynamic_slice_in_dim(array, (1 - half) * width, width, 1)

    def total(parts):
        value = parts[0].astype(jnp.float32)
        for part in parts[1:]:
            value = value + part.astype(jnp.float32)
        return value

    def spread_rows(piece):
        return [piece] + [to_row(piece, delta) for delta in range(1, outer)]

    first = jnp.where(odd, incoming[0], section_input[0])
    own_piece, sent_piece = own_columns(first), other_columns(first)
    other_piece = swap_half(sent_piece)
    first_piece = [own_piece, other_piece]
    later_own, _ = lax.optimization_barrier((own_piece, other_piece))
    first_mine = [spread_rows(later_own), spread_rows(other_piece)]
    own_probs = attention_probs(jnp.concatenate([query, key_stash]))
    note = jnp.full((NOTE_ROWS, LANES), version[0], jnp.int32).astype(jnp.bfloat16)
    own_probs = jnp.concatenate([own_probs, note])
    other_probs = swap_half(own_probs)
    late_value, late_out, _ = lax.optimization_barrier((w_value, w_out, own_probs))
    first_table = load_first(late_value, late_out)
    first_theirs = []
    for pieces in first_mine:
        later, _ = lax.optimization_barrier((pieces, first_table))
        first_theirs.append([swap_core(piece) for piece in later])

    probs = [own_probs, other_probs]
    partial, first_full = [None, None], [None, None]
    for m in (1, 0):
        mine = first_mine[m]
        if m == 0:
            mine, probs, _ = lax.optimization_barrier((mine, probs, partial[1]))
        partial[m], first_full[m] = project(
            shard, probs[m], (first_table,), mine, first_theirs[m]
        )
    arrived = [swap_half(partial[1]), swap_half(partial[0])]
    later_value, _ = lax.optimization_barrier((w_value, partial))
    value_table = load_table(later_value, VALUE_VMEM_BYTES)
    first_result, first_sent = [None, None], [None, None]
    second_piece, second_full = [None, None], [None, None]
    for m in range(2):
        first_result[m], keep, send = mix(
            True, probs[m], value_table, partial[m], arrived[m], outer
        )
        first_sent[m] = combine(keep, swap_core(send), first_piece[m])
    later_out, _ = lax.optimization_barrier((w_out, first_sent))
    out_table = load_table(later_out, OUT_VMEM_BYTES)
    later_input, _ = lax.optimization_barrier((section_input[0], out_table))
    input_own, input_sent = lax.optimization_barrier(
        (own_columns(later_input), other_columns(later_input))
    )
    input_piece = [input_own, swap_half(input_sent)]
    for m in range(2):
        received = [swap_section(part, d) for d, part in enumerate(first_sent[m])]
        last_received = received
        second_piece[m] = jnp.where(odd, input_piece[m], total(received).astype(jnp.bfloat16))
    for m in range(2):
        mine = spread_rows(second_piece[m])
        swapped = second_piece[m]
        if m == 0:
            swapped, _ = lax.optimization_barrier((swapped, last_received))
        theirs = [swap_core(swapped)]
        theirs += [to_row(second_piece[m], delta, 1) for delta in range(1, outer)]
        partial[m], second_full[m] = project(
            shard, probs[m], (value_table, out_table), mine, theirs
        )
    arrived = [swap_half(partial[1]), swap_half(partial[0])]
    second_result, last_sent = [None, None], [None, None]
    for m in (1, 0):
        second_result[m], keep, send = mix(
            False, probs[m], value_table, partial[m], arrived[m], outer
        )
        if m == 0:
            keep, _ = lax.optimization_barrier((keep, last_sent[1]))
        last_sent[m] = combine(keep, swap_core(send), second_piece[m], first_sent[m])
    other_parts = [to_other_half(part, d) for d, part in enumerate(last_sent[1])]
    own_parts = [last_sent[0][0]] + [to_row(part, d + 1) for d, part in enumerate(last_sent[0][1:])]
    second_result, _ = lax.optimization_barrier((second_result, last_sent))
    grad_value, grad_out = weight_grads(
        first_result, second_result, first_full, second_full
    )
    other_grad = lax.optimization_barrier(total(other_parts).astype(jnp.bfloat16))
    own_parts, _ = lax.optimization_barrier((own_parts, grad_value))
    own_grad = total(own_parts).astype(jnp.bfloat16)
    input_grad = jnp.concatenate(
        [jnp.where(half == 0, own_grad, other_grad), jnp.where(half == 0, other_grad, own_grad)],
        axis=1,
    )
    return (input_grad[None], grad_value, grad_out)


def solution(mesh):
    sections, tensor = mesh.devices.shape
    split = Mesh(
        mesh.devices.reshape(sections // 2, 2, tensor // 2, 2), ("pair", "half", "outer", "core")
    )
    slots, places = ("pair", "half"), ("outer", "core")
    by_tokens = P(slots, places, None)
    by_rows = P(slots, None, places, None)
    return jax.shard_map(
        on_device,
        mesh=split,
        in_specs=(by_tokens, by_tokens, by_tokens, by_tokens, P(slots), by_rows, by_rows),
        out_specs=(by_tokens, by_tokens, by_tokens),
        check_vma=False,
    )
```

```python
import functools
import math

import jax
import jax.numpy as jnp
from jax import lax
from jax.experimental import pallas as pl
from jax.experimental.pallas import tpu as pltpu
from jax.sharding import Mesh, PartitionSpec as P

HEAD_DIM = 96
CHUNKS = 4
VMEM_BYTES = 8 * 2**20
GRAD_VMEM_BYTES = 16 * 2**20
FIRST_VMEM_BYTES = 46 * 2**20
VALUE_VMEM_BYTES = 47 * 2**20
OUT_VMEM_BYTES = 42 * 2**20
LANES = 128
NOTE_ROWS = 16
SMALL = pl.CostEstimate(flops=1, bytes_accessed=1, transcendentals=0)
NN = (((1,), (0,)), ((), ()))
NT = (((1,), (1,)), ((), ()))
TN = (((0,), (0,)), ((), ()))


def matmul(left_side, right_side, dims):
    return lax.dot_general(left_side, right_side, dims, preferred_element_type=jnp.float32)


def in_vmem():
    return pl.BlockSpec(memory_space=pltpu.VMEM)


def in_hbm():
    return pl.BlockSpec(memory_space=pltpu.HBM)


def in_place():
    return pl.BlockSpec(memory_space=pl.ANY)


def is_odd():
    return (lax.axis_index("pair") & 1) == 1


def noted_version(message_ref):
    note = message_ref[message_ref.shape[0] - NOTE_ROWS :, :]
    return (jnp.max(note.astype(jnp.float32)) > 0.5).astype(jnp.int32)


def project_kernel(outer, shard, n_tables, message_ref, *refs):
    table_refs, piece_refs = refs[:n_tables], refs[n_tables:-2]
    partial_ref, full_ref = refs[-2:]
    version = noted_version(message_ref)
    first_core = lax.axis_index("core") == 0
    mine = [ref[:shard, :] for ref in piece_refs[:outer]]
    theirs = [ref[:shard, :] for ref in piece_refs[outer:]]
    for place in range(outer):
        offset = lax.axis_index("outer") ^ place
        own, other = mine[0], theirs[0]
        for delta in range(1, outer):
            own = jnp.where(offset == delta, mine[delta], own)
            other = jnp.where(offset == delta, theirs[delta], other)
        start = 2 * place * shard
        full_ref[start : start + shard, :] = jnp.where(first_core, own, other)
        full_ref[start + shard : start + 2 * shard, :] = jnp.where(first_core, other, own)
    flipped = full_ref[...].T

    def rows_of(table_ref):
        partial_ref[...] = matmul(table_ref[0, version], flipped, NN).astype(jnp.bfloat16)

    if n_tables == 1:
        rows_of(table_refs[0])
    else:
        pl.when(is_odd())(lambda: rows_of(table_refs[0]))
        pl.when(jnp.logical_not(is_odd()))(lambda: rows_of(table_refs[1]))


def project(shard, message, tables, mine, theirs):
    outer = len(mine)
    rows, width = tables[0].shape[2:]
    tokens = 2 * outer * shard
    return pl.pallas_call(
        functools.partial(project_kernel, outer, shard, len(tables)),
        out_shape=(
            jax.ShapeDtypeStruct((rows, tokens), jnp.bfloat16),
            jax.ShapeDtypeStruct((tokens, width), jnp.bfloat16),
        ),
        in_specs=[in_vmem()] * (1 + len(tables) + 2 * outer),
        out_specs=(in_vmem(), in_vmem()),
        compiler_params=pltpu.CompilerParams(vmem_limit_bytes=VMEM_BYTES),
        cost_estimate=SMALL,
        name="project",
    )(message, *tables, *mine, *theirs)


def mix_kernel(
    outer,
    odd_phase,
    message_ref,
    value_ref,
    mine_ref,
    arrived_ref,
    result_ref,
    keep_ref,
    send_ref,
):
    version = noted_version(message_ref)
    step = value_ref.shape[3] // CHUNKS
    tokens = mine_ref.shape[1]

    def heads(dims):
        for head in range(mine_ref.shape[0] // HEAD_DIM):
            rows = pl.ds(head * HEAD_DIM, HEAD_DIM)
            total = mine_ref[rows, :].astype(jnp.float32) + arrived_ref[rows, :].astype(jnp.float32)
            probs = message_ref[head * tokens : (head + 1) * tokens, :]
            mixed = matmul(total.astype(jnp.bfloat16), probs, dims)
            result_ref[rows, :] = mixed.astype(jnp.bfloat16)

    natural = is_odd() == odd_phase
    pl.when(natural)(lambda: heads(NN))
    pl.when(jnp.logical_not(natural))(lambda: heads(NT))

    flipped = result_ref[...].T
    second_core = lax.axis_index("core") == 1
    shard = tokens // (2 * outer)
    for chunk in range(CHUNKS):
        columns = pl.ds(chunk * step, step)
        partial = matmul(flipped, value_ref[0, version, :, columns], NN)
        for place in range(outer):
            low = partial[2 * place * shard : (2 * place + 1) * shard]
            high = partial[(2 * place + 1) * shard : (2 * place + 2) * shard]
            keep_ref[place, :, columns] = jnp.where(second_core, high, low).astype(jnp.bfloat16)
            send_ref[place, :, columns] = jnp.where(second_core, low, high).astype(jnp.bfloat16)


def mix(odd_phase, message, w_value, mine, arrived, outer):
    rows, width = w_value.shape[2:]
    tokens = mine.shape[1]
    half = jax.ShapeDtypeStruct((outer, tokens // (2 * outer), width), jnp.bfloat16)
    return pl.pallas_call(
        functools.partial(mix_kernel, outer, odd_phase),
        out_shape=(jax.ShapeDtypeStruct((rows, tokens), jnp.bfloat16), half, half),
        in_specs=[in_vmem()] * 4,
        out_specs=(in_vmem(), in_vmem(), in_vmem()),
        compiler_params=pltpu.CompilerParams(vmem_limit_bytes=VMEM_BYTES),
        cost_estimate=SMALL,
        name="mix",
    )(message, w_value, mine, arrived)


def combine_kernel(outer, last, keep_ref, arrived_ref, addend_ref, *refs):
    first_refs, sent_refs = refs[:-outer], refs[-outer:]
    for delta in range(outer):
        spot = lax.axis_index("outer") ^ delta
        total = keep_ref[spot].astype(jnp.float32) + arrived_ref[spot].astype(jnp.float32)
        if delta == 0:
            total = total + addend_ref[: total.shape[0], :].astype(jnp.float32)
        total = total.astype(jnp.bfloat16)
        if last:
            total = jnp.where(is_odd(), first_refs[delta][...], total)
        sent_refs[delta][...] = total


def combine(keep, arrived, addend, first_sent=()):
    outer, shard, width = keep.shape
    piece = jax.ShapeDtypeStruct((shard, width), jnp.bfloat16)
    return pl.pallas_call(
        functools.partial(combine_kernel, outer, len(first_sent) > 0),
        out_shape=(piece,) * outer,
        in_specs=[in_vmem()] * (3 + len(first_sent)),
        out_specs=(in_vmem(),) * outer,
        compiler_params=pltpu.CompilerParams(vmem_limit_bytes=VMEM_BYTES),
        cost_estimate=SMALL,
        name="combine",
    )(keep, arrived, addend, *first_sent)


def weight_grad_kernel(
    a0, a1, b0, b1, first0, first1, second0, second1, value_ref, out_ref
):
    odd = is_odd()
    left_first = jnp.concatenate([a0[...], a1[...]], axis=1)
    left_second = jnp.concatenate([b0[...], b1[...]], axis=1)
    right_second = jnp.concatenate([second0[...], second1[...]], axis=0)
    right_first = jnp.concatenate([first0[...], first1[...]], axis=0)
    grad_first = matmul(left_first, right_second, NN)
    grad_second = matmul(left_second, right_first, NN)
    value_ref[0] = jnp.where(odd, grad_first, grad_second).astype(jnp.bfloat16)
    out_ref[0] = jnp.where(odd, grad_second, grad_first).astype(jnp.bfloat16)


def weight_grads(first_results, second_results, first_full, second_full):
    rows, tokens = first_results[0].shape
    width = first_full[0].shape[1]
    step = rows // CHUNKS
    grad = jax.ShapeDtypeStruct((1, rows, width), jnp.bfloat16)
    left = pl.BlockSpec((step, tokens), lambda i: (i, 0))
    single = pl.BlockSpec((tokens, width), lambda i: (0, 0))
    wide = pl.BlockSpec((1, step, width), lambda i: (0, i, 0))
    return pl.pallas_call(
        weight_grad_kernel,
        grid=(CHUNKS,),
        out_shape=(grad, grad),
        in_specs=[left] * 4 + [single] * 4,
        out_specs=(wide, wide),
        compiler_params=pltpu.CompilerParams(vmem_limit_bytes=GRAD_VMEM_BYTES),
        cost_estimate=SMALL,
        name="weight_grads",
    )(*first_results, *second_results, *first_full, *second_full)


def load(source_ref, table_ref, sems):
    step = table_ref.shape[2] // CHUNKS
    copies = []
    for version in range(2):
        for chunk in range(CHUNKS):
            spot = (slice(None), version, pl.ds(chunk * step, step))
            copies.append(
                pltpu.make_async_copy(
                    source_ref.at[spot], table_ref.at[spot], sems.at[version * CHUNKS + chunk]
                )
            )
    return copies


def probs_kernel(stash_ref, probs_ref):
    tokens = stash_ref.shape[2]
    causal = lax.broadcasted_iota(jnp.int32, (tokens, tokens), 1) <= lax.broadcasted_iota(
        jnp.int32, (tokens, tokens), 0
    )
    for head in range(stash_ref.shape[1] // HEAD_DIM):
        rows = pl.ds(head * HEAD_DIM, HEAD_DIM)
        scores = matmul(stash_ref[0, rows, :], stash_ref[1, rows, :], TN)
        scores = jnp.where(causal, scores * (1.0 / math.sqrt(HEAD_DIM)), -jnp.inf)
        expo = jnp.exp(scores - jnp.max(scores, axis=1, keepdims=True))
        probs = (expo / jnp.sum(expo, axis=1, keepdims=True)).astype(jnp.bfloat16)
        probs_ref[head * tokens : (head + 1) * tokens, :] = probs


def attention_probs(stash):
    rows, tokens = stash.shape[1:]
    return pl.pallas_call(
        probs_kernel,
        out_shape=jax.ShapeDtypeStruct((rows // HEAD_DIM * tokens, tokens), jnp.bfloat16),
        in_specs=[in_vmem()],
        out_specs=in_vmem(),
        compiler_params=pltpu.CompilerParams(vmem_limit_bytes=VMEM_BYTES),
        cost_estimate=SMALL,
        name="probs",
    )(stash)


def load_kernel(source_ref, table_ref, sems):
    copies = load(source_ref, table_ref, sems)
    for copy in copies:
        copy.start()
    for copy in copies:
        copy.wait()


def load_first_kernel(value_ref, out_ref, table_ref, sems):
    def start(source_ref):
        for copy in load(source_ref, table_ref, sems):
            copy.start()

    pl.when(is_odd())(lambda: start(out_ref))
    pl.when(jnp.logical_not(is_odd()))(lambda: start(value_ref))
    for copy in load(value_ref, table_ref, sems):
        copy.wait()


def load_first(w_value, w_out):
    return pl.pallas_call(
        load_first_kernel,
        out_shape=jax.ShapeDtypeStruct(w_value.shape, jnp.bfloat16),
        in_specs=[in_hbm(), in_hbm()],
        out_specs=in_vmem(),
        scratch_shapes=[pltpu.SemaphoreType.DMA((2 * CHUNKS,))],
        compiler_params=pltpu.CompilerParams(vmem_limit_bytes=FIRST_VMEM_BYTES),
        cost_estimate=SMALL,
        name="load_first",
    )(w_value, w_out)


def load_table(table, grant):
    return pl.pallas_call(
        load_kernel,
        out_shape=jax.ShapeDtypeStruct(table.shape, jnp.bfloat16),
        in_specs=[in_hbm()],
        out_specs=in_vmem(),
        scratch_shapes=[pltpu.SemaphoreType.DMA((2 * CHUNKS,))],
        compiler_params=pltpu.CompilerParams(vmem_limit_bytes=grant),
        cost_estimate=SMALL,
        name="load_table",
    )(table)


def on_device(section_input, query, key_stash, incoming, version, w_value, w_out):
    half = lax.axis_index("half")
    odd = is_odd()
    n_pairs = lax.axis_size("pair")
    outer = lax.axis_size("outer")
    n_tensor = 2 * outer
    width = w_value.shape[3]
    shard = section_input.shape[1]

    def swap_half(array):
        return lax.ppermute(array, "half", [(0, 1), (1, 0)])

    def swap_core(array):
        return lax.ppermute(array, "core", [(0, 1), (1, 0)])

    def to_row(array, delta, other_core=0):
        pairs = [
            (2 * i + c, 2 * (i ^ delta) + (c ^ other_core)) for i in range(outer) for c in range(2)
        ]
        return lax.ppermute(array, ("outer", "core"), pairs)

    def to_other_half(array, delta):
        pairs = [
            (h * n_tensor + i, (1 - h) * n_tensor + (i ^ (2 * delta)))
            for h in range(2)
            for i in range(n_tensor)
        ]
        return lax.ppermute(array, ("half", "outer", "core"), pairs)

    def swap_section(array, delta):
        pairs = [
            (p * n_tensor + i, (p ^ 1) * n_tensor + (i ^ (2 * delta)))
            for p in range(n_pairs)
            for i in range(n_tensor)
        ]
        return lax.ppermute(array, ("pair", "outer", "core"), pairs)

    def own_columns(array):
        return lax.dynamic_slice_in_dim(array, half * width, width, 1)

    def other_columns(array):
        return lax.dynamic_slice_in_dim(array, (1 - half) * width, width, 1)

    def total(parts):
        value = parts[0].astype(jnp.float32)
        for part in parts[1:]:
            value = value + part.astype(jnp.float32)
        return value

    def spread_rows(piece):
        return [piece] + [to_row(piece, delta) for delta in range(1, outer)]

    first = jnp.where(odd, incoming[0], section_input[0])
    own_piece, sent_piece = own_columns(first), other_columns(first)
    other_piece = swap_half(sent_piece)
    first_piece = [own_piece, other_piece]
    later_own, _ = lax.optimization_barrier((own_piece, other_piece))
    first_mine = [spread_rows(later_own), spread_rows(other_piece)]
    own_probs = attention_probs(jnp.concatenate([query, key_stash]))
    note = jnp.full((NOTE_ROWS, LANES), version[0], jnp.int32).astype(jnp.bfloat16)
    own_probs = jnp.concatenate([own_probs, note])
    other_probs = swap_half(own_probs)
    late_value, late_out, _ = lax.optimization_barrier((w_value, w_out, own_probs))
    first_table = load_first(late_value, late_out)
    first_theirs = []
    for pieces in first_mine:
        later, _ = lax.optimization_barrier((pieces, first_table))
        first_theirs.append([swap_core(piece) for piece in later])

    probs = [own_probs, other_probs]
    partial, first_full = [None, None], [None, None]
    for m in (1, 0):
        mine = first_mine[m]
        if m == 0:
            mine, probs, _ = lax.optimization_barrier((mine, probs, partial[1]))
        partial[m], first_full[m] = project(
            shard, probs[m], (first_table,), mine, first_theirs[m]
        )
    arrived = [swap_half(partial[1]), swap_half(partial[0])]
    later_value, _ = lax.optimization_barrier((w_value, partial))
    value_table = load_table(later_value, VALUE_VMEM_BYTES)
    first_result, first_sent = [None, None], [None, None]
    second_piece, second_full = [None, None], [None, None]
    for m in range(2):
        first_result[m], keep, send = mix(
            True, probs[m], value_table, partial[m], arrived[m], outer
        )
        first_sent[m] = combine(keep, swap_core(send), first_piece[m])
    later_out, _ = lax.optimization_barrier((w_out, first_sent))
    out_table = load_table(later_out, OUT_VMEM_BYTES)
    later_input, _ = lax.optimization_barrier((section_input[0], out_table))
    input_own, input_sent = lax.optimization_barrier(
        (own_columns(later_input), other_columns(later_input))
    )
    input_piece = [input_own, swap_half(input_sent)]
    for m in range(2):
        received = [swap_section(part, d) for d, part in enumerate(first_sent[m])]
        last_received = received
        second_piece[m] = jnp.where(odd, input_piece[m], total(received).astype(jnp.bfloat16))
    for m in range(2):
        mine = spread_rows(second_piece[m])
        swapped = second_piece[m]
        if m == 0:
            swapped, _ = lax.optimization_barrier((swapped, last_received))
        theirs = [swap_core(swapped)]
        for delta in range(1, outer):
            if m == 0:
                theirs.append(to_row(second_piece[m], delta, 1))
            else:
                late, _ = lax.optimization_barrier((mine[delta], partial[0]))
                theirs.append(swap_core(late))
        partial[m], second_full[m] = project(
            shard, probs[m], (value_table, out_table), mine, theirs
        )
    arrived = [swap_half(partial[1]), swap_half(partial[0])]
    second_result, last_sent = [None, None], [None, None]
    for m in (1, 0):
        second_result[m], keep, send = mix(
            False, probs[m], value_table, partial[m], arrived[m], outer
        )
        if m == 0:
            keep, _ = lax.optimization_barrier((keep, last_sent[1]))
        last_sent[m] = combine(keep, swap_core(send), second_piece[m], first_sent[m])
    other_parts = [to_other_half(part, d) for d, part in enumerate(last_sent[1])]
    own_parts = [last_sent[0][0]] + [to_row(part, d + 1) for d, part in enumerate(last_sent[0][1:])]
    second_result, _ = lax.optimization_barrier((second_result, last_sent))
    grad_value, grad_out = weight_grads(
        first_result, second_result, first_full, second_full
    )
    other_parts, _ = lax.optimization_barrier((other_parts, grad_value))
    other_grad = lax.optimization_barrier(total(other_parts).astype(jnp.bfloat16))
    own_parts, _ = lax.optimization_barrier((own_parts, grad_value))
    own_grad = total(own_parts).astype(jnp.bfloat16)
    input_grad = jnp.concatenate(
        [jnp.where(half == 0, own_grad, other_grad), jnp.where(half == 0, other_grad, own_grad)],
        axis=1,
    )
    return (input_grad[None], grad_value, grad_out)


def solution(mesh):
    sections, tensor = mesh.devices.shape
    split = Mesh(
        mesh.devices.reshape(sections // 2, 2, tensor // 2, 2), ("pair", "half", "outer", "core")
    )
    slots, places = ("pair", "half"), ("outer", "core")
    by_tokens = P(slots, places, None)
    by_rows = P(slots, None, places, None)
    return jax.shard_map(
        on_device,
        mesh=split,
        in_specs=(by_tokens, by_tokens, by_tokens, by_tokens, P(slots), by_rows, by_rows),
        out_specs=(by_tokens, by_tokens, by_tokens),
        check_vma=False,
    )
```

```python
import functools
import math

import jax
import jax.numpy as jnp
from jax import lax
from jax.experimental import pallas as pl
from jax.experimental.pallas import tpu as pltpu
from jax.sharding import Mesh, PartitionSpec as P

HEAD_DIM = 96
CHUNKS = 4
VMEM_BYTES = 8 * 2**20
GRAD_VMEM_BYTES = 16 * 2**20
FIRST_VMEM_BYTES = 46 * 2**20
VALUE_VMEM_BYTES = 47 * 2**20
OUT_VMEM_BYTES = 42 * 2**20
LANES = 128
NOTE_ROWS = 16
SMALL = pl.CostEstimate(flops=1, bytes_accessed=1, transcendentals=0)
NN = (((1,), (0,)), ((), ()))
NT = (((1,), (1,)), ((), ()))
TN = (((0,), (0,)), ((), ()))


def matmul(left_side, right_side, dims):
    return lax.dot_general(left_side, right_side, dims, preferred_element_type=jnp.float32)


def in_vmem():
    return pl.BlockSpec(memory_space=pltpu.VMEM)


def in_hbm():
    return pl.BlockSpec(memory_space=pltpu.HBM)


def in_place():
    return pl.BlockSpec(memory_space=pl.ANY)


def is_odd():
    return (lax.axis_index("pair") & 1) == 1


def noted_version(message_ref):
    note = message_ref[message_ref.shape[0] - NOTE_ROWS :, :]
    return (jnp.max(note.astype(jnp.float32)) > 0.5).astype(jnp.int32)


def project_kernel(outer, shard, n_tables, message_ref, *refs):
    table_refs, piece_refs = refs[:n_tables], refs[n_tables:-2]
    partial_ref, full_ref = refs[-2:]
    version = noted_version(message_ref)
    first_core = lax.axis_index("core") == 0
    mine = [ref[:shard, :] for ref in piece_refs[:outer]]
    theirs = [ref[:shard, :] for ref in piece_refs[outer:]]
    for place in range(outer):
        offset = lax.axis_index("outer") ^ place
        own, other = mine[0], theirs[0]
        for delta in range(1, outer):
            own = jnp.where(offset == delta, mine[delta], own)
            other = jnp.where(offset == delta, theirs[delta], other)
        start = 2 * place * shard
        full_ref[start : start + shard, :] = jnp.where(first_core, own, other)
        full_ref[start + shard : start + 2 * shard, :] = jnp.where(first_core, other, own)
    flipped = full_ref[...].T

    def rows_of(table_ref):
        partial_ref[...] = matmul(table_ref[0, version], flipped, NN).astype(jnp.bfloat16)

    if n_tables == 1:
        rows_of(table_refs[0])
    else:
        pl.when(is_odd())(lambda: rows_of(table_refs[0]))
        pl.when(jnp.logical_not(is_odd()))(lambda: rows_of(table_refs[1]))


def project(shard, message, tables, mine, theirs):
    outer = len(mine)
    rows, width = tables[0].shape[2:]
    tokens = 2 * outer * shard
    return pl.pallas_call(
        functools.partial(project_kernel, outer, shard, len(tables)),
        out_shape=(
            jax.ShapeDtypeStruct((rows, tokens), jnp.bfloat16),
            jax.ShapeDtypeStruct((tokens, width), jnp.bfloat16),
        ),
        in_specs=[in_vmem()] * (1 + len(tables) + 2 * outer),
        out_specs=(in_vmem(), in_vmem()),
        compiler_params=pltpu.CompilerParams(vmem_limit_bytes=VMEM_BYTES),
        cost_estimate=SMALL,
        name="project",
    )(message, *tables, *mine, *theirs)


def mix_kernel(
    outer,
    odd_phase,
    message_ref,
    value_ref,
    mine_ref,
    arrived_ref,
    result_ref,
    keep_ref,
    send_ref,
):
    version = noted_version(message_ref)
    step = value_ref.shape[3] // CHUNKS
    tokens = mine_ref.shape[1]

    def heads(dims):
        for head in range(mine_ref.shape[0] // HEAD_DIM):
            rows = pl.ds(head * HEAD_DIM, HEAD_DIM)
            total = mine_ref[rows, :].astype(jnp.float32) + arrived_ref[rows, :].astype(jnp.float32)
            probs = message_ref[head * tokens : (head + 1) * tokens, :]
            mixed = matmul(total.astype(jnp.bfloat16), probs, dims)
            result_ref[rows, :] = mixed.astype(jnp.bfloat16)

    natural = is_odd() == odd_phase
    pl.when(natural)(lambda: heads(NN))
    pl.when(jnp.logical_not(natural))(lambda: heads(NT))

    flipped = result_ref[...].T
    second_core = lax.axis_index("core") == 1
    shard = tokens // (2 * outer)
    for chunk in range(CHUNKS):
        columns = pl.ds(chunk * step, step)
        partial = matmul(flipped, value_ref[0, version, :, columns], NN)
        for place in range(outer):
            low = partial[2 * place * shard : (2 * place + 1) * shard]
            high = partial[(2 * place + 1) * shard : (2 * place + 2) * shard]
            keep_ref[place, :, columns] = jnp.where(second_core, high, low).astype(jnp.bfloat16)
            send_ref[place, :, columns] = jnp.where(second_core, low, high).astype(jnp.bfloat16)


def mix(odd_phase, message, w_value, mine, arrived, outer):
    rows, width = w_value.shape[2:]
    tokens = mine.shape[1]
    half = jax.ShapeDtypeStruct((outer, tokens // (2 * outer), width), jnp.bfloat16)
    return pl.pallas_call(
        functools.partial(mix_kernel, outer, odd_phase),
        out_shape=(jax.ShapeDtypeStruct((rows, tokens), jnp.bfloat16), half, half),
        in_specs=[in_vmem()] * 4,
        out_specs=(in_vmem(), in_vmem(), in_vmem()),
        compiler_params=pltpu.CompilerParams(vmem_limit_bytes=VMEM_BYTES),
        cost_estimate=SMALL,
        name="mix",
    )(message, w_value, mine, arrived)


def combine_kernel(outer, last, keep_ref, arrived_ref, addend_ref, *refs):
    first_refs, sent_refs = refs[:-outer], refs[-outer:]
    for delta in range(outer):
        spot = lax.axis_index("outer") ^ delta
        total = keep_ref[spot].astype(jnp.float32) + arrived_ref[spot].astype(jnp.float32)
        if delta == 0:
            total = total + addend_ref[: total.shape[0], :].astype(jnp.float32)
        total = total.astype(jnp.bfloat16)
        if last:
            total = jnp.where(is_odd(), first_refs[delta][...], total)
        sent_refs[delta][...] = total


def combine(keep, arrived, addend, first_sent=()):
    outer, shard, width = keep.shape
    piece = jax.ShapeDtypeStruct((shard, width), jnp.bfloat16)
    return pl.pallas_call(
        functools.partial(combine_kernel, outer, len(first_sent) > 0),
        out_shape=(piece,) * outer,
        in_specs=[in_vmem()] * (3 + len(first_sent)),
        out_specs=(in_vmem(),) * outer,
        compiler_params=pltpu.CompilerParams(vmem_limit_bytes=VMEM_BYTES),
        cost_estimate=SMALL,
        name="combine",
    )(keep, arrived, addend, *first_sent)


def weight_grad_kernel(
    a0, a1, b0, b1, first0, first1, second0, second1, value_ref, out_ref
):
    odd = is_odd()
    left_first = jnp.concatenate([a0[...], a1[...]], axis=1)
    left_second = jnp.concatenate([b0[...], b1[...]], axis=1)
    right_second = jnp.concatenate([second0[...], second1[...]], axis=0)
    right_first = jnp.concatenate([first0[...], first1[...]], axis=0)
    grad_first = matmul(left_first, right_second, NN)
    grad_second = matmul(left_second, right_first, NN)
    value_ref[0] = jnp.where(odd, grad_first, grad_second).astype(jnp.bfloat16)
    out_ref[0] = jnp.where(odd, grad_second, grad_first).astype(jnp.bfloat16)


def weight_grads(first_results, second_results, first_full, second_full):
    rows, tokens = first_results[0].shape
    width = first_full[0].shape[1]
    step = rows // CHUNKS
    grad = jax.ShapeDtypeStruct((1, rows, width), jnp.bfloat16)
    left = pl.BlockSpec((step, tokens), lambda i: (i, 0))
    single = pl.BlockSpec((tokens, width), lambda i: (0, 0))
    wide = pl.BlockSpec((1, step, width), lambda i: (0, i, 0))
    return pl.pallas_call(
        weight_grad_kernel,
        grid=(CHUNKS,),
        out_shape=(grad, grad),
        in_specs=[left] * 4 + [single] * 4,
        out_specs=(wide, wide),
        compiler_params=pltpu.CompilerParams(vmem_limit_bytes=GRAD_VMEM_BYTES),
        cost_estimate=SMALL,
        name="weight_grads",
    )(*first_results, *second_results, *first_full, *second_full)


def load(source_ref, table_ref, sems):
    step = table_ref.shape[2] // CHUNKS
    copies = []
    for version in range(2):
        for chunk in range(CHUNKS):
            spot = (slice(None), version, pl.ds(chunk * step, step))
            copies.append(
                pltpu.make_async_copy(
                    source_ref.at[spot], table_ref.at[spot], sems.at[version * CHUNKS + chunk]
                )
            )
    return copies


def probs_kernel(stash_ref, probs_ref):
    tokens = stash_ref.shape[2]
    causal = lax.broadcasted_iota(jnp.int32, (tokens, tokens), 1) <= lax.broadcasted_iota(
        jnp.int32, (tokens, tokens), 0
    )
    for head in range(stash_ref.shape[1] // HEAD_DIM):
        rows = pl.ds(head * HEAD_DIM, HEAD_DIM)
        scores = matmul(stash_ref[0, rows, :], stash_ref[1, rows, :], TN)
        scores = jnp.where(causal, scores * (1.0 / math.sqrt(HEAD_DIM)), -jnp.inf)
        expo = jnp.exp(scores - jnp.max(scores, axis=1, keepdims=True))
        probs = (expo / jnp.sum(expo, axis=1, keepdims=True)).astype(jnp.bfloat16)
        probs_ref[head * tokens : (head + 1) * tokens, :] = probs


def attention_probs(stash):
    rows, tokens = stash.shape[1:]
    return pl.pallas_call(
        probs_kernel,
        out_shape=jax.ShapeDtypeStruct((rows // HEAD_DIM * tokens, tokens), jnp.bfloat16),
        in_specs=[in_vmem()],
        out_specs=in_vmem(),
        compiler_params=pltpu.CompilerParams(vmem_limit_bytes=VMEM_BYTES),
        cost_estimate=SMALL,
        name="probs",
    )(stash)


def load_kernel(source_ref, table_ref, sems):
    copies = load(source_ref, table_ref, sems)
    for copy in copies:
        copy.start()
    for copy in copies:
        copy.wait()


def load_first_kernel(value_ref, out_ref, table_ref, sems):
    def start(source_ref):
        for copy in load(source_ref, table_ref, sems):
            copy.start()

    pl.when(is_odd())(lambda: start(out_ref))
    pl.when(jnp.logical_not(is_odd()))(lambda: start(value_ref))
    for copy in load(value_ref, table_ref, sems):
        copy.wait()


def load_first(w_value, w_out):
    return pl.pallas_call(
        load_first_kernel,
        out_shape=jax.ShapeDtypeStruct(w_value.shape, jnp.bfloat16),
        in_specs=[in_hbm(), in_hbm()],
        out_specs=in_vmem(),
        scratch_shapes=[pltpu.SemaphoreType.DMA((2 * CHUNKS,))],
        compiler_params=pltpu.CompilerParams(vmem_limit_bytes=FIRST_VMEM_BYTES),
        cost_estimate=SMALL,
        name="load_first",
    )(w_value, w_out)


def load_table(table, grant):
    return pl.pallas_call(
        load_kernel,
        out_shape=jax.ShapeDtypeStruct(table.shape, jnp.bfloat16),
        in_specs=[in_hbm()],
        out_specs=in_vmem(),
        scratch_shapes=[pltpu.SemaphoreType.DMA((2 * CHUNKS,))],
        compiler_params=pltpu.CompilerParams(vmem_limit_bytes=grant),
        cost_estimate=SMALL,
        name="load_table",
    )(table)


def on_device(section_input, query, key_stash, incoming, version, w_value, w_out):
    half = lax.axis_index("half")
    odd = is_odd()
    n_pairs = lax.axis_size("pair")
    outer = lax.axis_size("outer")
    n_tensor = 2 * outer
    width = w_value.shape[3]
    shard = section_input.shape[1]

    def swap_half(array):
        return lax.ppermute(array, "half", [(0, 1), (1, 0)])

    def swap_core(array):
        return lax.ppermute(array, "core", [(0, 1), (1, 0)])

    def to_row(array, delta, other_core=0):
        pairs = [
            (2 * i + c, 2 * (i ^ delta) + (c ^ other_core)) for i in range(outer) for c in range(2)
        ]
        return lax.ppermute(array, ("outer", "core"), pairs)

    def to_other_half(array, delta):
        pairs = [
            (h * n_tensor + i, (1 - h) * n_tensor + (i ^ (2 * delta)))
            for h in range(2)
            for i in range(n_tensor)
        ]
        return lax.ppermute(array, ("half", "outer", "core"), pairs)

    def swap_section(array, delta):
        pairs = [
            (p * n_tensor + i, (p ^ 1) * n_tensor + (i ^ (2 * delta)))
            for p in range(n_pairs)
            for i in range(n_tensor)
        ]
        return lax.ppermute(array, ("pair", "outer", "core"), pairs)

    def own_columns(array):
        return lax.dynamic_slice_in_dim(array, half * width, width, 1)

    def other_columns(array):
        return lax.dynamic_slice_in_dim(array, (1 - half) * width, width, 1)

    def total(parts):
        value = parts[0].astype(jnp.float32)
        for part in parts[1:]:
            value = value + part.astype(jnp.float32)
        return value

    def spread_rows(piece):
        return [piece] + [to_row(piece, delta) for delta in range(1, outer)]

    first = jnp.where(odd, incoming[0], section_input[0])
    own_piece, sent_piece = own_columns(first), other_columns(first)
    other_piece = swap_half(sent_piece)
    first_piece = [own_piece, other_piece]
    later_own, _ = lax.optimization_barrier((own_piece, other_piece))
    first_mine = [spread_rows(later_own), spread_rows(other_piece)]
    own_probs = attention_probs(jnp.concatenate([query, key_stash]))
    note = jnp.full((NOTE_ROWS, LANES), version[0], jnp.int32).astype(jnp.bfloat16)
    own_probs = jnp.concatenate([own_probs, note])
    other_probs = swap_half(own_probs)
    late_value, late_out, _ = lax.optimization_barrier((w_value, w_out, own_probs))
    first_table = load_first(late_value, late_out)
    first_theirs = []
    for pieces in first_mine:
        later, _ = lax.optimization_barrier((pieces, first_table))
        first_theirs.append([swap_core(piece) for piece in later])

    probs = [own_probs, other_probs]
    partial, first_full = [None, None], [None, None]
    for m in (1, 0):
        mine = first_mine[m]
        if m == 0:
            mine, probs, _ = lax.optimization_barrier((mine, probs, partial[1]))
        partial[m], first_full[m] = project(
            shard, probs[m], (first_table,), mine, first_theirs[m]
        )
    arrived = [swap_half(partial[1]), swap_half(partial[0])]
    later_value, _ = lax.optimization_barrier((w_value, partial))
    value_table = load_table(later_value, VALUE_VMEM_BYTES)
    first_result, first_sent = [None, None], [None, None]
    second_piece, second_full = [None, None], [None, None]
    for m in range(2):
        first_result[m], keep, send = mix(
            True, probs[m], value_table, partial[m], arrived[m], outer
        )
        first_sent[m] = combine(keep, swap_core(send), first_piece[m])
    later_out, _ = lax.optimization_barrier((w_out, first_sent))
    out_table = load_table(later_out, OUT_VMEM_BYTES)
    later_input, _ = lax.optimization_barrier((section_input[0], out_table))
    input_own, input_sent = lax.optimization_barrier(
        (own_columns(later_input), other_columns(later_input))
    )
    input_piece = [input_own, swap_half(input_sent)]
    for m in range(2):
        received = [swap_section(part, d) for d, part in enumerate(first_sent[m])]
        last_received = received = received[:1] + lax.optimization_barrier(received[1:])
        second_piece[m] = jnp.where(odd, input_piece[m], total(received).astype(jnp.bfloat16))
    for m in range(2):
        mine = spread_rows(second_piece[m])
        swapped = second_piece[m]
        if m == 0:
            swapped, _ = lax.optimization_barrier((swapped, last_received))
        theirs = [swap_core(swapped)]
        theirs += [to_row(second_piece[m], delta, 1) for delta in range(1, outer)]
        partial[m], second_full[m] = project(
            shard, probs[m], (value_table, out_table), mine, theirs
        )
    arrived = [swap_half(partial[1]), swap_half(partial[0])]
    second_result, last_sent = [None, None], [None, None]
    for m in (1, 0):
        second_result[m], keep, send = mix(
            False, probs[m], value_table, partial[m], arrived[m], outer
        )
        if m == 0:
            keep, _ = lax.optimization_barrier((keep, last_sent[1]))
        last_sent[m] = combine(keep, swap_core(send), second_piece[m], first_sent[m])
    other_parts = [to_other_half(part, d) for d, part in enumerate(last_sent[1])]
    own_parts = [last_sent[0][0]] + [to_row(part, d + 1) for d, part in enumerate(last_sent[0][1:])]
    second_result, _ = lax.optimization_barrier((second_result, last_sent))
    grad_value, grad_out = weight_grads(
        first_result, second_result, first_full, second_full
    )
    other_parts = other_parts[:1] + lax.optimization_barrier(other_parts[1:])
    other_grad = lax.optimization_barrier(total(other_parts).astype(jnp.bfloat16))
    own_parts, _ = lax.optimization_barrier((own_parts, grad_value))
    own_grad = total(own_parts).astype(jnp.bfloat16)
    input_grad = jnp.concatenate(
        [jnp.where(half == 0, own_grad, other_grad), jnp.where(half == 0, other_grad, own_grad)],
        axis=1,
    )
    return (input_grad[None], grad_value, grad_out)


def solution(mesh):
    sections, tensor = mesh.devices.shape
    split = Mesh(
        mesh.devices.reshape(sections // 2, 2, tensor // 2, 2), ("pair", "half", "outer", "core")
    )
    slots, places = ("pair", "half"), ("outer", "core")
    by_tokens = P(slots, places, None)
    by_rows = P(slots, None, places, None)
    return jax.shard_map(
        on_device,
        mesh=split,
        in_specs=(by_tokens, by_tokens, by_tokens, by_tokens, P(slots), by_rows, by_rows),
        out_specs=(by_tokens, by_tokens, by_tokens),
        check_vma=False,
    )
```

```python
import functools
import math

import jax
import jax.numpy as jnp
from jax import lax
from jax.experimental import pallas as pl
from jax.experimental.pallas import tpu as pltpu
from jax.sharding import Mesh, PartitionSpec as P

HEAD_DIM = 96
CHUNKS = 4
VMEM_BYTES = 8 * 2**20
GRAD_VMEM_BYTES = 16 * 2**20
FIRST_VMEM_BYTES = 46 * 2**20
VALUE_VMEM_BYTES = 47 * 2**20
OUT_VMEM_BYTES = 42 * 2**20
LANES = 128
NOTE_ROWS = 16
SMALL = pl.CostEstimate(flops=1, bytes_accessed=1, transcendentals=0)
NN = (((1,), (0,)), ((), ()))
NT = (((1,), (1,)), ((), ()))
TN = (((0,), (0,)), ((), ()))


def matmul(left_side, right_side, dims):
    return lax.dot_general(left_side, right_side, dims, preferred_element_type=jnp.float32)


def in_vmem():
    return pl.BlockSpec(memory_space=pltpu.VMEM)


def in_hbm():
    return pl.BlockSpec(memory_space=pltpu.HBM)


def in_place():
    return pl.BlockSpec(memory_space=pl.ANY)


def is_odd():
    return (lax.axis_index("pair") & 1) == 1


def noted_version(message_ref):
    note = message_ref[message_ref.shape[0] - NOTE_ROWS :, :]
    return (jnp.max(note.astype(jnp.float32)) > 0.5).astype(jnp.int32)


def project_kernel(outer, shard, n_tables, message_ref, *refs):
    table_refs, piece_refs = refs[:n_tables], refs[n_tables:-2]
    partial_ref, full_ref = refs[-2:]
    version = noted_version(message_ref)
    first_core = lax.axis_index("core") == 0
    mine = [ref[:shard, :] for ref in piece_refs[:outer]]
    theirs = [ref[:shard, :] for ref in piece_refs[outer:]]
    for place in range(outer):
        offset = lax.axis_index("outer") ^ place
        own, other = mine[0], theirs[0]
        for delta in range(1, outer):
            own = jnp.where(offset == delta, mine[delta], own)
            other = jnp.where(offset == delta, theirs[delta], other)
        start = 2 * place * shard
        full_ref[start : start + shard, :] = jnp.where(first_core, own, other)
        full_ref[start + shard : start + 2 * shard, :] = jnp.where(first_core, other, own)
    flipped = full_ref[...].T

    def rows_of(table_ref):
        partial_ref[...] = matmul(table_ref[0, version], flipped, NN).astype(jnp.bfloat16)

    if n_tables == 1:
        rows_of(table_refs[0])
    else:
        pl.when(is_odd())(lambda: rows_of(table_refs[0]))
        pl.when(jnp.logical_not(is_odd()))(lambda: rows_of(table_refs[1]))


def project(shard, message, tables, mine, theirs):
    outer = len(mine)
    rows, width = tables[0].shape[2:]
    tokens = 2 * outer * shard
    return pl.pallas_call(
        functools.partial(project_kernel, outer, shard, len(tables)),
        out_shape=(
            jax.ShapeDtypeStruct((rows, tokens), jnp.bfloat16),
            jax.ShapeDtypeStruct((tokens, width), jnp.bfloat16),
        ),
        in_specs=[in_vmem()] * (1 + len(tables) + 2 * outer),
        out_specs=(in_vmem(), in_vmem()),
        compiler_params=pltpu.CompilerParams(vmem_limit_bytes=VMEM_BYTES),
        cost_estimate=SMALL,
        name="project",
    )(message, *tables, *mine, *theirs)


def mix_kernel(
    outer,
    odd_phase,
    message_ref,
    value_ref,
    mine_ref,
    arrived_ref,
    result_ref,
    keep_ref,
    send_ref,
):
    version = noted_version(message_ref)
    step = value_ref.shape[3] // CHUNKS
    tokens = mine_ref.shape[1]

    def heads(dims):
        for head in range(mine_ref.shape[0] // HEAD_DIM):
            rows = pl.ds(head * HEAD_DIM, HEAD_DIM)
            total = mine_ref[rows, :].astype(jnp.float32) + arrived_ref[rows, :].astype(jnp.float32)
            probs = message_ref[head * tokens : (head + 1) * tokens, :]
            mixed = matmul(total.astype(jnp.bfloat16), probs, dims)
            result_ref[rows, :] = mixed.astype(jnp.bfloat16)

    natural = is_odd() == odd_phase
    pl.when(natural)(lambda: heads(NN))
    pl.when(jnp.logical_not(natural))(lambda: heads(NT))

    flipped = result_ref[...].T
    second_core = lax.axis_index("core") == 1
    shard = tokens // (2 * outer)
    for chunk in range(CHUNKS):
        columns = pl.ds(chunk * step, step)
        partial = matmul(flipped, value_ref[0, version, :, columns], NN)
        for place in range(outer):
            low = partial[2 * place * shard : (2 * place + 1) * shard]
            high = partial[(2 * place + 1) * shard : (2 * place + 2) * shard]
            keep_ref[place, :, columns] = jnp.where(second_core, high, low).astype(jnp.bfloat16)
            send_ref[place, :, columns] = jnp.where(second_core, low, high).astype(jnp.bfloat16)


def mix(odd_phase, message, w_value, mine, arrived, outer):
    rows, width = w_value.shape[2:]
    tokens = mine.shape[1]
    half = jax.ShapeDtypeStruct((outer, tokens // (2 * outer), width), jnp.bfloat16)
    return pl.pallas_call(
        functools.partial(mix_kernel, outer, odd_phase),
        out_shape=(jax.ShapeDtypeStruct((rows, tokens), jnp.bfloat16), half, half),
        in_specs=[in_vmem()] * 4,
        out_specs=(in_vmem(), in_vmem(), in_vmem()),
        compiler_params=pltpu.CompilerParams(vmem_limit_bytes=VMEM_BYTES),
        cost_estimate=SMALL,
        name="mix",
    )(message, w_value, mine, arrived)


def combine_kernel(outer, last, keep_ref, arrived_ref, addend_ref, *refs):
    first_refs, sent_refs = refs[:-outer], refs[-outer:]
    for delta in range(outer):
        spot = lax.axis_index("outer") ^ delta
        total = keep_ref[spot].astype(jnp.float32) + arrived_ref[spot].astype(jnp.float32)
        if delta == 0:
            total = total + addend_ref[: total.shape[0], :].astype(jnp.float32)
        total = total.astype(jnp.bfloat16)
        if last:
            total = jnp.where(is_odd(), first_refs[delta][...], total)
        sent_refs[delta][...] = total


def combine(keep, arrived, addend, first_sent=()):
    outer, shard, width = keep.shape
    piece = jax.ShapeDtypeStruct((shard, width), jnp.bfloat16)
    return pl.pallas_call(
        functools.partial(combine_kernel, outer, len(first_sent) > 0),
        out_shape=(piece,) * outer,
        in_specs=[in_vmem()] * (3 + len(first_sent)),
        out_specs=(in_vmem(),) * outer,
        compiler_params=pltpu.CompilerParams(vmem_limit_bytes=VMEM_BYTES),
        cost_estimate=SMALL,
        name="combine",
    )(keep, arrived, addend, *first_sent)


def weight_grad_kernel(
    a0, a1, b0, b1, first0, first1, second0, second1, value_ref, out_ref
):
    odd = is_odd()
    left_first = jnp.concatenate([a0[...], a1[...]], axis=1)
    left_second = jnp.concatenate([b0[...], b1[...]], axis=1)
    right_second = jnp.concatenate([second0[...], second1[...]], axis=0)
    right_first = jnp.concatenate([first0[...], first1[...]], axis=0)
    grad_first = matmul(left_first, right_second, NN)
    grad_second = matmul(left_second, right_first, NN)
    value_ref[0] = jnp.where(odd, grad_first, grad_second).astype(jnp.bfloat16)
    out_ref[0] = jnp.where(odd, grad_second, grad_first).astype(jnp.bfloat16)


def weight_grads(first_results, second_results, first_full, second_full):
    rows, tokens = first_results[0].shape
    width = first_full[0].shape[1]
    step = rows // CHUNKS
    grad = jax.ShapeDtypeStruct((1, rows, width), jnp.bfloat16)
    left = pl.BlockSpec((step, tokens), lambda i: (i, 0))
    single = pl.BlockSpec((tokens, width), lambda i: (0, 0))
    wide = pl.BlockSpec((1, step, width), lambda i: (0, i, 0))
    return pl.pallas_call(
        weight_grad_kernel,
        grid=(CHUNKS,),
        out_shape=(grad, grad),
        in_specs=[left] * 4 + [single] * 4,
        out_specs=(wide, wide),
        compiler_params=pltpu.CompilerParams(vmem_limit_bytes=GRAD_VMEM_BYTES),
        cost_estimate=SMALL,
        name="weight_grads",
    )(*first_results, *second_results, *first_full, *second_full)


def load(source_ref, table_ref, sems):
    step = table_ref.shape[2] // CHUNKS
    copies = []
    for version in range(2):
        for chunk in range(CHUNKS):
            spot = (slice(None), version, pl.ds(chunk * step, step))
            copies.append(
                pltpu.make_async_copy(
                    source_ref.at[spot], table_ref.at[spot], sems.at[version * CHUNKS + chunk]
                )
            )
    return copies


def probs_kernel(stash_ref, probs_ref):
    tokens = stash_ref.shape[2]
    causal = lax.broadcasted_iota(jnp.int32, (tokens, tokens), 1) <= lax.broadcasted_iota(
        jnp.int32, (tokens, tokens), 0
    )
    for head in range(stash_ref.shape[1] // HEAD_DIM):
        rows = pl.ds(head * HEAD_DIM, HEAD_DIM)
        scores = matmul(stash_ref[0, rows, :], stash_ref[1, rows, :], TN)
        scores = jnp.where(causal, scores * (1.0 / math.sqrt(HEAD_DIM)), -jnp.inf)
        expo = jnp.exp(scores - jnp.max(scores, axis=1, keepdims=True))
        probs = (expo / jnp.sum(expo, axis=1, keepdims=True)).astype(jnp.bfloat16)
        probs_ref[head * tokens : (head + 1) * tokens, :] = probs


def attention_probs(stash):
    rows, tokens = stash.shape[1:]
    return pl.pallas_call(
        probs_kernel,
        out_shape=jax.ShapeDtypeStruct((rows // HEAD_DIM * tokens, tokens), jnp.bfloat16),
        in_specs=[in_vmem()],
        out_specs=in_vmem(),
        compiler_params=pltpu.CompilerParams(vmem_limit_bytes=VMEM_BYTES),
        cost_estimate=SMALL,
        name="probs",
    )(stash)


def load_kernel(source_ref, table_ref, sems):
    copies = load(source_ref, table_ref, sems)
    for copy in copies:
        copy.start()
    for copy in copies:
        copy.wait()


def load_first_kernel(value_ref, out_ref, table_ref, sems):
    def start(source_ref):
        for copy in load(source_ref, table_ref, sems):
            copy.start()

    pl.when(is_odd())(lambda: start(out_ref))
    pl.when(jnp.logical_not(is_odd()))(lambda: start(value_ref))
    for copy in load(value_ref, table_ref, sems):
        copy.wait()


def load_first(w_value, w_out):
    return pl.pallas_call(
        load_first_kernel,
        out_shape=jax.ShapeDtypeStruct(w_value.shape, jnp.bfloat16),
        in_specs=[in_hbm(), in_hbm()],
        out_specs=in_vmem(),
        scratch_shapes=[pltpu.SemaphoreType.DMA((2 * CHUNKS,))],
        compiler_params=pltpu.CompilerParams(vmem_limit_bytes=FIRST_VMEM_BYTES),
        cost_estimate=SMALL,
        name="load_first",
    )(w_value, w_out)


def load_table(table, grant):
    return pl.pallas_call(
        load_kernel,
        out_shape=jax.ShapeDtypeStruct(table.shape, jnp.bfloat16),
        in_specs=[in_hbm()],
        out_specs=in_vmem(),
        scratch_shapes=[pltpu.SemaphoreType.DMA((2 * CHUNKS,))],
        compiler_params=pltpu.CompilerParams(vmem_limit_bytes=grant),
        cost_estimate=SMALL,
        name="load_table",
    )(table)


def on_device(section_input, query, key_stash, incoming, version, w_value, w_out):
    half = lax.axis_index("half")
    odd = is_odd()
    n_pairs = lax.axis_size("pair")
    outer = lax.axis_size("outer")
    n_tensor = 2 * outer
    width = w_value.shape[3]
    shard = section_input.shape[1]

    def swap_half(array):
        return lax.ppermute(array, "half", [(0, 1), (1, 0)])

    def swap_core(array):
        return lax.ppermute(array, "core", [(0, 1), (1, 0)])

    def to_row(array, delta, other_core=0):
        pairs = [
            (2 * i + c, 2 * (i ^ delta) + (c ^ other_core)) for i in range(outer) for c in range(2)
        ]
        return lax.ppermute(array, ("outer", "core"), pairs)

    def to_other_half(array, delta):
        pairs = [
            (h * n_tensor + i, (1 - h) * n_tensor + (i ^ (2 * delta)))
            for h in range(2)
            for i in range(n_tensor)
        ]
        return lax.ppermute(array, ("half", "outer", "core"), pairs)

    def swap_section(array, delta):
        pairs = [
            (p * n_tensor + i, (p ^ 1) * n_tensor + (i ^ (2 * delta)))
            for p in range(n_pairs)
            for i in range(n_tensor)
        ]
        return lax.ppermute(array, ("pair", "outer", "core"), pairs)

    def own_columns(array):
        return lax.dynamic_slice_in_dim(array, half * width, width, 1)

    def other_columns(array):
        return lax.dynamic_slice_in_dim(array, (1 - half) * width, width, 1)

    def total(parts):
        value = parts[0].astype(jnp.float32)
        for part in parts[1:]:
            value = value + part.astype(jnp.float32)
        return value

    def spread_rows(piece):
        return [piece] + [to_row(piece, delta) for delta in range(1, outer)]

    first = jnp.where(odd, incoming[0], section_input[0])
    own_piece, sent_piece = own_columns(first), other_columns(first)
    other_piece = swap_half(sent_piece)
    first_piece = [own_piece, other_piece]
    later_own, _ = lax.optimization_barrier((own_piece, other_piece))
    first_mine = [spread_rows(later_own), spread_rows(other_piece)]
    own_probs = attention_probs(jnp.concatenate([query, key_stash]))
    note = jnp.full((NOTE_ROWS, LANES), version[0], jnp.int32).astype(jnp.bfloat16)
    own_probs = jnp.concatenate([own_probs, note])
    other_probs = swap_half(own_probs)
    late_value, late_out, _ = lax.optimization_barrier((w_value, w_out, own_probs))
    first_table = load_first(late_value, late_out)
    first_theirs = []
    for pieces in first_mine:
        later, _ = lax.optimization_barrier((pieces, first_table))
        first_theirs.append([swap_core(piece) for piece in later])

    probs = [own_probs, other_probs]
    partial, first_full = [None, None], [None, None]
    for m in (1, 0):
        mine = first_mine[m]
        if m == 0:
            mine, probs, _ = lax.optimization_barrier((mine, probs, partial[1]))
        partial[m], first_full[m] = project(
            shard, probs[m], (first_table,), mine, first_theirs[m]
        )
    arrived = [swap_half(partial[1]), swap_half(partial[0])]
    later_value, _ = lax.optimization_barrier((w_value, partial))
    value_table = load_table(later_value, VALUE_VMEM_BYTES)
    first_result, first_sent = [None, None], [None, None]
    second_piece, second_full = [None, None], [None, None]
    for m in range(2):
        first_result[m], keep, send = mix(
            True, probs[m], value_table, partial[m], arrived[m], outer
        )
        first_sent[m] = combine(keep, swap_core(send), first_piece[m])
    later_out, _ = lax.optimization_barrier((w_out, first_sent))
    out_table = load_table(later_out, OUT_VMEM_BYTES)
    later_input, _ = lax.optimization_barrier((section_input[0], out_table))
    input_own, input_sent = lax.optimization_barrier(
        (own_columns(later_input), other_columns(later_input))
    )
    input_piece = [input_own, swap_half(input_sent)]
    for m in range(2):
        received = [swap_section(part, d) for d, part in enumerate(first_sent[m])]
        last_received = received = received[:1] + lax.optimization_barrier(received[1:])
        second_piece[m] = jnp.where(odd, input_piece[m], total(received).astype(jnp.bfloat16))
    for m in range(2):
        mine = spread_rows(second_piece[m])
        swapped = second_piece[m]
        if m == 0:
            swapped, _ = lax.optimization_barrier((swapped, last_received))
        theirs = [swap_core(swapped)]
        theirs += [to_row(second_piece[m], delta, 1) for delta in range(1, outer)]
        partial[m], second_full[m] = project(
            shard, probs[m], (value_table, out_table), mine, theirs
        )
    arrived = [swap_half(partial[1]), swap_half(partial[0])]
    second_result, last_sent = [None, None], [None, None]
    for m in (1, 0):
        second_result[m], keep, send = mix(
            False, probs[m], value_table, partial[m], arrived[m], outer
        )
        if m == 0:
            keep, _ = lax.optimization_barrier((keep, last_sent[1]))
        last_sent[m] = combine(keep, swap_core(send), second_piece[m], first_sent[m])
    other_parts = [to_other_half(part, d) for d, part in enumerate(last_sent[1])]
    own_parts = [last_sent[0][0]] + [to_row(part, d + 1) for d, part in enumerate(last_sent[0][1:])]
    second_result, _ = lax.optimization_barrier((second_result, last_sent))
    grad_value, grad_out = weight_grads(
        first_result, second_result, first_full, second_full
    )
    far_sum = lax.optimization_barrier(total(other_parts[1:]))
    other_grad = total([other_parts[0], far_sum]).astype(jnp.bfloat16)
    own_parts, _ = lax.optimization_barrier((own_parts, grad_value))
    own_grad = total(own_parts).astype(jnp.bfloat16)
    input_grad = jnp.concatenate(
        [jnp.where(half == 0, own_grad, other_grad), jnp.where(half == 0, other_grad, own_grad)],
        axis=1,
    )
    return (input_grad[None], grad_value, grad_out)


def solution(mesh):
    sections, tensor = mesh.devices.shape
    split = Mesh(
        mesh.devices.reshape(sections // 2, 2, tensor // 2, 2), ("pair", "half", "outer", "core")
    )
    slots, places = ("pair", "half"), ("outer", "core")
    by_tokens = P(slots, places, None)
    by_rows = P(slots, None, places, None)
    return jax.shard_map(
        on_device,
        mesh=split,
        in_specs=(by_tokens, by_tokens, by_tokens, by_tokens, P(slots), by_rows, by_rows),
        out_specs=(by_tokens, by_tokens, by_tokens),
        check_vma=False,
    )
```
